32 devices in a mesh: mach: 2 (over x), panel: 16 (over z, y, core).
Axes of the slice: x: 2, y: 2, z: 4, core: 2. Of those that a mesh axis runs over, the one named last changes fastest.
Arguments:
- adjoint: bfloat16 [2, 128, 4, 128], P('mach', 'panel'), may hold values from -6 to 6
- near_blocks: bfloat16 [2, 128, 8, 128, 128], P('mach', 'panel'), may hold values from -0.1875 to 0.1875
- pattern: int32 [128, 8], P('panel'), may hold values from 0 to 127, as said below
- trim_mask: int32 [2, 4], P('mach'), may hold values 0 or 1
- spline_blocks: bfloat16 [128, 6, 128, 128], P('panel'), may hold values from -0.21875 to 0.21875
- spline_owner: int32 [128, 6], P('panel'), may hold values from 0 to 15, all different within a row; in each aligned block of 8 rows (0 to 7, 8 to 15, ...) at most 6 rows name the same one
- spline_local: int32 [128, 6], P('panel'), may hold values from 0 to 7
- struct_inverse: bfloat16 [128, 128, 128], P('panel'), may hold values from -0.375 to 0.375
Outputs:
- panel_loads: float32 [2, 128, 4, 128], P('mach', 'panel')
- struct_adjoint: float32 [128, 4, 128], P('panel')
The draws below stay inside these ranges and needn't reach their ends.
Inputs may be any that keep to these rules, and one draw needn't show every extreme that they name: `pattern`: entry 0 of row i is i itself; entry 1 is the mirror block (i + 64) mod 128; every other entry lies within 8 blocks of its row, and each row has one entry exactly 8 blocks away unless that falls outside the grid, where it is clipped to the end. `spline_owner`: the targets of one row are different owners; among the rows of one device no owner is named more than 6 times, a bound that some block reaches.
All inputs are finite; a program needn't handle non-finite values. No bound on the sum of `trim_mask` on one device may be relied on, other than what follows from the above.
Results may differ from the reference program's by a relative error of at most 0.004.
Values may be sent and summed in bfloat16 or wider, within the bound.
No kernel may reach another device: no remote copies, remote signals or barrier semaphores. Data moves between devices by JAX's collectives and lax.ppermute only.
A program may use at most 64 MiB of HBM per device.

```python
import math
import jax
import jax.numpy as jnp
import numpy as np
from jax import lax

BS = 128
NRHS = 4
NNZ = 8
S_PER = 6
NB_DEV = 8
SB_DEV = 8
MACHS = 2
OWNERS = 16
NPB = 128
NSB = 128
CAP = 6


def draw_pattern(key, part):
    first, second = jax.random.split(jax.random.fold_in(key, 17))
    blocks_all = jnp.arange(NPB, dtype=jnp.int32)
    columns = jnp.arange(NNZ, dtype=jnp.int32)
    offsets = jax.random.randint(first, (NPB, NNZ), -NB_DEV, NB_DEV + 1).astype(jnp.int32)
    signs = jax.random.randint(second, (NPB,), 0, 2).astype(jnp.int32) * 2 - 1
    far_column = 2 + blocks_all % (NNZ - 2)
    offsets = jnp.where(columns[None, :] == far_column[:, None], (signs * NB_DEV)[:, None], offsets)
    offsets = jnp.where(columns[None, :] == 0, 0, offsets)
    near = jnp.clip(blocks_all[:, None] + offsets, 0, NPB - 1).astype(jnp.int32)
    mirror = ((blocks_all + NPB // 2) % NPB).astype(jnp.int32)
    return jnp.where(columns[None, :] == 1, mirror[:, None], near).astype(jnp.int32)


def with_ends(drawn, rng, low, high):
    longest = drawn.shape.index(max(drawn.shape))
    spots = []
    for shift in (0, 1):
        where = [jax.random.randint(jax.random.fold_in(rng, axis), (), 0, length) for axis, length in enumerate(drawn.shape)]
        where[longest] = (where[longest] + shift) % drawn.shape[longest]
        spots.append(tuple(where))
    return drawn.at[spots[0]].set(low).at[spots[1]].set(high)


def block_scale(stream_key, dims, shards, least, largest):
    def one(position, blocks):
        heights = jax.random.uniform(jax.random.fold_in(jax.random.fold_in(stream_key, 6), position), (blocks,), jnp.float32, least / len(shards), largest / len(shards))
        return jnp.repeat(jnp.exp(heights), dims[position] // blocks).reshape((-1,) + (1,) * (len(dims) - position - 1))

    gain = one(*shards[0])
    for cut in shards[1:]:
        gain = gain * one(*cut)
    return gain


def shared_out(own_key, own, number, rows, number_of, top, reach, slope):
    ranking = jax.random.permutation(own_key, number_of)
    packed, usual = shares(number_of, rows * top, reach, slope, True), shares(number_of, rows * top, reach, slope, False)
    places = jnp.arange(number_of)

    def named(sizes, offset_by):
        used = int((sizes > 0).sum())
        fixed = max(1, used // 4)
        moved = fixed + (places - fixed + offset_by * (used - fixed)) % max(1, number_of - fixed)
        return jnp.zeros((number_of,), jnp.int32).at[ranking[jnp.where(places < fixed, places, moved)]].set(jnp.asarray(sizes, jnp.int32))

    sizes = jnp.where(number % 4 == 0, named(packed, number // 4), named(usual, number - number // 4 - 1))
    mixed = jax.random.permutation(jax.random.fold_in(own, 3), number_of)
    source_of, sink = mixed[0:number_of // 2 * 2:2], mixed[1:number_of // 2 * 2:2]
    slack = jnp.minimum(sizes[source_of] - 1, reach - sizes[sink]) // 2
    slack = jnp.where((source_of == ranking[0]) | (sink == ranking[0]) | (sizes[sink] == 0), 0, jnp.maximum(slack, 0))
    moved = jax.random.randint(jax.random.fold_in(own, 4), (number_of // 2,), 0, 1 << 20) % (slack + 1)
    sizes = sizes.at[source_of].add(-moved).at[sink].add(moved)
    items = jnp.searchsorted(jnp.cumsum(sizes), jnp.arange(rows * top), side="right").astype(jnp.int32)
    grid = items.reshape(top, rows).T
    grid = grid[jax.random.permutation(jax.random.fold_in(own, 1), rows)]
    offset_by = jax.random.randint(jax.random.fold_in(own, 2), (rows, 1), 0, top)
    return jnp.take_along_axis(grid, (jnp.arange(top)[None, :] + offset_by) % top, axis=1)


def shares(count, total, reach, skew, full):
    weights = [(1 << 20) // math.isqrt(standing ** skew) + 1 for standing in range(1, count + 1)]
    largest = reach if full else min(reach, max(-(-total // count), total * weights[0] // sum(weights)))
    least = 1 if total - largest >= count - 1 else 0
    holding, spare = [largest] + [least] * (count - 1), total - largest - least * (count - 1)
    while spare > 0:
        candidates = [i for i in range(1, count) if holding[i] < largest] or [i for i in range(1, count) if holding[i] < reach]
        mass, remaining = sum([weights[i] for i in candidates]), spare
        for i in candidates:
            addition = min(reach - holding[i], max(1, remaining * weights[i] // mass), spare)
            holding[i] = holding[i] + addition
            spare = spare - addition
    return np.array(holding)


def bell_draw(stream_key, extent, width, reach, shards=(), kind=jnp.bfloat16):
    entries = jax.random.normal(stream_key, extent, jnp.float32) * width
    if len(shards) > 0:
        entries = block_scale(stream_key, extent, shards, -0.22, 0.18) * entries
    return jnp.clip(entries, min=-reach, max=reach).astype(kind)


def setup_inputs(seed: int = 0) -> dict:
    key_of = jax.random.split(jax.random.key(seed), 9)
    adjoint = bell_draw(key_of[0], (MACHS, NPB, NRHS, BS), 1.0, 6.0, ((0, 2), (1, 16)))
    near_blocks = bell_draw(key_of[1], (MACHS, NPB, NNZ, BS, BS), (NNZ * BS) ** -0.5, 0.1875, ((0, 2), (1, 16)))
    pattern = draw_pattern(jax.random.fold_in(key_of[8], 71), 0)
    trim_mask = with_ends((jax.random.randint(key_of[3], (MACHS, NRHS), 0, 4) < 3).astype(jnp.int32), jax.random.fold_in(key_of[3], 1), 0, 1)
    spline_blocks = bell_draw(key_of[4], (NPB, S_PER, BS, BS), (BS * NB_DEV * S_PER // SB_DEV) ** -0.5, 0.21875, ((0, 16),))
    spline_owner_keys = jax.random.split(jax.random.fold_in(key_of[5], 1), NPB // NB_DEV)
    spline_owner_turns = jax.random.permutation(jax.random.fold_in(key_of[5], 3), NPB // NB_DEV)
    spline_owner = jax.vmap(lambda own, number: shared_out(jax.random.fold_in(key_of[5], 2), own, number, NB_DEV, OWNERS, S_PER, CAP, 2))(spline_owner_keys, spline_owner_turns).reshape((NPB, S_PER))
    spline_local = with_ends(jax.random.randint(key_of[6], (NPB, S_PER), 0, SB_DEV), jax.random.fold_in(key_of[6], 1), 0, SB_DEV - 1).astype(jnp.int32)
    struct_inverse = bell_draw(key_of[7], (NSB, BS, BS), (BS * MACHS) ** -0.5, 0.375, ((0, 16),))
    return {"adjoint": adjoint, "near_blocks": near_blocks, "pattern": pattern, "trim_mask": trim_mask, "spline_blocks": spline_blocks, "spline_owner": spline_owner, "spline_local": spline_local, "struct_inverse": struct_inverse}


def reference(adjoint, near_blocks, pattern, trim_mask, spline_blocks, spline_owner, spline_local, struct_inverse):
    targets = (spline_owner * SB_DEV + spline_local).reshape(-1).astype(jnp.int32)
    spline_wide = spline_blocks.astype(jnp.float32)

    def one_mach(which):
        pressures = adjoint[which]
        picked = pressures[pattern].astype(jnp.float32)
        blocks = near_blocks[which].astype(jnp.float32)
        near = jnp.einsum('bkrp,bkpq->brq', picked, blocks)
        gate = trim_mask[which].astype(jnp.float32)
        loads = near * gate[None, :, None]
        rounded = lax.optimization_barrier(loads.astype(jnp.bfloat16)).astype(jnp.float32)
        contrib = jnp.einsum('brp,bspq->bsrq', rounded, spline_wide)
        summed = jax.ops.segment_sum(contrib.reshape(-1, NRHS, BS), targets, NSB)
        return loads, summed

    panel_loads, per_mach = lax.map(one_mach, jnp.arange(MACHS, dtype=jnp.int32))
    struct_loads = jnp.sum(per_mach, axis=0)
    struct_rounded = lax.optimization_barrier(struct_loads.astype(jnp.bfloat16)).astype(jnp.float32)
    struct_adjoint = jnp.einsum('trp,tpq->trq', struct_rounded, struct_inverse.astype(jnp.float32))
    return panel_loads, struct_adjoint
```

```python
import functools

import jax
import jax.numpy as jnp
from jax import lax
from jax.experimental import pallas as pl
from jax.experimental.pallas import tpu as pltpu
from jax.sharding import PartitionSpec as P

SMEM = pl.BlockSpec(memory_space=pltpu.SMEM)
VMEM = pl.BlockSpec(memory_space=pltpu.VMEM)
PACK = 16
TILE = 8


def near_kernel(
    panels, rhs, pattern_ref, trim_ref, own_ref, pair_ref, cross_ref, mirror_ref, near_ref,
    loads_ref, rounded_ref,
):
    block_count, entries = pattern_ref.shape
    rows, width = own_ref.shape
    here = lax.axis_index("panel")
    pair = here + 1 - 2 * (here % 2)
    mirror = (here + panels // 2) % panels
    pool = jnp.concatenate(
        [own_ref[...], pair_ref[...], cross_ref[...], mirror_ref[...]], axis=0
    )
    shape = (rows, pool.shape[0])
    row = lax.broadcasted_iota(jnp.int32, shape, 0)
    offset = lax.broadcasted_iota(jnp.int32, shape, 1) - row % rhs
    picked = []
    for k in range(entries):
        first = jnp.zeros(shape, jnp.int32)
        for i in range(block_count):
            block = pattern_ref[i, k]
            owner = block // block_count
            slot = jnp.where(
                owner == here, 0, jnp.where(owner == mirror, 3, jnp.where(owner == pair, 1, 2))
            )
            base = (slot * block_count + block % block_count) * rhs
            first = jnp.where(row // rhs == i, base, first)
        hot = (offset == first).astype(jnp.bfloat16)
        picked.append(
            jnp.dot(hot, pool, preferred_element_type=jnp.float32).astype(jnp.bfloat16)
        )
    picked = jnp.concatenate(picked, axis=1)
    group_row = lax.broadcasted_iota(jnp.int32, (PACK, width), 0)
    gate = jnp.zeros((PACK, width), jnp.float32)
    for r in range(rhs):
        gate = jnp.where(group_row % rhs == r, trim_ref[0, r].astype(jnp.float32), gate)
    per_group = PACK // rhs
    for g in range(rows // PACK):
        left = picked[g * PACK : (g + 1) * PACK]
        loads = jnp.zeros((PACK, width), jnp.float32)
        for j in range(per_group):
            blocks = near_ref[g * per_group + j].reshape(entries * width, width)
            product = jnp.dot(left, blocks, preferred_element_type=jnp.float32)
            loads = jnp.where(group_row // rhs == j, product, loads)
        loads = loads * gate
        loads_ref[g * PACK : (g + 1) * PACK] = loads
        rounded_ref[g * PACK : (g + 1) * PACK] = loads.astype(jnp.bfloat16)


def spline_kernel(
    rhs, struct_count, owner_ref, local_ref, *refs
):
    machs = len(refs) - 3
    rounded_refs, spline_ref, out_ref, acc = refs[:machs], refs[machs], refs[-2], refs[-1]
    block_count, splines = owner_ref.shape
    rows, width = rounded_refs[0].shape
    acc[...] = jnp.zeros(acc.shape, jnp.float32)
    every = jnp.concatenate([ref[...] for ref in rounded_refs], axis=0)
    shape = (block_count * machs * TILE, machs * rows)
    row = lax.broadcasted_iota(jnp.int32, shape, 0)
    source = (
        (row // TILE) % machs * rows + row // (TILE * machs) * rhs + row % rhs
    )
    hot = (lax.broadcasted_iota(jnp.int32, shape, 1) == source).astype(jnp.bfloat16)
    left = jnp.dot(hot, every, preferred_element_type=jnp.float32).astype(jnp.bfloat16)
    part = lax.broadcasted_iota(jnp.int32, (TILE, width), 0) // rhs
    per_tile = TILE // rhs
    for i in range(block_count):
        mine = left[i * machs * TILE : (i + 1) * machs * TILE]
        for s in range(splines):
            product = jnp.dot(mine, spline_ref[i, s], preferred_element_type=jnp.float32)
            total = product[:TILE]
            for m in range(1, machs):
                total = total + product[m * TILE : (m + 1) * TILE]
            target = owner_ref[i, s] * struct_count + local_ref[i, s]
            place = target // per_tile
            acc[place] = acc[place] + jnp.where(part == target % per_tile, total, 0.0)
    out_ref[...] = acc[...].reshape(out_ref.shape).astype(jnp.bfloat16)


def inverse_kernel(rhs, got_ref, inverse_ref, out_ref):
    sources, rows, width = got_ref.shape
    total = got_ref[0].astype(jnp.float32)
    for source in range(1, sources):
        total = total + got_ref[source].astype(jnp.float32)
    rounded = total.astype(jnp.bfloat16)
    group_row = lax.broadcasted_iota(jnp.int32, (PACK, width), 0)
    per_group = PACK // rhs
    for g in range(rows // PACK):
        left = rounded[g * PACK : (g + 1) * PACK]
        out = jnp.zeros((PACK, width), jnp.float32)
        for j in range(per_group):
            product = jnp.dot(
                left, inverse_ref[g * per_group + j], preferred_element_type=jnp.float32
            )
            out = jnp.where(group_row // rhs == j, product, out)
        out_ref[g * PACK : (g + 1) * PACK] = out


def on_device(
    adjoint, near_blocks, pattern, trim_mask, spline_blocks, spline_owner, spline_local,
    struct_inverse,
):
    _, block_count, rhs, width = adjoint.shape
    panels, machs = lax.axis_size("panel"), lax.axis_size("mach")
    struct_count = struct_inverse.shape[0]
    rows = block_count * rhs
    own = adjoint.reshape(rows, width)
    half = panels // 2
    mirror = lax.ppermute(own, "panel", [(i, (i + half) % panels) for i in range(panels)])
    cross = lax.ppermute(
        own, "panel", [(i, i - 1 + 2 * (i % 2)) for i in range(1, panels - 1)]
    )
    pair = lax.ppermute(own, "panel", [(i, i + 1 - 2 * (i % 2)) for i in range(panels)])
    params = pltpu.CompilerParams(vmem_limit_bytes=16 * 1024 * 1024)
    loads, rounded = pl.pallas_call(
        functools.partial(near_kernel, panels, rhs),
        out_shape=(
            jax.ShapeDtypeStruct((rows, width), jnp.float32),
            jax.ShapeDtypeStruct((rows, width), jnp.bfloat16),
        ),
        in_specs=[SMEM, SMEM, VMEM, VMEM, VMEM, VMEM, VMEM],
        out_specs=(VMEM, VMEM),
        compiler_params=params,
        name="near_field",
    )(pattern, trim_mask, own, pair, cross, mirror, near_blocks[0])
    every = [rounded]
    for step in range(1, machs):
        every.append(
            lax.ppermute(rounded, "mach", [(i, (i + step) % machs) for i in range(machs)])
        )
    total_rows = panels * struct_count * rhs
    send = pl.pallas_call(
        functools.partial(spline_kernel, rhs, struct_count),
        out_shape=jax.ShapeDtypeStruct((panels, struct_count * rhs, width), jnp.bfloat16),
        in_specs=[SMEM, SMEM] + [VMEM] * (machs + 1),
        out_specs=VMEM,
        scratch_shapes=[pltpu.VMEM((total_rows // TILE, TILE, width), jnp.float32)],
        compiler_params=params,
        name="spline_loads",
    )(spline_owner, spline_local, *every, spline_blocks)
    got = lax.all_to_all(send, "panel", split_axis=0, concat_axis=0, tiled=True)
    struct_adjoint = pl.pallas_call(
        functools.partial(inverse_kernel, rhs),
        out_shape=jax.ShapeDtypeStruct((struct_count * rhs, width), jnp.float32),
        in_specs=[VMEM, VMEM],
        out_specs=VMEM,
        compiler_params=params,
        name="struct_solve",
    )(got, struct_inverse)
    return (
        loads.reshape(1, block_count, rhs, width),
        struct_adjoint.reshape(struct_count, rhs, width),
    )


def solution(mesh):
    in_specs = (
        P("mach", "panel", None, None),
        P("mach", "panel", None, None, None),
        P("panel", None),
        P("mach", None),
        P("panel", None, None, None),
        P("panel", None),
        P("panel", None),
        P("panel", None, None),
    )
    out_specs = (P("mach", "panel", None, None), P("panel", None, None))
    return jax.shard_map(
        on_device, mesh=mesh, in_specs=in_specs, out_specs=out_specs, check_vma=False
    )
```

```python
import functools

import jax
import jax.numpy as jnp
from jax import lax
from jax.experimental import pallas as pl
from jax.experimental.pallas import tpu as pltpu
from jax.sharding import PartitionSpec as P

SMEM = pl.BlockSpec(memory_space=pltpu.SMEM)
VMEM = pl.BlockSpec(memory_space=pltpu.VMEM)
PACK = 16
TILE = 8


def pick_kernel(rhs, pattern_ref, trim_ref, hot_ref, gate_ref):
    block_count, entries = pattern_ref.shape
    shape = hot_ref.shape[1:]
    row = lax.broadcasted_iota(jnp.int32, shape, 0)
    offset = lax.broadcasted_iota(jnp.int32, shape, 1) - row % rhs
    for k in range(entries):
        first = jnp.zeros(shape, jnp.int32)
        for i in range(block_count):
            first = jnp.where(row // rhs == i, pattern_ref[i, k] * rhs, first)
        hot_ref[k] = (offset == first).astype(jnp.bfloat16)
    row = lax.broadcasted_iota(jnp.int32, gate_ref.shape, 0)
    gate = jnp.zeros(gate_ref.shape, jnp.float32)
    for r in range(rhs):
        gate = jnp.where(row % rhs == r, trim_ref[0, r].astype(jnp.float32), gate)
    gate_ref[...] = gate


def near_kernel(rhs, hot_ref, gate_ref, pool_ref, near_ref, loads_ref, rounded_ref):
    entries, rows, _ = hot_ref.shape
    width = pool_ref.shape[1]
    pool = pool_ref[...]
    picked = jnp.concatenate(
        [
            jnp.dot(hot_ref[k], pool, preferred_element_type=jnp.float32).astype(jnp.bfloat16)
            for k in range(entries)
        ],
        axis=1,
    )
    group_row = lax.broadcasted_iota(jnp.int32, (PACK, width), 0)
    per_group = PACK // rhs
    for g in range(rows // PACK):
        left = picked[g * PACK : (g + 1) * PACK]
        loads = jnp.zeros((PACK, width), jnp.float32)
        for j in range(per_group):
            blocks = near_ref[g * per_group + j].reshape(entries * width, width)
            product = jnp.dot(left, blocks, preferred_element_type=jnp.float32)
            loads = jnp.where(group_row // rhs == j, product, loads)
        loads = loads * gate_ref[...]
        loads_ref[g * PACK : (g + 1) * PACK] = loads
        rounded_ref[g * PACK : (g + 1) * PACK] = loads.astype(jnp.bfloat16)


def spline_kernel(
    rhs, struct_count, owner_ref, local_ref, *refs
):
    machs = len(refs) - 3
    rounded_refs, spline_ref, out_ref, acc = refs[:machs], refs[machs], refs[-2], refs[-1]
    block_count, splines = owner_ref.shape
    rows, width = rounded_refs[0].shape
    acc[...] = jnp.zeros(acc.shape, jnp.float32)
    every = jnp.concatenate([ref[...] for ref in rounded_refs], axis=0)
    shape = (block_count * machs * TILE, machs * rows)
    row = lax.broadcasted_iota(jnp.int32, shape, 0)
    source = (
        (row // TILE) % machs * rows + row // (TILE * machs) * rhs + row % rhs
    )
    hot = (lax.broadcasted_iota(jnp.int32, shape, 1) == source).astype(jnp.bfloat16)
    left = jnp.dot(hot, every, preferred_element_type=jnp.float32).astype(jnp.bfloat16)
    part = lax.broadcasted_iota(jnp.int32, (TILE, width), 0) // rhs
    per_tile = TILE // rhs
    for i in range(block_count):
        mine = left[i * machs * TILE : (i + 1) * machs * TILE]
        for s in range(splines):
            product = jnp.dot(mine, spline_ref[i, s], preferred_element_type=jnp.float32)
            total = product[:TILE]
            for m in range(1, machs):
                total = total + product[m * TILE : (m + 1) * TILE]
            target = owner_ref[i, s] * struct_count + local_ref[i, s]
            place = target // per_tile
            acc[place] = acc[place] + jnp.where(part == target % per_tile, total, 0.0)
    out_ref[...] = acc[...].reshape(out_ref.shape).astype(out_ref.dtype)


def inverse_kernel(rhs, got_ref, inverse_ref, out_ref):
    sources, rows, width = got_ref.shape
    total = got_ref[0].astype(jnp.float32)
    for source in range(1, sources):
        total = total + got_ref[source].astype(jnp.float32)
    rounded = total.astype(jnp.bfloat16)
    group_row = lax.broadcasted_iota(jnp.int32, (PACK, width), 0)
    per_group = PACK // rhs
    for g in range(rows // PACK):
        left = rounded[g * PACK : (g + 1) * PACK]
        out = jnp.zeros((PACK, width), jnp.float32)
        for j in range(per_group):
            product = jnp.dot(
                left, inverse_ref[g * per_group + j], preferred_element_type=jnp.float32
            )
            out = jnp.where(group_row // rhs == j, product, out)
        out_ref[g * PACK : (g + 1) * PACK] = out


def on_device(
    adjoint, near_blocks, pattern, trim_mask, spline_blocks, spline_owner, spline_local,
    struct_inverse,
):
    _, block_count, rhs, width = adjoint.shape
    panels, machs = lax.axis_size("panel"), lax.axis_size("mach")
    struct_count = struct_inverse.shape[0]
    rows = block_count * rhs
    own = adjoint.reshape(rows, width)
    pool = lax.all_gather(own, "panel", axis=0, tiled=True)
    entries = pattern.shape[1]
    params = pltpu.CompilerParams(vmem_limit_bytes=16 * 1024 * 1024)
    hot, gate = pl.pallas_call(
        functools.partial(pick_kernel, rhs),
        out_shape=(
            jax.ShapeDtypeStruct((entries, rows, panels * rows), jnp.bfloat16),
            jax.ShapeDtypeStruct((PACK, width), jnp.float32),
        ),
        in_specs=[SMEM, SMEM],
        out_specs=(VMEM, VMEM),
        compiler_params=params,
        cost_estimate=pl.CostEstimate(flops=4 * 10**9, bytes_accessed=16 * 2**20, transcendentals=0),
        name="pick_rows",
    )(pattern, trim_mask)
    loads, rounded = pl.pallas_call(
        functools.partial(near_kernel, rhs),
        out_shape=(
            jax.ShapeDtypeStruct((rows, width), jnp.float32),
            jax.ShapeDtypeStruct((rows, width), jnp.bfloat16),
        ),
        in_specs=[VMEM] * 4,
        out_specs=(VMEM, VMEM),
        compiler_params=params,
        cost_estimate=pl.CostEstimate(flops=2 * 10**9, bytes_accessed=4 * 2**20, transcendentals=0),
        name="near_field",
    )(hot, gate, pool, near_blocks[0])
    every = [rounded]
    for step in range(1, machs):
        every.append(
            lax.ppermute(rounded, "mach", [(i, (i + step) % machs) for i in range(machs)])
        )
    total_rows = panels * struct_count * rhs
    send = pl.pallas_call(
        functools.partial(spline_kernel, rhs, struct_count),
        out_shape=jax.ShapeDtypeStruct((panels, struct_count * rhs, width), jnp.float32),
        in_specs=[SMEM, SMEM] + [VMEM] * (machs + 1),
        out_specs=VMEM,
        scratch_shapes=[pltpu.VMEM((total_rows // TILE, TILE, width), jnp.float32)],
        compiler_params=params,
        name="spline_loads",
    )(spline_owner, spline_local, *every, spline_blocks)
    got = lax.psum_scatter(send, "panel", scatter_dimension=0, tiled=True)
    struct_adjoint = pl.pallas_call(
        functools.partial(inverse_kernel, rhs),
        out_shape=jax.ShapeDtypeStruct((struct_count * rhs, width), jnp.float32),
        in_specs=[VMEM, VMEM],
        out_specs=VMEM,
        compiler_params=params,
        name="struct_solve",
    )(got, struct_inverse)
    return (
        loads.reshape(1, block_count, rhs, width),
        struct_adjoint.reshape(struct_count, rhs, width),
    )


def solution(mesh):
    in_specs = (
        P("mach", "panel", None, None),
        P("mach", "panel", None, None, None),
        P("panel", None),
        P("mach", None),
        P("panel", None, None, None),
        P("panel", None),
        P("panel", None),
        P("panel", None, None),
    )
    out_specs = (P("mach", "panel", None, None), P("panel", None, None))
    return jax.shard_map(
        on_device, mesh=mesh, in_specs=in_specs, out_specs=out_specs, check_vma=False
    )
```

```python
import functools

import jax
import jax.numpy as jnp
from jax import lax
from jax.experimental import pallas as pl
from jax.experimental.pallas import tpu as pltpu
from jax.sharding import PartitionSpec as P

SMEM = pl.BlockSpec(memory_space=pltpu.SMEM)
VMEM = pl.BlockSpec(memory_space=pltpu.VMEM)
PACK = 16
TILE = 8


def pick_kernel(panels, rhs, pattern_ref, trim_ref, own_ref, hot_ref, gate_ref, held_ref):
    block_count, entries = pattern_ref.shape
    here = lax.axis_index("panel")
    shape = hot_ref.shape[1:]
    row = lax.broadcasted_iota(jnp.int32, shape, 0)
    offset = lax.broadcasted_iota(jnp.int32, shape, 1) - row % rhs
    for k in range(entries):
        first = jnp.zeros(shape, jnp.int32)
        for i in range(block_count):
            block = pattern_ref[i, k]
            apart = (block // block_count) ^ here
            slot = jnp.where(
                apart == 0, 0, jnp.where(apart == panels // 2, 3, jnp.where(apart == 1, 1, 2))
            )
            base = (slot * block_count + block % block_count) * rhs
            first = jnp.where(row // rhs == i, base, first)
        hot_ref[k] = (offset == first).astype(jnp.bfloat16)
    row = lax.broadcasted_iota(jnp.int32, gate_ref.shape, 0)
    gate = jnp.zeros(gate_ref.shape, jnp.float32)
    for r in range(rhs):
        gate = jnp.where(row % rhs == r, trim_ref[0, r].astype(jnp.float32), gate)
    gate_ref[...] = gate
    held_ref[...] = own_ref[...]


def near_kernel(
    rhs, hot_ref, gate_ref, own_ref, pair_ref, cross_ref, mirror_ref, near_ref,
    loads_ref, rounded_ref,
):
    entries, rows, _ = hot_ref.shape
    width = own_ref.shape[1]
    pool = jnp.concatenate(
        [own_ref[...], pair_ref[...], cross_ref[...], mirror_ref[...]], axis=0
    )
    picked = jnp.concatenate(
        [
            jnp.dot(hot_ref[k], pool, preferred_element_type=jnp.float32).astype(jnp.bfloat16)
            for k in range(entries)
        ],
        axis=1,
    )
    group_row = lax.broadcasted_iota(jnp.int32, (PACK, width), 0)
    per_group = PACK // rhs
    for g in range(rows // PACK):
        left = picked[g * PACK : (g + 1) * PACK]
        loads = jnp.zeros((PACK, width), jnp.float32)
        for j in range(per_group):
            blocks = near_ref[g * per_group + j].reshape(entries * width, width)
            product = jnp.dot(left, blocks, preferred_element_type=jnp.float32)
            loads = jnp.where(group_row // rhs == j, product, loads)
        loads = loads * gate_ref[...]
        loads_ref[g * PACK : (g + 1) * PACK] = loads
        rounded_ref[g * PACK : (g + 1) * PACK] = loads.astype(jnp.bfloat16)


def spline_kernel(machs, rhs, struct_count, owner_ref, local_ref, *refs):
    rounded_refs, spline_ref, out_refs, acc = refs[:machs], refs[machs], refs[machs + 1 : -1], refs[-1]
    block_count, splines = owner_ref.shape
    rows, width = rounded_refs[0].shape
    near_by = len(out_refs)
    here = lax.axis_index("panel")
    acc[...] = jnp.zeros(acc.shape, jnp.float32)
    every = jnp.concatenate([ref[...] for ref in rounded_refs], axis=0)
    shape = (block_count * machs * TILE, machs * rows)
    row = lax.broadcasted_iota(jnp.int32, shape, 0)
    source = (
        (row // TILE) % machs * rows + row // (TILE * machs) * rhs + row % rhs
    )
    hot = (lax.broadcasted_iota(jnp.int32, shape, 1) == source).astype(jnp.bfloat16)
    left = jnp.dot(hot, every, preferred_element_type=jnp.float32).astype(jnp.bfloat16)
    part = lax.broadcasted_iota(jnp.int32, (TILE, width), 0) // rhs
    per_tile = TILE // rhs
    tiles = acc.shape[1]
    owner_tiles = struct_count // per_tile
    for i in range(block_count):
        mine = left[i * machs * TILE : (i + 1) * machs * TILE]
        for s in range(splines):
            product = jnp.dot(mine, spline_ref[i, s], preferred_element_type=jnp.float32)
            total = product[:TILE]
            for m in range(1, machs):
                total = total + product[m * TILE : (m + 1) * TILE]
            apart = owner_ref[i, s] ^ here
            local = local_ref[i, s]
            group = apart % near_by
            place = apart // near_by * owner_tiles + local // per_tile
            acc[group, place] = acc[group, place] + jnp.where(
                part == local % per_tile, total, 0.0
            )
    for group, out_ref in enumerate(out_refs):
        out_ref[...] = acc[group].reshape(out_ref.shape).astype(out_ref.dtype)


def sum_kernel(near_by, *refs):
    in_refs, out_refs = refs[:near_by], refs[near_by:]
    for step, out_ref in enumerate(out_refs):
        total = in_refs[0][step]
        for ref in in_refs[1:]:
            total = total + ref[step].astype(jnp.float32)
        out_ref[...] = total.astype(out_ref.dtype)


def inverse_kernel(rhs, *refs):
    in_refs, inverse_ref, out_ref = refs[:-2], refs[-2], refs[-1]
    total = in_refs[0][...]
    for ref in in_refs[1:]:
        total = total + ref[...].astype(jnp.float32)
    rows, width = total.shape
    rounded = total.astype(jnp.bfloat16)
    group_row = lax.broadcasted_iota(jnp.int32, (PACK, width), 0)
    per_group = PACK // rhs
    for g in range(rows // PACK):
        left = rounded[g * PACK : (g + 1) * PACK]
        out = jnp.zeros((PACK, width), jnp.float32)
        for j in range(per_group):
            product = jnp.dot(
                left, inverse_ref[g * per_group + j], preferred_element_type=jnp.float32
            )
            out = jnp.where(group_row // rhs == j, product, out)
        out_ref[g * PACK : (g + 1) * PACK] = out


def swap(value, panels, apart):
    return lax.ppermute(value, "panel", [(i, i ^ apart) for i in range(panels)])


def cost(flops, size):
    return pl.CostEstimate(flops=flops, bytes_accessed=size, transcendentals=0)


def on_device(
    adjoint, near_blocks, pattern, trim_mask, spline_blocks, spline_owner, spline_local,
    struct_inverse,
):
    _, block_count, rhs, width = adjoint.shape
    entries = pattern.shape[1]
    panels, machs = lax.axis_size("panel"), lax.axis_size("mach")
    struct_count = struct_inverse.shape[0]
    rows, struct_rows = block_count * rhs, struct_count * rhs
    params = pltpu.CompilerParams(vmem_limit_bytes=16 * 1024 * 1024)
    f32, bf16 = jnp.float32, jnp.bfloat16
    own = adjoint.reshape(rows, width)
    mirror = swap(own, panels, panels // 2)
    cross = lax.ppermute(
        own, "panel", [(i, i - 1 + 2 * (i % 2)) for i in range(1, panels - 1)]
    )
    pair = swap(own, panels, 1)
    hot, gate, held = pl.pallas_call(
        functools.partial(pick_kernel, panels, rhs),
        out_shape=(
            jax.ShapeDtypeStruct((entries, rows, 4 * rows), bf16),
            jax.ShapeDtypeStruct((PACK, width), f32),
            jax.ShapeDtypeStruct((rows, width), bf16),
        ),
        in_specs=[SMEM, SMEM, VMEM],
        out_specs=(VMEM, VMEM, VMEM),
        compiler_params=params,
        cost_estimate=cost(4 * 10**9, 16 * 2**20),
        name="pick_rows",
    )(pattern, trim_mask, own)
    loads, rounded = pl.pallas_call(
        functools.partial(near_kernel, rhs),
        out_shape=(
            jax.ShapeDtypeStruct((rows, width), f32),
            jax.ShapeDtypeStruct((rows, width), bf16),
        ),
        in_specs=[VMEM] * 7,
        out_specs=(VMEM, VMEM),
        compiler_params=params,
        cost_estimate=cost(2 * 10**9, 4 * 2**20),
        name="near_field",
    )(hot, gate, held, pair, cross, mirror, near_blocks[0])
    every = [rounded]
    for step in range(1, machs):
        every.append(
            lax.ppermute(rounded, "mach", [(i, (i + step) % machs) for i in range(machs)])
        )
    near_by = 1 << ((panels.bit_length() - 1) // 2)
    far = panels // near_by
    parts = pl.pallas_call(
        functools.partial(spline_kernel, machs, rhs, struct_count),
        out_shape=tuple(
            jax.ShapeDtypeStruct((far, struct_rows, width), f32 if group == 0 else bf16)
            for group in range(near_by)
        ),
        in_specs=[SMEM, SMEM] + [VMEM] * (machs + 1),
        out_specs=(VMEM,) * near_by,
        scratch_shapes=[pltpu.VMEM((near_by, far * struct_rows // TILE, TILE, width), f32)],
        compiler_params=params,
        cost_estimate=cost(2 * 10**9, 4 * 2**20),
        name="spline_loads",
    )(spline_owner, spline_local, *every, spline_blocks)
    got = [parts[0]] + [swap(parts[step], panels, step) for step in range(1, near_by)]
    sums = pl.pallas_call(
        functools.partial(sum_kernel, near_by),
        out_shape=tuple(
            jax.ShapeDtypeStruct((struct_rows, width), f32 if step == 0 else bf16)
            for step in range(far)
        ),
        in_specs=[VMEM] * near_by,
        out_specs=(VMEM,) * far,
        compiler_params=params,
        cost_estimate=cost(10**6, 2**20),
        name="group_sum",
    )(*got)
    got = [sums[0]] + [swap(sums[step], panels, step * near_by) for step in range(1, far)]
    struct_adjoint = pl.pallas_call(
        functools.partial(inverse_kernel, rhs),
        out_shape=jax.ShapeDtypeStruct((struct_rows, width), f32),
        in_specs=[VMEM] * (far + 1),
        out_specs=VMEM,
        compiler_params=params,
        name="struct_solve",
    )(*got, struct_inverse)
    return (
        loads.reshape(1, block_count, rhs, width),
        struct_adjoint.reshape(struct_count, rhs, width),
    )


def solution(mesh):
    in_specs = (
        P("mach", "panel", None, None),
        P("mach", "panel", None, None, None),
        P("panel", None),
        P("mach", None),
        P("panel", None, None, None),
        P("panel", None),
        P("panel", None),
        P("panel", None, None),
    )
    out_specs = (P("mach", "panel", None, None), P("panel", None, None))
    return jax.shard_map(
        on_device, mesh=mesh, in_specs=in_specs, out_specs=out_specs, check_vma=False
    )
```

```python
import functools

import jax
import jax.numpy as jnp
from jax import lax
from jax.experimental import pallas as pl
from jax.experimental.pallas import tpu as pltpu
from jax.sharding import PartitionSpec as P

SMEM = pl.BlockSpec(memory_space=pltpu.SMEM)
VMEM = pl.BlockSpec(memory_space=pltpu.VMEM)
PACK = 16
TILE = 8


def spread_kernel(machs, rhs, block_count, expand_ref, order_ref):
    shape = expand_ref.shape
    expand_ref[...] = (
        lax.broadcasted_iota(jnp.int32, shape, 0) // rhs == lax.broadcasted_iota(jnp.int32, shape, 1)
    ).astype(jnp.bfloat16)
    shape = order_ref.shape
    row = lax.broadcasted_iota(jnp.int32, shape, 0)
    source = (
        (row // TILE) % machs * (block_count * rhs) + row // (TILE * machs) * rhs + row % rhs
    )
    order_ref[...] = (lax.broadcasted_iota(jnp.int32, shape, 1) == source).astype(jnp.bfloat16)


def pick_kernel(
    panels, rhs, expand_ref, pattern_ref, trim_ref, own_ref, hot_ref, gate_ref, held_ref
):
    block_count, entries = pattern_ref.shape
    rows = own_ref.shape[0]
    here = lax.axis_index("panel")
    shape = (rows, hot_ref.shape[1])
    offset = lax.broadcasted_iota(jnp.int32, shape, 1) - (
        lax.broadcasted_iota(jnp.int32, shape, 0) % rhs
    )
    block = pattern_ref[...]
    apart = (block // block_count) ^ here
    slot = jnp.where(
        apart == 0, 0, jnp.where(apart == panels // 2, 3, jnp.where(apart == 1, 1, 2))
    )
    first = (slot * block_count + block % block_count) * rhs
    first = jnp.dot(
        expand_ref[...],
        first.astype(jnp.float32).astype(jnp.bfloat16),
        preferred_element_type=jnp.float32,
    ).astype(jnp.int32)
    for k in range(entries):
        hot_ref[k * rows : (k + 1) * rows] = (offset == first[:, k : k + 1]).astype(jnp.bfloat16)
    shape = (gate_ref.shape[0], rhs)
    mine = lax.broadcasted_iota(jnp.int32, shape, 0) % rhs == lax.broadcasted_iota(
        jnp.int32, shape, 1
    )
    gate = jnp.sum(jnp.where(mine, trim_ref[...], 0).astype(jnp.float32), axis=1, keepdims=True)
    gate_ref[...] = jnp.broadcast_to(gate, gate_ref.shape)
    held_ref[...] = own_ref[...]


def grouped_product(rhs, left, blocks_of, group):
    per_group = PACK // rhs
    every = jnp.concatenate([blocks_of(group * per_group + j) for j in range(per_group)], axis=1)
    product = jnp.dot(left, every, preferred_element_type=jnp.float32)
    width = product.shape[1] // per_group
    row = lax.broadcasted_iota(jnp.int32, (PACK, width), 0)
    out = product[:, :width]
    for j in range(1, per_group):
        out = jnp.where(row // rhs == j, product[:, j * width : (j + 1) * width], out)
    return out


def near_kernel(
    rhs, hot_ref, gate_ref, own_ref, pair_ref, cross_ref, mirror_ref, near_ref,
    loads_ref, rounded_ref,
):
    rows, width = own_ref.shape
    entries = hot_ref.shape[0] // rows
    pool = jnp.concatenate(
        [own_ref[...], pair_ref[...], cross_ref[...], mirror_ref[...]], axis=0
    )
    picked = jnp.dot(hot_ref[...], pool, preferred_element_type=jnp.float32)
    picked = picked.astype(jnp.bfloat16)
    for g in range(rows // PACK):
        left = jnp.concatenate(
            [picked[k * rows + g * PACK : k * rows + (g + 1) * PACK] for k in range(entries)],
            axis=1,
        )
        loads = gate_ref[...] * grouped_product(
            rhs, left, lambda i: near_ref[i].reshape(entries * width, width), g
        )
        loads_ref[g * PACK : (g + 1) * PACK] = loads
        rounded_ref[g * PACK : (g + 1) * PACK] = loads.astype(jnp.bfloat16)


def spline_kernel(machs, rhs, struct_count, owner_ref, local_ref, order_ref, *refs):
    rounded_refs, spline_ref, keep_ref, send_ref, acc = refs[:machs], *refs[machs:]
    block_count, splines = owner_ref.shape
    rows, width = rounded_refs[0].shape
    here = lax.axis_index("panel")
    acc[...] = jnp.zeros(acc.shape, jnp.float32)
    every = jnp.concatenate([ref[...] for ref in rounded_refs], axis=0)
    left = jnp.dot(order_ref[...], every, preferred_element_type=jnp.float32)
    left = left.astype(jnp.bfloat16)
    part = lax.broadcasted_iota(jnp.int32, (TILE, width), 0) // rhs
    per_tile = TILE // rhs
    owner_tiles = struct_count // per_tile
    height = machs * TILE
    blank = jnp.zeros((height, width), jnp.bfloat16)
    for pair in range(0, block_count, 2):
        mine = left[pair * height : (pair + 2) * height]
        mine = jnp.concatenate(
            [
                jnp.concatenate([mine[:height], blank], axis=1),
                jnp.concatenate([blank, mine[height:]], axis=1),
            ],
            axis=0,
        )
        blocks = jnp.concatenate(
            [
                jnp.concatenate([spline_ref[i, s] for s in range(splines)], axis=1)
                for i in (pair, pair + 1)
            ],
            axis=0,
        )
        product = jnp.dot(mine, blocks, preferred_element_type=jnp.float32)
        for i in (pair, pair + 1):
            total = product[(i - pair) * height : (i - pair) * height + TILE]
            for m in range(1, machs):
                start = (i - pair) * height + m * TILE
                total = total + product[start : start + TILE]
            places, sums = [], []
            for s in range(splines):
                apart = owner_ref[i, s] ^ here
                local = local_ref[i, s]
                place = (apart % 2, apart // 2 * owner_tiles + local // per_tile)
                added = jnp.where(
                    part == local % per_tile, total[:, s * width : (s + 1) * width], 0.0
                )
                places.append(place)
                sums.append(acc[place] + added)
            for place, value in zip(places, sums):
                acc[place] = value
    keep_ref[...] = acc[0].reshape(keep_ref.shape)
    send_ref[...] = acc[1].reshape(send_ref.shape).astype(send_ref.dtype)


def sum_kernel(held_ref, got_ref, keep_ref, send_ref):
    for place in range(held_ref.shape[0]):
        total = held_ref[place] + got_ref[place].astype(jnp.float32)
        if place % 2 == 0:
            keep_ref[place // 2] = total
        else:
            send_ref[place // 2] = total.astype(send_ref.dtype)


def inverse_kernel(rhs, held_ref, got_ref, inverse_ref, out_ref):
    total = held_ref[0] + got_ref[0].astype(jnp.float32)
    rounded = total.astype(jnp.bfloat16)
    for g in range(total.shape[0] // PACK):
        out_ref[g * PACK : (g + 1) * PACK] = grouped_product(
            rhs, rounded[g * PACK : (g + 1) * PACK], lambda t: inverse_ref[t], g
        )


def swap(value, panels, apart):
    return lax.ppermute(value, "panel", [(i, i ^ apart) for i in range(panels)])


def cost(flops, size):
    return pl.CostEstimate(flops=flops, bytes_accessed=size, transcendentals=0)


def on_device(
    adjoint, near_blocks, pattern, trim_mask, spline_blocks, spline_owner, spline_local,
    struct_inverse,
):
    _, block_count, rhs, width = adjoint.shape
    entries = pattern.shape[1]
    panels, machs = lax.axis_size("panel"), lax.axis_size("mach")
    struct_count = struct_inverse.shape[0]
    rows, struct_rows = block_count * rhs, struct_count * rhs
    params = pltpu.CompilerParams(vmem_limit_bytes=16 * 1024 * 1024)
    f32, bf16 = jnp.float32, jnp.bfloat16
    own = adjoint.reshape(rows, width)
    mirror = swap(own, panels, panels // 2)
    cross = lax.ppermute(
        own, "panel", [(i, min(max(i - 1 + 2 * (i % 2), 0), panels - 1)) for i in range(panels)]
    )
    pair = swap(own, panels, 1)
    expand, order = pl.pallas_call(
        functools.partial(spread_kernel, machs, rhs, block_count),
        out_shape=(
            jax.ShapeDtypeStruct((rows, block_count), bf16),
            jax.ShapeDtypeStruct((block_count * machs * TILE, machs * rows), bf16),
        ),
        out_specs=(VMEM, VMEM),
        compiler_params=params,
        cost_estimate=cost(4 * 10**9, 16 * 2**20),
        name="row_order",
    )()
    hot, gate, held = pl.pallas_call(
        functools.partial(pick_kernel, panels, rhs),
        out_shape=(
            jax.ShapeDtypeStruct((entries * rows, 4 * rows), bf16),
            jax.ShapeDtypeStruct((PACK, width), f32),
            jax.ShapeDtypeStruct((rows, width), bf16),
        ),
        in_specs=[VMEM] * 4,
        out_specs=(VMEM, VMEM, VMEM),
        compiler_params=params,
        cost_estimate=cost(10**6, 2**17),
        name="pick_rows",
    )(expand, pattern, trim_mask, own)
    loads, rounded = pl.pallas_call(
        functools.partial(near_kernel, rhs),
        out_shape=(
            jax.ShapeDtypeStruct((rows, width), f32),
            jax.ShapeDtypeStruct((rows, width), bf16),
        ),
        in_specs=[VMEM] * 7,
        out_specs=(VMEM, VMEM),
        compiler_params=params,
        cost_estimate=cost(2 * 10**9, 4 * 2**20),
        name="near_field",
    )(hot, gate, held, pair, cross, mirror, near_blocks[0])
    every = [rounded]
    for step in range(1, machs):
        every.append(
            lax.ppermute(rounded, "mach", [(i, (i + step) % machs) for i in range(machs)])
        )
    half = (panels // 2, struct_rows, width)
    keep, send = pl.pallas_call(
        functools.partial(spline_kernel, machs, rhs, struct_count),
        out_shape=(jax.ShapeDtypeStruct(half, f32), jax.ShapeDtypeStruct(half, bf16)),
        in_specs=[SMEM, SMEM] + [VMEM] * (machs + 2),
        out_specs=(VMEM, VMEM),
        scratch_shapes=[pltpu.VMEM((2, panels // 2 * struct_rows // TILE, TILE, width), f32)],
        compiler_params=params,
        cost_estimate=cost(2 * 10**9, 4 * 2**20),
        name="spline_loads",
    )(spline_owner, spline_local, order, *every, spline_blocks)
    apart = 1
    got = swap(send, panels, apart)
    while 2 * apart < panels:
        apart *= 2
        half = (panels // (2 * apart), struct_rows, width)
        keep, send = pl.pallas_call(
            sum_kernel,
            out_shape=(jax.ShapeDtypeStruct(half, f32), jax.ShapeDtypeStruct(half, bf16)),
            in_specs=[VMEM, VMEM],
            out_specs=(VMEM, VMEM),
            compiler_params=params,
            cost_estimate=cost(10**6, 2**20),
            name="pair_sum",
        )(keep, got)
        got = swap(send, panels, apart)
    struct_adjoint = pl.pallas_call(
        functools.partial(inverse_kernel, rhs),
        out_shape=jax.ShapeDtypeStruct((struct_rows, width), f32),
        in_specs=[VMEM] * 3,
        out_specs=VMEM,
        compiler_params=params,
        cost_estimate=cost(10**9, 2**20),
        name="struct_solve",
    )(keep, got, struct_inverse)
    return (
        loads.reshape(1, block_count, rhs, width),
        struct_adjoint.reshape(struct_count, rhs, width),
    )


def solution(mesh):
    in_specs = (
        P("mach", "panel", None, None),
        P("mach", "panel", None, None, None),
        P("panel", None),
        P("mach", None),
        P("panel", None, None, None),
        P("panel", None),
        P("panel", None),
        P("panel", None, None),
    )
    out_specs = (P("mach", "panel", None, None), P("panel", None, None))
    return jax.shard_map(
        on_device, mesh=mesh, in_specs=in_specs, out_specs=out_specs, check_vma=False
    )
```

```python
import functools

import jax
import jax.numpy as jnp
from jax import lax
from jax.experimental import pallas as pl
from jax.experimental.pallas import tpu as pltpu
from jax.sharding import PartitionSpec as P

SMEM = pl.BlockSpec(memory_space=pltpu.SMEM)
VMEM = pl.BlockSpec(memory_space=pltpu.VMEM)
PACK = 16
TILE = 8


def spread_kernel(rhs, expand_ref, order_ref):
    shape = expand_ref.shape
    expand_ref[...] = (
        lax.broadcasted_iota(jnp.int32, shape, 0) // rhs == lax.broadcasted_iota(jnp.int32, shape, 1)
    ).astype(jnp.bfloat16)
    shape = order_ref.shape
    row = lax.broadcasted_iota(jnp.int32, shape, 0)
    source = row // TILE * rhs + row % rhs
    order_ref[...] = (lax.broadcasted_iota(jnp.int32, shape, 1) == source).astype(jnp.bfloat16)


def pick_kernel(
    panels, rhs, expand_ref, pattern_ref, trim_ref, own_ref, hot_ref, gate_ref, held_ref
):
    block_count, entries = pattern_ref.shape
    rows = own_ref.shape[0]
    here = lax.axis_index("panel")
    shape = (rows, hot_ref.shape[1])
    offset = lax.broadcasted_iota(jnp.int32, shape, 1) - (
        lax.broadcasted_iota(jnp.int32, shape, 0) % rhs
    )
    block = pattern_ref[...]
    apart = (block // block_count) ^ here
    slot = jnp.where(
        apart == 0, 0, jnp.where(apart == panels // 2, 3, jnp.where(apart == 1, 1, 2))
    )
    first = (slot * block_count + block % block_count) * rhs
    first = jnp.dot(
        expand_ref[...],
        first.astype(jnp.float32).astype(jnp.bfloat16),
        preferred_element_type=jnp.float32,
    ).astype(jnp.int32)
    for k in range(entries):
        hot_ref[k * rows : (k + 1) * rows] = (offset == first[:, k : k + 1]).astype(jnp.bfloat16)
    shape = (gate_ref.shape[0], rhs)
    mine = lax.broadcasted_iota(jnp.int32, shape, 0) % rhs == lax.broadcasted_iota(
        jnp.int32, shape, 1
    )
    gate = jnp.sum(jnp.where(mine, trim_ref[...], 0).astype(jnp.float32), axis=1, keepdims=True)
    gate_ref[...] = jnp.broadcast_to(gate, gate_ref.shape)
    held_ref[...] = own_ref[...]


def grouped_product(rhs, left, blocks_of, group):
    per_group = PACK // rhs
    every = jnp.concatenate([blocks_of(group * per_group + j) for j in range(per_group)], axis=1)
    product = jnp.dot(left, every, preferred_element_type=jnp.float32)
    width = product.shape[1] // per_group
    row = lax.broadcasted_iota(jnp.int32, (PACK, width), 0)
    out = product[:, :width]
    for j in range(1, per_group):
        out = jnp.where(row // rhs == j, product[:, j * width : (j + 1) * width], out)
    return out


def near_kernel(
    rhs, hot_ref, gate_ref, own_ref, pair_ref, cross_ref, mirror_ref, near_ref,
    loads_ref, rounded_ref,
):
    rows, width = own_ref.shape
    entries = hot_ref.shape[0] // rows
    pool = jnp.concatenate(
        [own_ref[...], pair_ref[...], cross_ref[...], mirror_ref[...]], axis=0
    )
    picked = jnp.dot(hot_ref[...], pool, preferred_element_type=jnp.float32)
    picked = picked.astype(jnp.bfloat16)
    for g in range(rows // PACK):
        left = jnp.concatenate(
            [picked[k * rows + g * PACK : k * rows + (g + 1) * PACK] for k in range(entries)],
            axis=1,
        )
        loads = gate_ref[...] * grouped_product(
            rhs, left, lambda i: near_ref[i].reshape(entries * width, width), g
        )
        loads_ref[g * PACK : (g + 1) * PACK] = loads
        rounded_ref[g * PACK : (g + 1) * PACK] = loads.astype(jnp.bfloat16)


def spline_kernel(
    rhs, struct_count, owner_ref, local_ref, order_ref, rounded_ref, spline_ref,
    keep_ref, send_ref, acc,
):
    block_count, splines = owner_ref.shape
    width = rounded_ref.shape[1]
    here = lax.axis_index("panel")
    acc[...] = jnp.zeros(acc.shape, jnp.float32)
    left = jnp.dot(order_ref[...], rounded_ref[...], preferred_element_type=jnp.float32)
    left = left.astype(jnp.bfloat16)
    part = lax.broadcasted_iota(jnp.int32, (TILE, width), 0) // rhs
    per_tile = TILE // rhs
    owner_tiles = struct_count // per_tile
    height = TILE
    blank = jnp.zeros((height, width), jnp.bfloat16)
    for pair in range(0, block_count, 2):
        mine = left[pair * height : (pair + 2) * height]
        mine = jnp.concatenate(
            [
                jnp.concatenate([mine[:height], blank], axis=1),
                jnp.concatenate([blank, mine[height:]], axis=1),
            ],
            axis=0,
        )
        blocks = jnp.concatenate(
            [
                jnp.concatenate([spline_ref[i, s] for s in range(splines)], axis=1)
                for i in (pair, pair + 1)
            ],
            axis=0,
        )
        product = jnp.dot(mine, blocks, preferred_element_type=jnp.float32)
        for i in (pair, pair + 1):
            total = product[(i - pair) * height : (i - pair + 1) * height]
            places, sums = [], []
            for s in range(splines):
                apart = owner_ref[i, s] ^ (here - here % 2)
                local = local_ref[i, s]
                place = apart * owner_tiles + local // per_tile
                added = jnp.where(
                    part == local % per_tile, total[:, s * width : (s + 1) * width], 0.0
                )
                places.append(place)
                sums.append(acc[place] + added)
            for place, value in zip(places, sums):
                acc[place] = value
    total = acc[...].reshape(keep_ref.shape)
    keep_ref[...] = total
    send_ref[...] = total.astype(send_ref.dtype)


def split_kernel(held_ref, got_ref, *out_refs):
    size = out_refs[0].shape[0]
    for step, out_ref in enumerate(out_refs):
        for place in range(size):
            total = held_ref[step * size + place] + got_ref[step * size + place].astype(jnp.float32)
            out_ref[place] = total.astype(out_ref.dtype)


def column_kernel(held_ref, *refs):
    got_refs, out_refs = refs[:-2], refs[-2:]
    size = out_refs[0].shape[0]
    for place in range(held_ref.shape[0]):
        total = held_ref[place]
        for got_ref in got_refs:
            total = total + got_ref[place].astype(jnp.float32)
        out_ref = out_refs[place // size]
        out_ref[place % size] = total.astype(out_ref.dtype)


def round_kernel(machs, *refs):
    same_refs, other_refs, out_refs = refs[:machs], refs[machs : 2 * machs], refs[2 * machs :]
    for place, out_ref in enumerate(out_refs):
        parts = [
            same[place].astype(jnp.float32) + other[place].astype(jnp.float32)
            for same, other in zip(same_refs, other_refs)
        ]
        out_ref[...] = sum(parts[1:], parts[0]).astype(out_ref.dtype)


def inverse_kernel(rhs, mine_ref, got_ref, inverse_ref, out_ref):
    leads = jnp.broadcast_to(lax.axis_index("panel") % 2, mine_ref.shape) == 1
    rounded = jnp.where(leads, mine_ref[...].astype(jnp.float32), got_ref[...].astype(jnp.float32))
    rounded = rounded.astype(jnp.bfloat16)
    for g in range(rounded.shape[0] // PACK):
        out_ref[g * PACK : (g + 1) * PACK] = grouped_product(
            rhs, rounded[g * PACK : (g + 1) * PACK], lambda t: inverse_ref[t], g
        )


def swap(value, panels, apart):
    return lax.ppermute(value, "panel", [(i, i ^ apart) for i in range(panels)])


def leader_swap(value, machs, panels, turn, apart):
    pairs = [
        (m * panels + i, (m + turn) % machs * panels + (i ^ apart))
        for m in range(machs)
        for i in range(1, panels, 2)
    ]
    return lax.ppermute(value, ("mach", "panel"), pairs)


def cost(flops, size):
    return pl.CostEstimate(flops=flops, bytes_accessed=size, transcendentals=0)


def on_device(
    adjoint, near_blocks, pattern, trim_mask, spline_blocks, spline_owner, spline_local,
    struct_inverse,
):
    _, block_count, rhs, width = adjoint.shape
    entries = pattern.shape[1]
    panels, machs = lax.axis_size("panel"), lax.axis_size("mach")
    struct_count = struct_inverse.shape[0]
    rows, struct_rows = block_count * rhs, struct_count * rhs
    params = pltpu.CompilerParams(vmem_limit_bytes=16 * 1024 * 1024)
    f32, bf16 = jnp.float32, jnp.bfloat16
    own = adjoint.reshape(rows, width)
    expand, order = pl.pallas_call(
        functools.partial(spread_kernel, rhs),
        out_shape=(
            jax.ShapeDtypeStruct((rows, block_count), bf16),
            jax.ShapeDtypeStruct((block_count * TILE, rows), bf16),
        ),
        out_specs=(VMEM, VMEM),
        compiler_params=params,
        cost_estimate=cost(4 * 10**9, 16 * 2**20),
        name="row_order",
    )()
    hot, gate, held = pl.pallas_call(
        functools.partial(pick_kernel, panels, rhs),
        out_shape=(
            jax.ShapeDtypeStruct((entries * rows, 4 * rows), bf16),
            jax.ShapeDtypeStruct((PACK, width), f32),
            jax.ShapeDtypeStruct((rows, width), bf16),
        ),
        in_specs=[VMEM] * 4,
        out_specs=(VMEM, VMEM, VMEM),
        compiler_params=params,
        cost_estimate=cost(10**6, 2**17),
        name="pick_rows",
    )(expand, pattern, trim_mask, own)
    mirror = swap(held, panels, panels // 2)
    cross = lax.ppermute(
        held, "panel", [(i, i - 1 + 2 * (i % 2)) for i in range(1, panels - 1)]
    )
    pair = swap(held, panels, 1)
    loads, rounded = pl.pallas_call(
        functools.partial(near_kernel, rhs),
        out_shape=(
            jax.ShapeDtypeStruct((rows, width), f32),
            jax.ShapeDtypeStruct((rows, width), bf16),
        ),
        in_specs=[VMEM] * 7,
        out_specs=(VMEM, VMEM),
        compiler_params=params,
        cost_estimate=cost(2 * 10**9, 4 * 2**20),
        name="near_field",
    )(hot, gate, held, pair, cross, mirror, near_blocks[0])
    whole = (panels, struct_rows, width)
    keep, send = pl.pallas_call(
        functools.partial(spline_kernel, rhs, struct_count),
        out_shape=(jax.ShapeDtypeStruct(whole, f32), jax.ShapeDtypeStruct(whole, bf16)),
        in_specs=[SMEM, SMEM, VMEM, VMEM, VMEM],
        out_specs=(VMEM, VMEM),
        scratch_shapes=[pltpu.VMEM((panels * struct_rows // TILE, TILE, width), f32)],
        compiler_params=params,
        cost_estimate=cost(2 * 10**9, 4 * 2**20),
        name="spline_loads",
    )(spline_owner, spline_local, order, rounded, spline_blocks)
    got = lax.ppermute(send, "panel", [(i, i + 1) for i in range(0, panels, 2)])
    steps = panels // 4
    quarter = (4, struct_rows, width)
    keep, *sends = pl.pallas_call(
        split_kernel,
        out_shape=tuple(
            jax.ShapeDtypeStruct(quarter, f32 if step == 0 else bf16) for step in range(steps)
        ),
        in_specs=[VMEM, VMEM],
        out_specs=(VMEM,) * steps,
        compiler_params=params,
        cost_estimate=cost(10**6, 2**20),
        name="pair_sum",
    )(keep, got)
    got = [leader_swap(sends[step - 1], machs, panels, 0, 4 * step) for step in range(steps - 1, 0, -1)]
    two = jax.ShapeDtypeStruct((2, struct_rows, width), bf16)
    same, other = pl.pallas_call(
        column_kernel,
        out_shape=(two, two),
        in_specs=[VMEM] * steps,
        out_specs=(VMEM, VMEM),
        compiler_params=params,
        cost_estimate=cost(10**6, 2**20),
        name="column_sum",
    )(keep, *got)
    others = [leader_swap(other, machs, panels, turn, 2) for turn in range(machs - 1, -1, -1)]
    sames = [same] + [leader_swap(same, machs, panels, turn, 0) for turn in range(1, machs)]
    one = (struct_rows, width)
    even, odd = pl.pallas_call(
        functools.partial(round_kernel, machs),
        out_shape=(jax.ShapeDtypeStruct(one, bf16), jax.ShapeDtypeStruct(one, bf16)),
        in_specs=[VMEM] * (2 * machs),
        out_specs=(VMEM, VMEM),
        compiler_params=params,
        cost_estimate=cost(10**6, 2**20),
        name="mach_sum",
    )(*sames, *others[::-1])
    even = lax.ppermute(even, "panel", [(i + 1, i) for i in range(0, panels, 2)])
    struct_adjoint = pl.pallas_call(
        functools.partial(inverse_kernel, rhs),
        out_shape=jax.ShapeDtypeStruct((struct_rows, width), f32),
        in_specs=[VMEM] * 3,
        out_specs=VMEM,
        compiler_params=params,
        cost_estimate=cost(10**9, 2**20),
        name="struct_solve",
    )(odd, even, struct_inverse)
    return (
        loads.reshape(1, block_count, rhs, width),
        struct_adjoint.reshape(struct_count, rhs, width),
    )


def solution(mesh):
    in_specs = (
        P("mach", "panel", None, None),
        P("mach", "panel", None, None, None),
        P("panel", None),
        P("mach", None),
        P("panel", None, None, None),
        P("panel", None),
        P("panel", None),
        P("panel", None, None),
    )
    out_specs = (P("mach", "panel", None, None), P("panel", None, None))
    return jax.shard_map(
        on_device, mesh=mesh, in_specs=in_specs, out_specs=out_specs, check_vma=False
    )
```

```python
import functools

import jax
import jax.numpy as jnp
from jax import lax
from jax.experimental import pallas as pl
from jax.experimental.pallas import tpu as pltpu
from jax.sharding import PartitionSpec as P

SMEM = pl.BlockSpec(memory_space=pltpu.SMEM)
VMEM = pl.BlockSpec(memory_space=pltpu.VMEM)
PACK = 16
TILE = 8


def spread_kernel(machs, rhs, block_count, expand_ref, order_ref):
    shape = expand_ref.shape
    expand_ref[...] = (
        lax.broadcasted_iota(jnp.int32, shape, 0) // rhs == lax.broadcasted_iota(jnp.int32, shape, 1)
    ).astype(jnp.bfloat16)
    shape = order_ref.shape
    row = lax.broadcasted_iota(jnp.int32, shape, 0)
    source = (
        (row // TILE) % machs * (block_count * rhs) + row // (TILE * machs) * rhs + row % rhs
    )
    order_ref[...] = (lax.broadcasted_iota(jnp.int32, shape, 1) == source).astype(jnp.bfloat16)


def pick_kernel(
    panels, rhs, expand_ref, pattern_ref, trim_ref, own_ref, hot_ref, gate_ref, held_ref
):
    block_count, entries = pattern_ref.shape
    rows = own_ref.shape[0]
    here = lax.axis_index("panel")
    shape = (rows, hot_ref.shape[1])
    offset = lax.broadcasted_iota(jnp.int32, shape, 1) - (
        lax.broadcasted_iota(jnp.int32, shape, 0) % rhs
    )
    block = pattern_ref[...]
    apart = (block // block_count) ^ here
    slot = jnp.where(
        apart == 0, 0, jnp.where(apart == panels // 2, 3, jnp.where(apart == 1, 1, 2))
    )
    first = (slot * block_count + block % block_count) * rhs
    first = jnp.dot(
        expand_ref[...],
        first.astype(jnp.float32).astype(jnp.bfloat16),
        preferred_element_type=jnp.float32,
    ).astype(jnp.int32)
    for k in range(entries):
        hot_ref[k * rows : (k + 1) * rows] = (offset == first[:, k : k + 1]).astype(jnp.bfloat16)
    shape = (gate_ref.shape[0], rhs)
    mine = lax.broadcasted_iota(jnp.int32, shape, 0) % rhs == lax.broadcasted_iota(
        jnp.int32, shape, 1
    )
    gate = jnp.sum(jnp.where(mine, trim_ref[...], 0).astype(jnp.float32), axis=1, keepdims=True)
    gate_ref[...] = jnp.broadcast_to(gate, gate_ref.shape)
    held_ref[...] = own_ref[...]


def grouped_product(rhs, left, blocks_of, group):
    per_group = PACK // rhs
    every = jnp.concatenate([blocks_of(group * per_group + j) for j in range(per_group)], axis=1)
    product = jnp.dot(left, every, preferred_element_type=jnp.float32)
    width = product.shape[1] // per_group
    row = lax.broadcasted_iota(jnp.int32, (PACK, width), 0)
    out = product[:, :width]
    for j in range(1, per_group):
        out = jnp.where(row // rhs == j, product[:, j * width : (j + 1) * width], out)
    return out


def near_kernel(
    rhs, hot_ref, gate_ref, own_ref, pair_ref, cross_ref, mirror_ref, near_ref,
    loads_ref, rounded_ref,
):
    rows, width = own_ref.shape
    entries = hot_ref.shape[0] // rows
    pool = jnp.concatenate(
        [own_ref[...], pair_ref[...], cross_ref[...], mirror_ref[...]], axis=0
    )
    picked = jnp.dot(hot_ref[...], pool, preferred_element_type=jnp.float32)
    picked = picked.astype(jnp.bfloat16)
    for g in range(rows // PACK):
        left = jnp.concatenate(
            [picked[k * rows + g * PACK : k * rows + (g + 1) * PACK] for k in range(entries)],
            axis=1,
        )
        loads = gate_ref[...] * grouped_product(
            rhs, left, lambda i: near_ref[i].reshape(entries * width, width), g
        )
        loads_ref[g * PACK : (g + 1) * PACK] = loads
        rounded_ref[g * PACK : (g + 1) * PACK] = loads.astype(jnp.bfloat16)


def spline_kernel(machs, rhs, struct_count, owner_ref, local_ref, order_ref, *refs):
    rounded_refs, spline_ref, keep_ref, send_ref, acc = refs[:machs], *refs[machs:]
    block_count, splines = owner_ref.shape
    rows, width = rounded_refs[0].shape
    here = lax.axis_index("panel")
    acc[...] = jnp.zeros(acc.shape, jnp.float32)
    every = jnp.concatenate([ref[...] for ref in rounded_refs], axis=0)
    left = jnp.dot(order_ref[...], every, preferred_element_type=jnp.float32)
    left = left.astype(jnp.bfloat16)
    part = lax.broadcasted_iota(jnp.int32, (TILE, width), 0) // rhs
    per_tile = TILE // rhs
    owner_tiles = struct_count // per_tile
    height = machs * TILE
    blank = jnp.zeros((height, width), jnp.bfloat16)
    for pair in range(0, block_count, 2):
        mine = left[pair * height : (pair + 2) * height]
        mine = jnp.concatenate(
            [
                jnp.concatenate([mine[:height], blank], axis=1),
                jnp.concatenate([blank, mine[height:]], axis=1),
            ],
            axis=0,
        )
        blocks = jnp.concatenate(
            [
                jnp.concatenate([spline_ref[i, s] for s in range(splines)], axis=1)
                for i in (pair, pair + 1)
            ],
            axis=0,
        )
        product = jnp.dot(mine, blocks, preferred_element_type=jnp.float32)
        for i in (pair, pair + 1):
            total = product[(i - pair) * height : (i - pair) * height + TILE]
            for m in range(1, machs):
                start = (i - pair) * height + m * TILE
                total = total + product[start : start + TILE]
            places, sums = [], []
            for s in range(splines):
                apart = owner_ref[i, s] ^ here
                local = local_ref[i, s]
                place = (apart % 2, owner_ref[i, s] // 2 * owner_tiles + local // per_tile)
                added = jnp.where(
                    part == local % per_tile, total[:, s * width : (s + 1) * width], 0.0
                )
                places.append(place)
                sums.append(acc[place] + added)
            for place, value in zip(places, sums):
                acc[place] = value
    keep_ref[...] = acc[0].reshape(keep_ref.shape)
    send_ref[...] = acc[1].reshape(send_ref.shape).astype(send_ref.dtype)


def sum_kernel(held_ref, got_ref, out_ref):
    for place in range(held_ref.shape[0]):
        total = held_ref[place] + got_ref[place].astype(jnp.float32)
        out_ref[place] = total.astype(out_ref.dtype)


def inverse_kernel(rhs, got_ref, inverse_ref, out_ref):
    total = got_ref[0].astype(jnp.float32)
    for source in range(1, got_ref.shape[0]):
        total = total + got_ref[source].astype(jnp.float32)
    rounded = total.astype(jnp.bfloat16)
    for g in range(total.shape[0] // PACK):
        out_ref[g * PACK : (g + 1) * PACK] = grouped_product(
            rhs, rounded[g * PACK : (g + 1) * PACK], lambda t: inverse_ref[t], g
        )


def swap(value, panels, apart):
    return lax.ppermute(value, "panel", [(i, i ^ apart) for i in range(panels)])


def cost(flops, size):
    return pl.CostEstimate(flops=flops, bytes_accessed=size, transcendentals=0)


def on_device(
    adjoint, near_blocks, pattern, trim_mask, spline_blocks, spline_owner, spline_local,
    struct_inverse,
):
    _, block_count, rhs, width = adjoint.shape
    entries = pattern.shape[1]
    panels, machs = lax.axis_size("panel"), lax.axis_size("mach")
    struct_count = struct_inverse.shape[0]
    rows, struct_rows = block_count * rhs, struct_count * rhs
    params = pltpu.CompilerParams(vmem_limit_bytes=16 * 1024 * 1024)
    f32, bf16 = jnp.float32, jnp.bfloat16
    own = adjoint.reshape(rows, width)
    mirror = swap(own, panels, panels // 2)
    cross = lax.ppermute(
        own, "panel", [(i, (i - 1 + 2 * (i % 2)) % panels) for i in range(panels)]
    )
    pair = swap(own, panels, 1)
    expand, order = pl.pallas_call(
        functools.partial(spread_kernel, machs, rhs, block_count),
        out_shape=(
            jax.ShapeDtypeStruct((rows, block_count), bf16),
            jax.ShapeDtypeStruct((block_count * machs * TILE, machs * rows), bf16),
        ),
        out_specs=(VMEM, VMEM),
        compiler_params=params,
        cost_estimate=cost(4 * 10**9, 16 * 2**20),
        name="row_order",
    )()
    hot, gate, held = pl.pallas_call(
        functools.partial(pick_kernel, panels, rhs),
        out_shape=(
            jax.ShapeDtypeStruct((entries * rows, 4 * rows), bf16),
            jax.ShapeDtypeStruct((PACK, width), f32),
            jax.ShapeDtypeStruct((rows, width), bf16),
        ),
        in_specs=[VMEM] * 4,
        out_specs=(VMEM, VMEM, VMEM),
        compiler_params=params,
        cost_estimate=cost(10**6, 2**17),
        name="pick_rows",
    )(expand, pattern, trim_mask, own)
    loads, rounded = pl.pallas_call(
        functools.partial(near_kernel, rhs),
        out_shape=(
            jax.ShapeDtypeStruct((rows, width), f32),
            jax.ShapeDtypeStruct((rows, width), bf16),
        ),
        in_specs=[VMEM] * 7,
        out_specs=(VMEM, VMEM),
        compiler_params=params,
        cost_estimate=cost(2 * 10**9, 4 * 2**20),
        name="near_field",
    )(hot, gate, held, pair, cross, mirror, near_blocks[0])
    every = [rounded]
    for step in range(1, machs):
        every.append(
            lax.ppermute(rounded, "mach", [(i, (i + step) % machs) for i in range(machs)])
        )
    half = (panels // 2, struct_rows, width)
    keep, send = pl.pallas_call(
        functools.partial(spline_kernel, machs, rhs, struct_count),
        out_shape=(jax.ShapeDtypeStruct(half, f32), jax.ShapeDtypeStruct(half, bf16)),
        in_specs=[SMEM, SMEM] + [VMEM] * (machs + 2),
        out_specs=(VMEM, VMEM),
        scratch_shapes=[pltpu.VMEM((2, panels // 2 * struct_rows // TILE, TILE, width), f32)],
        compiler_params=params,
        cost_estimate=cost(2 * 10**9, 4 * 2**20),
        name="spline_loads",
    )(spline_owner, spline_local, order, *every, spline_blocks)
    got = swap(send, panels, 1)
    send = pl.pallas_call(
        sum_kernel,
        out_shape=jax.ShapeDtypeStruct(half, bf16),
        in_specs=[VMEM, VMEM],
        out_specs=VMEM,
        compiler_params=params,
        cost_estimate=cost(10**6, 2**20),
        name="pair_sum",
    )(keep, got)
    got = lax.all_to_all(
        send, "panel", split_axis=0, concat_axis=0, tiled=True,
        axis_index_groups=[list(range(core, panels, 2)) for core in range(2)],
    )
    struct_adjoint = pl.pallas_call(
        functools.partial(inverse_kernel, rhs),
        out_shape=jax.ShapeDtypeStruct((struct_rows, width), f32),
        in_specs=[VMEM] * 2,
        out_specs=VMEM,
        compiler_params=params,
        cost_estimate=cost(10**9, 2**20),
        name="struct_solve",
    )(got, struct_inverse)
    return (
        loads.reshape(1, block_count, rhs, width),
        struct_adjoint.reshape(struct_count, rhs, width),
    )


def solution(mesh):
    in_specs = (
        P("mach", "panel", None, None),
        P("mach", "panel", None, None, None),
        P("panel", None),
        P("mach", None),
        P("panel", None, None, None),
        P("panel", None),
        P("panel", None),
        P("panel", None, None),
    )
    out_specs = (P("mach", "panel", None, None), P("panel", None, None))
    return jax.shard_map(
        on_device, mesh=mesh, in_specs=in_specs, out_specs=out_specs, check_vma=False
    )
```

```python
import functools

import jax
import jax.numpy as jnp
from jax import lax
from jax.experimental import pallas as pl
from jax.experimental.pallas import tpu as pltpu
from jax.sharding import PartitionSpec as P

SMEM = pl.BlockSpec(memory_space=pltpu.SMEM)
VMEM = pl.BlockSpec(memory_space=pltpu.VMEM)
PACK = 16
TILE = 8


def spread_kernel(rhs, expand_ref, order_ref):
    shape = expand_ref.shape
    expand_ref[...] = (
        lax.broadcasted_iota(jnp.int32, shape, 0) // rhs == lax.broadcasted_iota(jnp.int32, shape, 1)
    ).astype(jnp.bfloat16)
    shape = order_ref.shape
    row = lax.broadcasted_iota(jnp.int32, shape, 0)
    source = row // TILE * rhs + row % rhs
    order_ref[...] = (lax.broadcasted_iota(jnp.int32, shape, 1) == source).astype(jnp.bfloat16)


def pick_kernel(
    panels, rhs, expand_ref, pattern_ref, trim_ref, own_ref, hot_ref, gate_ref, held_ref
):
    block_count, entries = pattern_ref.shape
    rows = own_ref.shape[0]
    here = lax.axis_index("panel")
    shape = (rows, hot_ref.shape[1])
    offset = lax.broadcasted_iota(jnp.int32, shape, 1) - (
        lax.broadcasted_iota(jnp.int32, shape, 0) % rhs
    )
    block = pattern_ref[...]
    apart = (block // block_count) ^ here
    slot = jnp.where(
        apart == 0, 0, jnp.where(apart == panels // 2, 3, jnp.where(apart == 1, 1, 2))
    )
    first = (slot * block_count + block % block_count) * rhs
    first = jnp.dot(
        expand_ref[...],
        first.astype(jnp.float32).astype(jnp.bfloat16),
        preferred_element_type=jnp.float32,
    ).astype(jnp.int32)
    for k in range(entries):
        hot_ref[k * rows : (k + 1) * rows] = (offset == first[:, k : k + 1]).astype(jnp.bfloat16)
    shape = (gate_ref.shape[0], rhs)
    mine = lax.broadcasted_iota(jnp.int32, shape, 0) % rhs == lax.broadcasted_iota(
        jnp.int32, shape, 1
    )
    gate = jnp.sum(jnp.where(mine, trim_ref[...], 0).astype(jnp.float32), axis=1, keepdims=True)
    gate_ref[...] = jnp.broadcast_to(gate, gate_ref.shape)
    held_ref[...] = own_ref[...]


def grouped_product(rhs, left, blocks_of, group):
    per_group = PACK // rhs
    every = jnp.concatenate([blocks_of(group * per_group + j) for j in range(per_group)], axis=1)
    product = jnp.dot(left, every, preferred_element_type=jnp.float32)
    width = product.shape[1] // per_group
    row = lax.broadcasted_iota(jnp.int32, (PACK, width), 0)
    out = product[:, :width]
    for j in range(1, per_group):
        out = jnp.where(row // rhs == j, product[:, j * width : (j + 1) * width], out)
    return out


def near_kernel(
    rhs, hot_ref, gate_ref, own_ref, pair_ref, cross_ref, mirror_ref, near_ref,
    loads_ref, rounded_ref,
):
    rows, width = own_ref.shape
    entries = hot_ref.shape[0] // rows
    pool = jnp.concatenate(
        [own_ref[...], pair_ref[...], cross_ref[...], mirror_ref[...]], axis=0
    )
    picked = jnp.dot(hot_ref[...], pool, preferred_element_type=jnp.float32)
    picked = picked.astype(jnp.bfloat16)
    for g in range(rows // PACK):
        left = jnp.concatenate(
            [picked[k * rows + g * PACK : k * rows + (g + 1) * PACK] for k in range(entries)],
            axis=1,
        )
        loads = gate_ref[...] * grouped_product(
            rhs, left, lambda i: near_ref[i].reshape(entries * width, width), g
        )
        loads_ref[g * PACK : (g + 1) * PACK] = loads
        rounded_ref[g * PACK : (g + 1) * PACK] = loads.astype(jnp.bfloat16)


def parity(index):
    for shift in (16, 8, 4, 2, 1):
        index = index ^ (index >> shift)
    return index & 1


def spline_kernel(
    rhs, struct_count, owner_ref, local_ref, order_ref, rounded_ref, spline_ref,
    keep_ref, send_ref, acc,
):
    block_count, splines = owner_ref.shape
    width = rounded_ref.shape[1]
    mine_class = parity(lax.axis_index("panel"))
    acc[...] = jnp.zeros(acc.shape, jnp.float32)
    left = jnp.dot(order_ref[...], rounded_ref[...], preferred_element_type=jnp.float32)
    left = left.astype(jnp.bfloat16)
    part = lax.broadcasted_iota(jnp.int32, (TILE, width), 0) // rhs
    per_tile = TILE // rhs
    owner_tiles = struct_count // per_tile
    height = TILE
    blank = jnp.zeros((height, width), jnp.bfloat16)
    for pair in range(0, block_count, 2):
        mine = left[pair * height : (pair + 2) * height]
        mine = jnp.concatenate(
            [
                jnp.concatenate([mine[:height], blank], axis=1),
                jnp.concatenate([blank, mine[height:]], axis=1),
            ],
            axis=0,
        )
        blocks = jnp.concatenate(
            [
                jnp.concatenate([spline_ref[i, s] for s in range(splines)], axis=1)
                for i in (pair, pair + 1)
            ],
            axis=0,
        )
        product = jnp.dot(mine, blocks, preferred_element_type=jnp.float32)
        for i in (pair, pair + 1):
            total = product[(i - pair) * height : (i - pair + 1) * height]
            places, sums = [], []
            for s in range(splines):
                owner, local = owner_ref[i, s], local_ref[i, s]
                place = (parity(owner) ^ mine_class, owner // 2 * owner_tiles + local // per_tile)
                added = jnp.where(
                    part == local % per_tile, total[:, s * width : (s + 1) * width], 0.0
                )
                places.append(place)
                sums.append(acc[place] + added)
            for place, value in zip(places, sums):
                acc[place] = value
    keep_ref[...] = acc[0].reshape(keep_ref.shape)
    send_ref[...] = acc[1].reshape(send_ref.shape).astype(send_ref.dtype)


def sum_kernel(held_ref, got_ref, out_ref):
    for place in range(held_ref.shape[0]):
        total = held_ref[place] + got_ref[place].astype(jnp.float32)
        for copy in range(out_ref.shape[0]):
            out_ref[copy, place] = total.astype(out_ref.dtype)


def inverse_kernel(rhs, got_ref, inverse_ref, out_ref):
    sources = [got_ref[index].astype(jnp.float32) for index in range(got_ref.shape[0])]
    while len(sources) > 1:
        sources = [a + b for a, b in zip(sources[::2], sources[1::2])] + sources[len(sources) & ~1 :]
    total = sources[0]
    rounded = total.astype(jnp.bfloat16)
    for g in range(total.shape[0] // PACK):
        out_ref[g * PACK : (g + 1) * PACK] = grouped_product(
            rhs, rounded[g * PACK : (g + 1) * PACK], lambda t: inverse_ref[t], g
        )


def swap(value, panels, apart):
    return lax.ppermute(value, "panel", [(i, i ^ apart) for i in range(panels)])


def cost(flops, size):
    return pl.CostEstimate(flops=flops, bytes_accessed=size, transcendentals=0)


def on_device(
    adjoint, near_blocks, pattern, trim_mask, spline_blocks, spline_owner, spline_local,
    struct_inverse,
):
    _, block_count, rhs, width = adjoint.shape
    entries = pattern.shape[1]
    panels, machs = lax.axis_size("panel"), lax.axis_size("mach")
    struct_count = struct_inverse.shape[0]
    rows, struct_rows = block_count * rhs, struct_count * rhs
    params = pltpu.CompilerParams(vmem_limit_bytes=16 * 1024 * 1024)
    f32, bf16 = jnp.float32, jnp.bfloat16
    own = adjoint.reshape(rows, width)
    mirror = swap(own, panels, panels // 2)
    beside = {0: 0, panels - 1: panels - 1}
    cross = lax.ppermute(
        own, ("mach", "panel"),
        [
            (
                mach * panels + i,
                (mach ^ (i in beside)) * panels + beside.get(i, i - 1 + 2 * (i % 2)),
            )
            for mach in range(machs)
            for i in range(panels)
        ],
    )
    pair = swap(own, panels, 1)
    expand, order = pl.pallas_call(
        functools.partial(spread_kernel, rhs),
        out_shape=(
            jax.ShapeDtypeStruct((rows, block_count), bf16),
            jax.ShapeDtypeStruct((block_count * TILE, rows), bf16),
        ),
        out_specs=(VMEM, VMEM),
        compiler_params=params,
        cost_estimate=cost(4 * 10**9, 16 * 2**20),
        name="row_order",
    )()
    hot, gate, held = pl.pallas_call(
        functools.partial(pick_kernel, panels, rhs),
        out_shape=(
            jax.ShapeDtypeStruct((entries * rows, 4 * rows), bf16),
            jax.ShapeDtypeStruct((PACK, width), f32),
            jax.ShapeDtypeStruct((rows, width), bf16),
        ),
        in_specs=[VMEM] * 4,
        out_specs=(VMEM, VMEM, VMEM),
        compiler_params=params,
        cost_estimate=cost(10**6, 2**17),
        name="pick_rows",
    )(expand, pattern, trim_mask, own)
    loads, rounded = pl.pallas_call(
        functools.partial(near_kernel, rhs),
        out_shape=(
            jax.ShapeDtypeStruct((rows, width), f32),
            jax.ShapeDtypeStruct((rows, width), bf16),
        ),
        in_specs=[VMEM] * 7,
        out_specs=(VMEM, VMEM),
        compiler_params=params,
        cost_estimate=cost(2 * 10**9, 4 * 2**20),
        name="near_field",
    )(hot, gate, held, pair, cross, mirror, near_blocks[0])
    half = (panels // 2, struct_rows, width)
    keep, send = pl.pallas_call(
        functools.partial(spline_kernel, rhs, struct_count),
        out_shape=(jax.ShapeDtypeStruct(half, f32), jax.ShapeDtypeStruct(half, bf16)),
        in_specs=[SMEM, SMEM, VMEM, VMEM, VMEM],
        out_specs=(VMEM, VMEM),
        scratch_shapes=[pltpu.VMEM((2, panels // 2 * struct_rows // TILE, TILE, width), f32)],
        compiler_params=params,
        cost_estimate=cost(2 * 10**9, 4 * 2**20),
        name="spline_loads",
    )(spline_owner, spline_local, order, rounded, spline_blocks)
    got = swap(send, panels, 1)
    send = pl.pallas_call(
        sum_kernel,
        out_shape=jax.ShapeDtypeStruct((machs, *half), bf16),
        in_specs=[VMEM, VMEM],
        out_specs=VMEM,
        compiler_params=params,
        cost_estimate=cost(10**6, 2**20),
        name="pair_sum",
    )(keep, got)
    got = lax.all_to_all(
        send.reshape(machs * panels // 2, struct_rows, width), ("mach", "panel"),
        split_axis=0, concat_axis=0, tiled=True,
        axis_index_groups=[
            [
                mach * panels + 2 * chip + (parity(2 * chip) ^ which)
                for mach in range(machs)
                for chip in range(panels // 2)
            ]
            for which in range(2)
        ],
    )
    struct_adjoint = pl.pallas_call(
        functools.partial(inverse_kernel, rhs),
        out_shape=jax.ShapeDtypeStruct((struct_rows, width), f32),
        in_specs=[VMEM] * 2,
        out_specs=VMEM,
        compiler_params=params,
        cost_estimate=cost(10**9, 2**20),
        name="struct_solve",
    )(got, struct_inverse)
    return (
        loads.reshape(1, block_count, rhs, width),
        struct_adjoint.reshape(struct_count, rhs, width),
    )


def solution(mesh):
    in_specs = (
        P("mach", "panel", None, None),
        P("mach", "panel", None, None, None),
        P("panel", None),
        P("mach", None),
        P("panel", None, None, None),
        P("panel", None),
        P("panel", None),
        P("panel", None, None),
    )
    out_specs = (P("mach", "panel", None, None), P("panel", None, None))
    return jax.shard_map(
        on_device, mesh=mesh, in_specs=in_specs, out_specs=out_specs, check_vma=False
    )
```

```python
import functools

import jax
import jax.numpy as jnp
from jax import lax
from jax.experimental import pallas as pl
from jax.experimental.pallas import tpu as pltpu
from jax.sharding import PartitionSpec as P

SMEM = pl.BlockSpec(memory_space=pltpu.SMEM)
VMEM = pl.BlockSpec(memory_space=pltpu.VMEM)
PACK = 16
TILE = 8


def parity(index):
    for shift in (16, 8, 4, 2, 1):
        index = index ^ (index >> shift)
    return index & 1


def spread_kernel(rhs, expand_ref):
    shape = expand_ref.shape
    expand_ref[...] = (
        lax.broadcasted_iota(jnp.int32, shape, 0) // rhs == lax.broadcasted_iota(jnp.int32, shape, 1)
    ).astype(jnp.bfloat16)


def pick_kernel(
    panels, rhs, struct_count, expand_ref, pattern_ref, trim_ref, own_ref, owner_ref, local_ref,
    hot_ref, gate_ref, held_ref, code_ref,
):
    block_count, entries = pattern_ref.shape
    rows = own_ref.shape[0]
    here = lax.axis_index("panel")
    shape = (rows, hot_ref.shape[1])
    offset = lax.broadcasted_iota(jnp.int32, shape, 1) - (
        lax.broadcasted_iota(jnp.int32, shape, 0) % rhs
    )
    block = pattern_ref[...]
    apart = (block // block_count) ^ here
    slot = jnp.where(apart == 0, 0, jnp.where(apart == 1, 1, 2))
    first = (slot * block_count + block % block_count) * rhs
    first = jnp.dot(
        expand_ref[...],
        first.astype(jnp.float32).astype(jnp.bfloat16),
        preferred_element_type=jnp.float32,
    ).astype(jnp.int32)
    for k in range(2, entries):
        hot_ref[(k - 2) * rows : (k - 1) * rows] = (offset == first[:, k : k + 1]).astype(
            jnp.bfloat16
        )
    shape = (gate_ref.shape[0], rhs)
    mine = lax.broadcasted_iota(jnp.int32, shape, 0) % rhs == lax.broadcasted_iota(
        jnp.int32, shape, 1
    )
    gate = jnp.sum(jnp.where(mine, trim_ref[...], 0).astype(jnp.float32), axis=1, keepdims=True)
    gate_ref[...] = jnp.broadcast_to(gate, gate_ref.shape)
    held_ref[...] = own_ref[...]
    owner = owner_ref[...]
    code_ref[...] = (
        (parity(owner) ^ parity(here)) * (panels // 2) + owner // 2
    ) * struct_count + local_ref[...]


def grouped_product(rhs, left, blocks_of, group):
    per_group = PACK // rhs
    every = jnp.concatenate([blocks_of(group * per_group + j) for j in range(per_group)], axis=1)
    product = jnp.dot(left, every, preferred_element_type=jnp.float32)
    width = product.shape[1] // per_group
    row = lax.broadcasted_iota(jnp.int32, (PACK, width), 0)
    out = product[:, :width]
    for j in range(1, per_group):
        out = jnp.where(row // rhs == j, product[:, j * width : (j + 1) * width], out)
    return out


def near_kernel(rhs, hot_ref, own_ref, pair_ref, cross_ref, near_ref, part_ref):
    rows, width = own_ref.shape
    others = hot_ref.shape[0] // rows
    own = own_ref[...]
    pool = jnp.concatenate([own, pair_ref[...], cross_ref[...], own], axis=0)
    picked = jnp.dot(hot_ref[...], pool, preferred_element_type=jnp.float32)
    picked = picked.astype(jnp.bfloat16)
    for g in range(rows // PACK):
        left = [own[g * PACK : (g + 1) * PACK]] + [
            picked[k * rows + g * PACK : k * rows + (g + 1) * PACK] for k in range(others)
        ]
        part_ref[g * PACK : (g + 1) * PACK] = grouped_product(
            rhs,
            jnp.concatenate(left, axis=1),
            lambda i: jnp.concatenate(
                [near_ref[i, 0], near_ref[i, 2:].reshape(others * width, width)], axis=0
            ),
            g,
        )


def spline_kernel(
    rhs, code_ref, part_ref, mirror_ref, gate_ref, near_ref, spline_ref,
    loads_hbm, keep_ref, send_ref, loads_ref, acc, sem,
):
    block_count, splines = code_ref.shape
    rows, width = part_ref.shape
    for g in range(rows // PACK):
        group = slice(g * PACK, (g + 1) * PACK)
        far = grouped_product(rhs, mirror_ref[group], lambda i: near_ref[i, 1], g)
        loads_ref[group] = gate_ref[...] * (part_ref[group] + far)
    copy = pltpu.make_async_copy(loads_ref, loads_hbm, sem)
    copy.start()
    acc[...] = jnp.zeros(acc.shape, jnp.float32)
    upper = lax.broadcasted_iota(jnp.int32, (TILE, width), 0) // rhs
    blank = jnp.zeros((TILE, width), jnp.float32)
    for pair in range(0, block_count, 2):
        both = loads_ref[pair * rhs : (pair + 2) * rhs]
        turned = pltpu.roll(both, rhs, 0)
        mine = jnp.concatenate(
            [
                jnp.concatenate([jnp.where(upper == 0, both, turned), blank], axis=1),
                jnp.concatenate([blank, jnp.where(upper == 0, turned, both)], axis=1),
            ],
            axis=0,
        ).astype(jnp.bfloat16)
        blocks = jnp.concatenate(
            [
                jnp.concatenate([spline_ref[i, s] for s in range(splines)], axis=1)
                for i in (pair, pair + 1)
            ],
            axis=0,
        )
        product = jnp.dot(mine, blocks, preferred_element_type=jnp.float32)
        for i in (pair, pair + 1):
            total = product[(i - pair) * TILE : (i - pair + 1) * TILE]
            places, sums = [], []
            for s in range(splines):
                code = code_ref[i, s]
                place = code >> 1
                added = jnp.where(upper == (code & 1), total[:, s * width : (s + 1) * width], 0.0)
                places.append(place)
                sums.append(acc[place] + added)
            for place, value in zip(places, sums):
                acc[place] = value
    tiles = acc.shape[0] // 2
    keep_ref[...] = acc[:tiles].reshape(keep_ref.shape)
    send_ref[...] = acc[tiles:].reshape(send_ref.shape).astype(send_ref.dtype)
    copy.wait()


def sum_kernel(held_ref, got_ref, out_ref):
    for place in range(held_ref.shape[0]):
        total = held_ref[place] + got_ref[place].astype(jnp.float32)
        for copy in range(out_ref.shape[0]):
            out_ref[copy, place] = total.astype(out_ref.dtype)


def inverse_kernel(rhs, got_ref, inverse_ref, out_ref):
    sources = [got_ref[index].astype(jnp.float32) for index in range(got_ref.shape[0])]
    while len(sources) > 1:
        sources = [a + b for a, b in zip(sources[::2], sources[1::2])] + sources[len(sources) & ~1 :]
    total = sources[0]
    rounded = total.astype(jnp.bfloat16)
    for g in range(total.shape[0] // PACK):
        out_ref[g * PACK : (g + 1) * PACK] = grouped_product(
            rhs, rounded[g * PACK : (g + 1) * PACK], lambda t: inverse_ref[t], g
        )


def swap(value, panels, apart):
    return lax.ppermute(value, "panel", [(i, i ^ apart) for i in range(panels)])


def cost(flops, size):
    return pl.CostEstimate(flops=flops, bytes_accessed=size, transcendentals=0)


def on_device(
    adjoint, near_blocks, pattern, trim_mask, spline_blocks, spline_owner, spline_local,
    struct_inverse,
):
    _, block_count, rhs, width = adjoint.shape
    entries = pattern.shape[1]
    panels, machs = lax.axis_size("panel"), lax.axis_size("mach")
    struct_count = struct_inverse.shape[0]
    rows, struct_rows = block_count * rhs, struct_count * rhs
    params = pltpu.CompilerParams(vmem_limit_bytes=16 * 1024 * 1024)
    f32, bf16 = jnp.float32, jnp.bfloat16
    own = adjoint.reshape(rows, width)
    mirror = swap(own, panels, panels // 2)
    beside = {0: 0, panels - 1: panels - 1}
    cross = lax.ppermute(
        own, ("mach", "panel"),
        [
            (
                mach * panels + i,
                (mach ^ (i in beside)) * panels + beside.get(i, i - 1 + 2 * (i % 2)),
            )
            for mach in range(machs)
            for i in range(panels)
        ],
    )
    pair = swap(own, panels, 1)
    expand = pl.pallas_call(
        functools.partial(spread_kernel, rhs),
        out_shape=jax.ShapeDtypeStruct((rows, block_count), bf16),
        out_specs=VMEM,
        compiler_params=params,
        cost_estimate=cost(8 * 10**9, 32 * 2**20),
        name="row_order",
    )()
    hot, gate, held, code = pl.pallas_call(
        functools.partial(pick_kernel, panels, rhs, struct_count),
        out_shape=(
            jax.ShapeDtypeStruct(((entries - 2) * rows, 4 * rows), bf16),
            jax.ShapeDtypeStruct((PACK, width), f32),
            jax.ShapeDtypeStruct((rows, width), bf16),
            jax.ShapeDtypeStruct(spline_owner.shape, jnp.int32),
        ),
        in_specs=[VMEM] * 6,
        out_specs=(VMEM,) * 4,
        compiler_params=params,
        cost_estimate=cost(10**6, 2**17),
        name="pick_rows",
    )(expand, pattern, trim_mask, own, spline_owner, spline_local)
    part = pl.pallas_call(
        functools.partial(near_kernel, rhs),
        out_shape=jax.ShapeDtypeStruct((rows, width), f32),
        in_specs=[VMEM] * 5,
        out_specs=VMEM,
        compiler_params=params,
        cost_estimate=cost(10**6, 2**17),
        name="near_field",
    )(hot, held, pair, cross, near_blocks[0])
    half = (panels // 2, struct_rows, width)
    loads, keep, send = pl.pallas_call(
        functools.partial(spline_kernel, rhs),
        out_shape=(
            jax.ShapeDtypeStruct((rows, width), f32),
            jax.ShapeDtypeStruct(half, f32),
            jax.ShapeDtypeStruct(half, bf16),
        ),
        in_specs=[SMEM] + [VMEM] * 5,
        out_specs=(pl.BlockSpec(memory_space=pl.ANY), VMEM, VMEM),
        scratch_shapes=[
            pltpu.VMEM((rows, width), f32),
            pltpu.VMEM((panels * struct_rows // TILE, TILE, width), f32),
            pltpu.SemaphoreType.DMA,
        ],
        compiler_params=params,
        cost_estimate=cost(10**6, 2**17),
        name="spline_loads",
    )(code, part, mirror, gate, near_blocks[0], spline_blocks)
    got = swap(send, panels, 1)
    send = pl.pallas_call(
        sum_kernel,
        out_shape=jax.ShapeDtypeStruct((machs, *half), bf16),
        in_specs=[VMEM, VMEM],
        out_specs=VMEM,
        compiler_params=params,
        cost_estimate=cost(10**6, 2**20),
        name="pair_sum",
    )(keep, got)
    got = lax.all_to_all(
        send.reshape(machs * panels // 2, struct_rows, width), ("mach", "panel"),
        split_axis=0, concat_axis=0, tiled=True,
        axis_index_groups=[
            [
                mach * panels + 2 * chip + (parity(2 * chip) ^ which)
                for mach in range(machs)
                for chip in range(panels // 2)
            ]
            for which in range(2)
        ],
    )
    struct_adjoint = pl.pallas_call(
        functools.partial(inverse_kernel, rhs),
        out_shape=jax.ShapeDtypeStruct((struct_rows, width), f32),
        in_specs=[VMEM] * 2,
        out_specs=VMEM,
        compiler_params=params,
        cost_estimate=cost(10**9, 2**20),
        name="struct_solve",
    )(got, struct_inverse)
    return (
        loads.reshape(1, block_count, rhs, width),
        struct_adjoint.reshape(struct_count, rhs, width),
    )


def solution(mesh):
    in_specs = (
        P("mach", "panel", None, None),
        P("mach", "panel", None, None, None),
        P("panel", None),
        P("mach", None),
        P("panel", None, None, None),
        P("panel", None),
        P("panel", None),
        P("panel", None, None),
    )
    out_specs = (P("mach", "panel", None, None), P("panel", None, None))
    return jax.shard_map(
        on_device, mesh=mesh, in_specs=in_specs, out_specs=out_specs, check_vma=False
    )
```

```python
import functools

import jax
import jax.numpy as jnp
from jax import lax
from jax.experimental import pallas as pl
from jax.experimental.pallas import tpu as pltpu
from jax.sharding import PartitionSpec as P

SMEM = pl.BlockSpec(memory_space=pltpu.SMEM)
VMEM = pl.BlockSpec(memory_space=pltpu.VMEM)
PACK = 16
TILE = 8


def device_class(index):
    return (index ^ (index >> 1) ^ (index >> 2)) & 1


def spread_kernel(rhs, expand_ref):
    shape = expand_ref.shape
    expand_ref[...] = (
        lax.broadcasted_iota(jnp.int32, shape, 0) // rhs == lax.broadcasted_iota(jnp.int32, shape, 1)
    ).astype(jnp.bfloat16)


def pick_kernel(
    panels, rhs, struct_count, expand_ref, pattern_ref, trim_ref, own_ref, owner_ref, local_ref,
    hot_ref, gate_ref, held_ref, code_ref,
):
    block_count, entries = pattern_ref.shape
    rows = own_ref.shape[0]
    here = lax.axis_index("panel")
    shape = (rows, hot_ref.shape[1])
    offset = lax.broadcasted_iota(jnp.int32, shape, 1) - (
        lax.broadcasted_iota(jnp.int32, shape, 0) % rhs
    )
    block = pattern_ref[...]
    apart = (block // block_count) ^ here
    slot = jnp.where(apart == 0, 0, jnp.where(apart == 1, 1, 2))
    first = (slot * block_count + block % block_count) * rhs
    first = jnp.dot(
        expand_ref[...],
        first.astype(jnp.float32).astype(jnp.bfloat16),
        preferred_element_type=jnp.float32,
    ).astype(jnp.int32)
    for k in range(2, entries):
        hot_ref[(k - 2) * rows : (k - 1) * rows] = (offset == first[:, k : k + 1]).astype(
            jnp.bfloat16
        )
    shape = (gate_ref.shape[0], rhs)
    mine = lax.broadcasted_iota(jnp.int32, shape, 0) % rhs == lax.broadcasted_iota(
        jnp.int32, shape, 1
    )
    gate = jnp.sum(jnp.where(mine, trim_ref[...], 0).astype(jnp.float32), axis=1, keepdims=True)
    gate_ref[...] = jnp.broadcast_to(gate, gate_ref.shape)
    held_ref[...] = own_ref[...]
    owner = owner_ref[...]
    code_ref[...] = (
        (device_class(owner) ^ device_class(here)) * (panels // 2) + ((owner ^ here) >> 1)
    ) * struct_count + local_ref[...]


def grouped_product(rhs, left, blocks_of, group):
    per_group = PACK // rhs
    every = jnp.concatenate([blocks_of(group * per_group + j) for j in range(per_group)], axis=1)
    product = jnp.dot(left, every, preferred_element_type=jnp.float32)
    width = product.shape[1] // per_group
    row = lax.broadcasted_iota(jnp.int32, (PACK, width), 0)
    out = product[:, :width]
    for j in range(1, per_group):
        out = jnp.where(row // rhs == j, product[:, j * width : (j + 1) * width], out)
    return out


def near_kernel(rhs, hot_ref, own_ref, pair_ref, cross_ref, near_ref, part_ref):
    rows, width = own_ref.shape
    others = hot_ref.shape[0] // rows
    own = own_ref[...]
    pool = jnp.concatenate([own, pair_ref[...], cross_ref[...], own], axis=0)
    picked = jnp.dot(hot_ref[...], pool, preferred_element_type=jnp.float32)
    picked = picked.astype(jnp.bfloat16)
    for g in range(rows // PACK):
        left = [own[g * PACK : (g + 1) * PACK]] + [
            picked[k * rows + g * PACK : k * rows + (g + 1) * PACK] for k in range(others)
        ]
        part_ref[g * PACK : (g + 1) * PACK] = grouped_product(
            rhs,
            jnp.concatenate(left, axis=1),
            lambda i: jnp.concatenate(
                [near_ref[i, 0], near_ref[i, 2:].reshape(others * width, width)], axis=0
            ),
            g,
        )


def spline_kernel(
    rhs, code_vmem, part_ref, mirror_ref, gate_ref, near_ref, spline_ref,
    loads_ref, keep_ref, send_ref, code_ref, acc, sem,
):
    copy = pltpu.make_async_copy(code_vmem, code_ref, sem)
    copy.start()
    block_count, splines = code_ref.shape
    rows, width = part_ref.shape
    for g in range(rows // PACK):
        group = slice(g * PACK, (g + 1) * PACK)
        far = grouped_product(rhs, mirror_ref[group], lambda i: near_ref[i, 1], g)
        loads_ref[group] = gate_ref[...] * (part_ref[group] + far)
    acc[...] = jnp.zeros(acc.shape, jnp.float32)
    upper = lax.broadcasted_iota(jnp.int32, (TILE, width), 0) // rhs
    blank = jnp.zeros((TILE, width), jnp.float32)
    copy.wait()
    for pair in range(0, block_count, 2):
        both = loads_ref[pair * rhs : (pair + 2) * rhs]
        turned = pltpu.roll(both, rhs, 0)
        mine = jnp.concatenate(
            [
                jnp.concatenate([jnp.where(upper == 0, both, turned), blank], axis=1),
                jnp.concatenate([blank, jnp.where(upper == 0, turned, both)], axis=1),
            ],
            axis=0,
        ).astype(jnp.bfloat16)
        blocks = jnp.concatenate(
            [
                jnp.concatenate([spline_ref[i, s] for s in range(splines)], axis=1)
                for i in (pair, pair + 1)
            ],
            axis=0,
        )
        product = jnp.dot(mine, blocks, preferred_element_type=jnp.float32)
        for i in (pair, pair + 1):
            total = product[(i - pair) * TILE : (i - pair + 1) * TILE]
            places, sums = [], []
            for s in range(splines):
                code = code_ref[i, s]
                place = code >> 1
                added = jnp.where(upper == (code & 1), total[:, s * width : (s + 1) * width], 0.0)
                places.append(place)
                sums.append(acc[place] + added)
            for place, value in zip(places, sums):
                acc[place] = value
    tiles = acc.shape[0] // 2
    keep_ref[...] = acc[:tiles].reshape(keep_ref.shape)
    send_ref[...] = acc[tiles:].reshape(send_ref.shape).astype(send_ref.dtype)


def split_kernel(held_ref, got_ref, *out_refs):
    size = out_refs[0].shape[0]
    for step, out_ref in enumerate(out_refs):
        for place in range(size):
            total = held_ref[step * size + place] + got_ref[step * size + place].astype(jnp.float32)
            out_ref[place] = total.astype(out_ref.dtype)


def column_kernel(machs, held_ref, *refs):
    got_refs, out_refs = refs[: -2 * machs], refs[-2 * machs :]
    for place in range(2):
        total = held_ref[place]
        for got_ref in got_refs:
            total = total + got_ref[place].astype(jnp.float32)
        for out_ref in out_refs[place * machs : (place + 1) * machs]:
            out_ref[...] = total


def inverse_kernel(rhs, machs, loads_ref, *refs):
    other_refs, same_refs = refs[: 2 * machs : 2], refs[1 : 2 * machs : 2]
    inverse_ref, loads_hbm, out_ref, sem = refs[2 * machs :]
    copy = pltpu.make_async_copy(loads_ref, loads_hbm, sem)
    copy.start()
    parts = [same[...] + other[...] for same, other in zip(same_refs, other_refs)]
    rounded = sum(parts[1:], parts[0]).astype(jnp.bfloat16)
    for g in range(rounded.shape[0] // PACK):
        out_ref[g * PACK : (g + 1) * PACK] = grouped_product(
            rhs, rounded[g * PACK : (g + 1) * PACK], lambda t: inverse_ref[t], g
        )
    copy.wait()


def swap(value, panels, apart):
    return lax.ppermute(value, "panel", [(i, i ^ apart) for i in range(panels)])


def mach_swap(value, machs, panels, turn, apart):
    pairs = [
        (mach * panels + i, (mach + turn) % machs * panels + (i ^ apart))
        for mach in range(machs)
        for i in range(panels)
    ]
    return lax.ppermute(value, ("mach", "panel"), pairs)


def cost(flops, size):
    return pl.CostEstimate(flops=flops, bytes_accessed=size, transcendentals=0)


def on_device(
    adjoint, near_blocks, pattern, trim_mask, spline_blocks, spline_owner, spline_local,
    struct_inverse,
):
    _, block_count, rhs, width = adjoint.shape
    entries = pattern.shape[1]
    panels, machs = lax.axis_size("panel"), lax.axis_size("mach")
    struct_count = struct_inverse.shape[0]
    rows, struct_rows = block_count * rhs, struct_count * rhs
    params = pltpu.CompilerParams(vmem_limit_bytes=16 * 1024 * 1024)
    f32, bf16 = jnp.float32, jnp.bfloat16
    own = adjoint.reshape(rows, width)
    beside = {0: 0, panels - 1: panels - 1}
    cross = lax.ppermute(
        own, ("mach", "panel"),
        [
            (
                mach * panels + i,
                (mach ^ (i in beside)) * panels + beside.get(i, i - 1 + 2 * (i % 2)),
            )
            for mach in range(machs)
            for i in range(panels)
        ],
    )
    mirror = swap(own, panels, panels // 2)
    pair = swap(own, panels, 1)
    expand = pl.pallas_call(
        functools.partial(spread_kernel, rhs),
        out_shape=jax.ShapeDtypeStruct((rows, block_count), bf16),
        out_specs=VMEM,
        compiler_params=params,
        cost_estimate=cost(8 * 10**9, 32 * 2**20),
        name="row_order",
    )()
    hot, gate, held, code = pl.pallas_call(
        functools.partial(pick_kernel, panels, rhs, struct_count),
        out_shape=(
            jax.ShapeDtypeStruct(((entries - 2) * rows, 4 * rows), bf16),
            jax.ShapeDtypeStruct((PACK, width), f32),
            jax.ShapeDtypeStruct((rows, width), bf16),
            jax.ShapeDtypeStruct(spline_owner.shape, jnp.int32),
        ),
        in_specs=[VMEM] * 6,
        out_specs=(VMEM,) * 4,
        compiler_params=params,
        cost_estimate=cost(10**6, 2**17),
        name="pick_rows",
    )(expand, pattern, trim_mask, own, spline_owner, spline_local)
    part = pl.pallas_call(
        functools.partial(near_kernel, rhs),
        out_shape=jax.ShapeDtypeStruct((rows, width), f32),
        in_specs=[VMEM] * 5,
        out_specs=VMEM,
        compiler_params=params,
        cost_estimate=cost(10**6, 2**17),
        name="near_field",
    )(hot, held, pair, cross, near_blocks[0])
    half = (panels // 2, struct_rows, width)
    loads, keep, send = pl.pallas_call(
        functools.partial(spline_kernel, rhs),
        out_shape=(
            jax.ShapeDtypeStruct((rows, width), f32),
            jax.ShapeDtypeStruct(half, f32),
            jax.ShapeDtypeStruct(half, bf16),
        ),
        in_specs=[VMEM] * 6,
        out_specs=(VMEM,) * 3,
        scratch_shapes=[
            pltpu.SMEM(spline_owner.shape, jnp.int32),
            pltpu.VMEM((panels * struct_rows // TILE, TILE, width), f32),
            pltpu.SemaphoreType.DMA,
        ],
        compiler_params=params,
        cost_estimate=cost(10**6, 2**17),
        name="spline_loads",
    )(code, part, mirror, gate, near_blocks[0], spline_blocks)
    got = swap(send, panels, 1)
    steps = panels // 4
    two = (2, struct_rows, width)
    keep, *sends = pl.pallas_call(
        split_kernel,
        out_shape=tuple(
            jax.ShapeDtypeStruct(two, f32 if step == 0 else bf16) for step in range(steps)
        ),
        in_specs=[VMEM, VMEM],
        out_specs=(VMEM,) * steps,
        compiler_params=params,
        cost_estimate=cost(10**6, 2**17),
        name="pair_sum",
    )(keep, got)
    got = [
        swap(sends[step - 1], panels, 4 * step + step % 2) for step in range(steps - 1, 0, -1)
    ]
    one = jax.ShapeDtypeStruct((struct_rows, width), f32)
    columns = pl.pallas_call(
        functools.partial(column_kernel, machs),
        out_shape=(one,) * (2 * machs),
        in_specs=[VMEM] * steps,
        out_specs=(VMEM,) * (2 * machs),
        compiler_params=params,
        cost_estimate=cost(10**6, 2**17),
        name="column_sum",
    )(keep, *got)
    sames = [
        mach_swap(columns[turn], machs, panels, turn, 0) if turn else columns[0]
        for turn in range(machs)
    ]
    others = [mach_swap(columns[machs + turn], machs, panels, turn, 3) for turn in range(machs)]
    loads, struct_adjoint = pl.pallas_call(
        functools.partial(inverse_kernel, rhs, machs),
        out_shape=(jax.ShapeDtypeStruct((rows, width), f32), one),
        in_specs=[VMEM] * (2 * machs + 2),
        out_specs=(pl.BlockSpec(memory_space=pl.ANY), VMEM),
        scratch_shapes=[pltpu.SemaphoreType.DMA],
        compiler_params=params,
        cost_estimate=cost(10**6, 2**17),
        name="struct_solve",
    )(
        loads,
        *(value for turn in range(machs - 1, -1, -1) for value in (others[turn], sames[turn])),
        struct_inverse,
    )
    return (
        loads.reshape(1, block_count, rhs, width),
        struct_adjoint.reshape(struct_count, rhs, width),
    )


def solution(mesh):
    in_specs = (
        P("mach", "panel", None, None),
        P("mach", "panel", None, None, None),
        P("panel", None),
        P("mach", None),
        P("panel", None, None, None),
        P("panel", None),
        P("panel", None),
        P("panel", None, None),
    )
    out_specs = (P("mach", "panel", None, None), P("panel", None, None))
    return jax.shard_map(
        on_device, mesh=mesh, in_specs=in_specs, out_specs=out_specs, check_vma=False
    )
```

```python
import functools

import jax
import jax.numpy as jnp
from jax import lax
from jax.experimental import pallas as pl
from jax.experimental.pallas import tpu as pltpu
from jax.sharding import PartitionSpec as P

SMEM = pl.BlockSpec(memory_space=pltpu.SMEM)
VMEM = pl.BlockSpec(memory_space=pltpu.VMEM)
PACK = 16
TILE = 8


def device_class(index):
    return (index ^ (index >> 1) ^ (index >> 2)) & 1


def spread_kernel(rhs, expand_ref):
    shape = expand_ref.shape
    expand_ref[...] = (
        lax.broadcasted_iota(jnp.int32, shape, 0) // rhs == lax.broadcasted_iota(jnp.int32, shape, 1)
    ).astype(jnp.bfloat16)


def pick_kernel(
    panels, rhs, struct_count, expand_ref, pattern_ref, trim_ref, own_ref, owner_ref, local_ref,
    hot_ref, gate_ref, held_ref, code_ref,
):
    block_count, entries = pattern_ref.shape
    rows = own_ref.shape[0]
    here = lax.axis_index("panel")
    shape = (rows, hot_ref.shape[1])
    offset = lax.broadcasted_iota(jnp.int32, shape, 1) - (
        lax.broadcasted_iota(jnp.int32, shape, 0) % rhs
    )
    block = pattern_ref[...]
    apart = (block // block_count) ^ here
    slot = jnp.where(apart == 0, 0, jnp.where(apart == 1, 1, 2))
    first = (slot * block_count + block % block_count) * rhs
    first = jnp.dot(
        expand_ref[...],
        first.astype(jnp.float32).astype(jnp.bfloat16),
        preferred_element_type=jnp.float32,
    ).astype(jnp.int32)
    for k in range(2, entries):
        hot_ref[(k - 2) * rows : (k - 1) * rows] = (offset == first[:, k : k + 1]).astype(
            jnp.bfloat16
        )
    shape = (gate_ref.shape[0], rhs)
    mine = lax.broadcasted_iota(jnp.int32, shape, 0) % rhs == lax.broadcasted_iota(
        jnp.int32, shape, 1
    )
    gate = jnp.sum(jnp.where(mine, trim_ref[...], 0).astype(jnp.float32), axis=1, keepdims=True)
    gate_ref[...] = jnp.broadcast_to(gate, gate_ref.shape)
    held_ref[...] = own_ref[...]
    owner = owner_ref[...]
    code_ref[...] = (
        (device_class(owner) ^ device_class(here)) * (panels // 2) + ((owner ^ here) >> 1)
    ) * struct_count + local_ref[...]


def grouped_product(rhs, left, blocks_of, group):
    per_group = PACK // rhs
    every = jnp.concatenate([blocks_of(group * per_group + j) for j in range(per_group)], axis=1)
    product = jnp.dot(left, every, preferred_element_type=jnp.float32)
    width = product.shape[1] // per_group
    row = lax.broadcasted_iota(jnp.int32, (PACK, width), 0)
    out = product[:, :width]
    for j in range(1, per_group):
        out = jnp.where(row // rhs == j, product[:, j * width : (j + 1) * width], out)
    return out


def near_kernel(rhs, hot_ref, own_ref, pair_ref, cross_ref, near_ref, part_ref):
    rows, width = own_ref.shape
    others = hot_ref.shape[0] // rows
    own = own_ref[...]
    pool = jnp.concatenate([own, pair_ref[...], cross_ref[...], own], axis=0)
    picked = jnp.dot(hot_ref[...], pool, preferred_element_type=jnp.float32)
    picked = picked.astype(jnp.bfloat16)
    for g in range(rows // PACK):
        left = [own[g * PACK : (g + 1) * PACK]] + [
            picked[k * rows + g * PACK : k * rows + (g + 1) * PACK] for k in range(others)
        ]
        part_ref[g * PACK : (g + 1) * PACK] = grouped_product(
            rhs,
            jnp.concatenate(left, axis=1),
            lambda i: jnp.concatenate(
                [near_ref[i, 0], near_ref[i, 2:].reshape(others * width, width)], axis=0
            ),
            g,
        )


def spline_kernel(
    rhs, code_vmem, part_ref, mirror_ref, gate_ref, near_ref, spline_ref,
    sums_ref, keep_ref, send_ref, code_ref, loads_ref, acc, sem,
):
    copy = pltpu.make_async_copy(code_vmem, code_ref, sem)
    copy.start()
    block_count, splines = code_ref.shape
    rows, width = part_ref.shape
    for g in range(rows // PACK):
        group = slice(g * PACK, (g + 1) * PACK)
        far = grouped_product(rhs, mirror_ref[group], lambda i: near_ref[i, 1], g)
        sums_ref[group] = part_ref[group] + far
        loads_ref[group] = gate_ref[...] * sums_ref[group]
    acc[...] = jnp.zeros(acc.shape, jnp.float32)
    upper = lax.broadcasted_iota(jnp.int32, (TILE, width), 0) // rhs
    blank = jnp.zeros((TILE, width), jnp.float32)
    copy.wait()
    for pair in range(0, block_count, 2):
        both = loads_ref[pair * rhs : (pair + 2) * rhs]
        turned = pltpu.roll(both, rhs, 0)
        mine = jnp.concatenate(
            [
                jnp.concatenate([jnp.where(upper == 0, both, turned), blank], axis=1),
                jnp.concatenate([blank, jnp.where(upper == 0, turned, both)], axis=1),
            ],
            axis=0,
        ).astype(jnp.bfloat16)
        blocks = jnp.concatenate(
            [
                jnp.concatenate([spline_ref[i, s] for s in range(splines)], axis=1)
                for i in (pair, pair + 1)
            ],
            axis=0,
        )
        product = jnp.dot(mine, blocks, preferred_element_type=jnp.float32)
        for i in (pair, pair + 1):
            total = product[(i - pair) * TILE : (i - pair + 1) * TILE]
            places, sums = [], []
            for s in range(splines):
                code = code_ref[i, s]
                place = code >> 1
                added = jnp.where(upper == (code & 1), total[:, s * width : (s + 1) * width], 0.0)
                places.append(place)
                sums.append(acc[place] + added)
            for place, value in zip(places, sums):
                acc[place] = value
    tiles = acc.shape[0] // 2
    keep_ref[...] = acc[:tiles].reshape(keep_ref.shape)
    send_ref[...] = acc[tiles:].reshape(send_ref.shape).astype(send_ref.dtype)


def split_kernel(held_ref, got_ref, *out_refs):
    size = out_refs[0].shape[0]
    for step, out_ref in enumerate(out_refs):
        for place in range(size):
            total = held_ref[step * size + place] + got_ref[step * size + place].astype(jnp.float32)
            out_ref[place] = total.astype(out_ref.dtype)


def column_kernel(machs, held_ref, *refs):
    got_refs, out_refs = refs[: -2 * machs], refs[-2 * machs :]
    for place in range(2):
        total = held_ref[place]
        for got_ref in got_refs:
            total = total + got_ref[place].astype(jnp.float32)
        for out_ref in out_refs[place * machs : (place + 1) * machs]:
            out_ref[...] = total.astype(out_ref.dtype)


def inverse_kernel(rhs, machs, *refs):
    other_refs, same_refs = refs[: 2 * machs : 2], refs[1 : 2 * machs : 2]
    inverse_ref, out_ref = refs[2 * machs :]
    parts = [
        same[...].astype(jnp.float32) + other[...].astype(jnp.float32)
        for same, other in zip(same_refs, other_refs)
    ]
    rounded = sum(parts[1:], parts[0]).astype(jnp.bfloat16)
    for g in range(rounded.shape[0] // PACK):
        out_ref[g * PACK : (g + 1) * PACK] = grouped_product(
            rhs, rounded[g * PACK : (g + 1) * PACK], lambda t: inverse_ref[t], g
        )


def swap(value, panels, apart):
    return lax.ppermute(value, "panel", [(i, i ^ apart) for i in range(panels)])


def mach_swap(value, machs, panels, turn, apart):
    pairs = [
        (mach * panels + i, (mach + turn) % machs * panels + (i ^ apart))
        for mach in range(machs)
        for i in range(panels)
    ]
    return lax.ppermute(value, ("mach", "panel"), pairs)


def cost(flops, size):
    return pl.CostEstimate(flops=flops, bytes_accessed=size, transcendentals=0)


def on_device(
    adjoint, near_blocks, pattern, trim_mask, spline_blocks, spline_owner, spline_local,
    struct_inverse,
):
    _, block_count, rhs, width = adjoint.shape
    entries = pattern.shape[1]
    panels, machs = lax.axis_size("panel"), lax.axis_size("mach")
    struct_count = struct_inverse.shape[0]
    rows, struct_rows = block_count * rhs, struct_count * rhs
    params = pltpu.CompilerParams(vmem_limit_bytes=16 * 1024 * 1024)
    f32, bf16 = jnp.float32, jnp.bfloat16
    own = adjoint.reshape(rows, width)
    beside = {0: 0, panels - 1: panels - 1}
    cross = lax.ppermute(
        own, ("mach", "panel"),
        [
            (
                mach * panels + i,
                (mach ^ (i in beside)) * panels + beside.get(i, i - 1 + 2 * (i % 2)),
            )
            for mach in range(machs)
            for i in range(panels)
        ],
    )
    mirror = swap(own, panels, panels // 2)
    pair = swap(own, panels, 1)
    expand = pl.pallas_call(
        functools.partial(spread_kernel, rhs),
        out_shape=jax.ShapeDtypeStruct((rows, block_count), bf16),
        out_specs=VMEM,
        compiler_params=params,
        cost_estimate=cost(8 * 10**9, 32 * 2**20),
        name="row_order",
    )()
    hot, gate, held, code = pl.pallas_call(
        functools.partial(pick_kernel, panels, rhs, struct_count),
        out_shape=(
            jax.ShapeDtypeStruct(((entries - 2) * rows, 4 * rows), bf16),
            jax.ShapeDtypeStruct((PACK, width), f32),
            jax.ShapeDtypeStruct((rows, width), bf16),
            jax.ShapeDtypeStruct(spline_owner.shape, jnp.int32),
        ),
        in_specs=[VMEM] * 6,
        out_specs=(VMEM,) * 4,
        compiler_params=params,
        cost_estimate=cost(10**6, 2**17),
        name="pick_rows",
    )(expand, pattern, trim_mask, own, spline_owner, spline_local)
    part = pl.pallas_call(
        functools.partial(near_kernel, rhs),
        out_shape=jax.ShapeDtypeStruct((rows, width), f32),
        in_specs=[VMEM] * 5,
        out_specs=VMEM,
        compiler_params=params,
        cost_estimate=cost(10**6, 2**17),
        name="near_field",
    )(hot, held, pair, cross, near_blocks[0])
    half = (panels // 2, struct_rows, width)
    sums, keep, send = pl.pallas_call(
        functools.partial(spline_kernel, rhs),
        out_shape=(
            jax.ShapeDtypeStruct((rows, width), f32),
            jax.ShapeDtypeStruct(half, f32),
            jax.ShapeDtypeStruct(half, bf16),
        ),
        in_specs=[VMEM] * 6,
        out_specs=(VMEM,) * 3,
        scratch_shapes=[
            pltpu.SMEM(spline_owner.shape, jnp.int32),
            pltpu.VMEM((rows, width), f32),
            pltpu.VMEM((panels * struct_rows // TILE, TILE, width), f32),
            pltpu.SemaphoreType.DMA,
        ],
        compiler_params=params,
        cost_estimate=cost(10**6, 2**17),
        name="spline_loads",
    )(code, part, mirror, gate, near_blocks[0], spline_blocks)
    loads = sums.reshape(adjoint.shape) * trim_mask[0].astype(f32)[None, None, :, None]
    got = swap(send, panels, 1)
    steps = panels // 4
    two = (2, struct_rows, width)
    keep, *sends = pl.pallas_call(
        split_kernel,
        out_shape=tuple(
            jax.ShapeDtypeStruct(two, f32 if step == 0 else bf16) for step in range(steps)
        ),
        in_specs=[VMEM, VMEM],
        out_specs=(VMEM,) * steps,
        compiler_params=params,
        cost_estimate=cost(10**6, 2**17),
        name="pair_sum",
    )(keep, got)
    got = [
        swap(sends[step - 1], panels, 4 * step + step % 2) for step in range(steps - 1, 0, -1)
    ]
    one = jax.ShapeDtypeStruct((struct_rows, width), bf16)
    columns = pl.pallas_call(
        functools.partial(column_kernel, machs),
        out_shape=(one,) * (2 * machs),
        in_specs=[VMEM] * steps,
        out_specs=(VMEM,) * (2 * machs),
        compiler_params=params,
        cost_estimate=cost(10**6, 2**17),
        name="column_sum",
    )(keep, *got)
    sames = [
        mach_swap(columns[turn], machs, panels, turn, 0) if turn else columns[0]
        for turn in range(machs)
    ]
    others = [mach_swap(columns[machs + turn], machs, panels, turn, 3) for turn in range(machs)]
    struct_adjoint = pl.pallas_call(
        functools.partial(inverse_kernel, rhs, machs),
        out_shape=jax.ShapeDtypeStruct((struct_rows, width), f32),
        in_specs=[VMEM] * (2 * machs + 1),
        out_specs=VMEM,
        compiler_params=params,
        cost_estimate=cost(10**6, 2**17),
        name="struct_solve",
    )(
        *(value for turn in range(machs - 1, -1, -1) for value in (others[turn], sames[turn])),
        struct_inverse,
    )
    return (
        loads,
        struct_adjoint.reshape(struct_count, rhs, width),
    )


def solution(mesh):
    in_specs = (
        P("mach", "panel", None, None),
        P("mach", "panel", None, None, None),
        P("panel", None),
        P("mach", None),
        P("panel", None, None, None),
        P("panel", None),
        P("panel", None),
        P("panel", None, None),
    )
    out_specs = (P("mach", "panel", None, None), P("panel", None, None))
    return jax.shard_map(
        on_device, mesh=mesh, in_specs=in_specs, out_specs=out_specs, check_vma=False
    )
```

```python
import functools

import jax
import jax.numpy as jnp
from jax import lax
from jax.experimental import pallas as pl
from jax.experimental.pallas import tpu as pltpu
from jax.sharding import PartitionSpec as P

SMEM = pl.BlockSpec(memory_space=pltpu.SMEM)
VMEM = pl.BlockSpec(memory_space=pltpu.VMEM)
PACK = 16
TILE = 8


def device_class(index):
    return (index ^ (index >> 1) ^ (index >> 2)) & 1


def spread_kernel(rhs, expand_ref):
    shape = expand_ref.shape
    expand_ref[...] = (
        lax.broadcasted_iota(jnp.int32, shape, 0) // rhs == lax.broadcasted_iota(jnp.int32, shape, 1)
    ).astype(jnp.bfloat16)


def pick_kernel(
    panels, rhs, struct_count, expand_ref, pattern_ref, trim_ref, own_ref, owner_ref, local_ref,
    hot_ref, gate_ref, held_ref, code_ref,
):
    block_count, entries = pattern_ref.shape
    rows = own_ref.shape[0]
    here = lax.axis_index("panel")
    shape = (rows, hot_ref.shape[1])
    offset = lax.broadcasted_iota(jnp.int32, shape, 1) - (
        lax.broadcasted_iota(jnp.int32, shape, 0) % rhs
    )
    block = pattern_ref[...]
    apart = (block // block_count) ^ here
    slot = jnp.where(apart == 0, 0, jnp.where(apart == 1, 1, 2))
    first = (slot * block_count + block % block_count) * rhs
    first = jnp.dot(
        expand_ref[...],
        first.astype(jnp.float32).astype(jnp.bfloat16),
        preferred_element_type=jnp.float32,
    ).astype(jnp.int32)
    for k in range(2, entries):
        hot_ref[(k - 2) * rows : (k - 1) * rows] = (offset == first[:, k : k + 1]).astype(
            jnp.bfloat16
        )
    shape = (gate_ref.shape[0], rhs)
    mine = lax.broadcasted_iota(jnp.int32, shape, 0) % rhs == lax.broadcasted_iota(
        jnp.int32, shape, 1
    )
    gate = jnp.sum(jnp.where(mine, trim_ref[...], 0).astype(jnp.float32), axis=1, keepdims=True)
    gate_ref[...] = jnp.broadcast_to(gate, gate_ref.shape)
    held_ref[...] = own_ref[...]
    owner = owner_ref[...]
    code_ref[...] = (
        (device_class(owner) ^ device_class(here)) * (panels // 2) + ((owner ^ here) >> 1)
    ) * struct_count + local_ref[...]


def grouped_product(rhs, left, blocks_of, group):
    per_group = PACK // rhs
    every = jnp.concatenate([blocks_of(group * per_group + j) for j in range(per_group)], axis=1)
    product = jnp.dot(left, every, preferred_element_type=jnp.float32)
    width = product.shape[1] // per_group
    row = lax.broadcasted_iota(jnp.int32, (PACK, width), 0)
    out = product[:, :width]
    for j in range(1, per_group):
        out = jnp.where(row // rhs == j, product[:, j * width : (j + 1) * width], out)
    return out


def near_kernel(rhs, hot_ref, own_ref, pair_ref, cross_ref, near_ref, part_ref):
    rows, width = own_ref.shape
    others = hot_ref.shape[0] // rows
    own = own_ref[...]
    pool = jnp.concatenate([own, pair_ref[...], cross_ref[...], own], axis=0)
    picked = jnp.dot(hot_ref[...], pool, preferred_element_type=jnp.float32)
    picked = picked.astype(jnp.bfloat16)
    for g in range(rows // PACK):
        left = [own[g * PACK : (g + 1) * PACK]] + [
            picked[k * rows + g * PACK : k * rows + (g + 1) * PACK] for k in range(others)
        ]
        part_ref[g * PACK : (g + 1) * PACK] = grouped_product(
            rhs,
            jnp.concatenate(left, axis=1),
            lambda i: jnp.concatenate(
                [near_ref[i, 0], near_ref[i, 2:].reshape(others * width, width)], axis=0
            ),
            g,
        )


def spline_kernel(
    rhs, _, mirror_ref, code_vmem, part_ref, gate_ref, near_ref, spline_ref,
    sums_ref, keep_ref, send_ref, code_ref, loads_ref, acc, sem,
):
    copy = pltpu.make_async_copy(code_vmem, code_ref, sem)
    copy.start()
    block_count, splines = code_ref.shape
    rows, width = part_ref.shape
    for g in range(rows // PACK):
        group = slice(g * PACK, (g + 1) * PACK)
        far = grouped_product(rhs, mirror_ref[group], lambda i: near_ref[i, 1], g)
        sums_ref[group] = part_ref[group] + far
        loads_ref[group] = gate_ref[...] * sums_ref[group]
    acc[...] = jnp.zeros(acc.shape, jnp.float32)
    upper = lax.broadcasted_iota(jnp.int32, (TILE, width), 0) // rhs
    blank = jnp.zeros((TILE, width), jnp.float32)
    copy.wait()
    for pair in range(0, block_count, 2):
        both = loads_ref[pair * rhs : (pair + 2) * rhs]
        turned = pltpu.roll(both, rhs, 0)
        mine = jnp.concatenate(
            [
                jnp.concatenate([jnp.where(upper == 0, both, turned), blank], axis=1),
                jnp.concatenate([blank, jnp.where(upper == 0, turned, both)], axis=1),
            ],
            axis=0,
        ).astype(jnp.bfloat16)
        blocks = jnp.concatenate(
            [
                jnp.concatenate([spline_ref[i, s] for s in range(splines)], axis=1)
                for i in (pair, pair + 1)
            ],
            axis=0,
        )
        product = jnp.dot(mine, blocks, preferred_element_type=jnp.float32)
        for i in (pair, pair + 1):
            total = product[(i - pair) * TILE : (i - pair + 1) * TILE]
            places, sums = [], []
            for s in range(splines):
                code = code_ref[i, s]
                place = code >> 1
                added = jnp.where(upper == (code & 1), total[:, s * width : (s + 1) * width], 0.0)
                places.append(place)
                sums.append(acc[place] + added)
            for place, value in zip(places, sums):
                acc[place] = value
    tiles = acc.shape[0] // 2
    keep_ref[...] = acc[:tiles].reshape(keep_ref.shape)
    send_ref[...] = acc[tiles:].reshape(send_ref.shape).astype(send_ref.dtype)


def split_kernel(held_ref, got_ref, *out_refs):
    size = out_refs[0].shape[0]
    for step, out_ref in enumerate(out_refs):
        for place in range(size):
            total = held_ref[step * size + place] + got_ref[step * size + place].astype(jnp.float32)
            out_ref[place] = total.astype(out_ref.dtype)


def column_kernel(machs, held_ref, *refs):
    got_refs, out_refs = refs[: -2 * machs], refs[-2 * machs :]
    for place in range(2):
        total = held_ref[place]
        for got_ref in got_refs:
            total = total + got_ref[place].astype(jnp.float32)
        for out_ref in out_refs[place * machs : (place + 1) * machs]:
            out_ref[...] = total.astype(out_ref.dtype)


def inverse_kernel(rhs, machs, *refs):
    other_refs, same_refs = refs[: 2 * machs : 2], refs[1 : 2 * machs : 2]
    inverse_ref, out_ref = refs[2 * machs :]
    parts = [
        same[...].astype(jnp.float32) + other[...].astype(jnp.float32)
        for same, other in zip(same_refs, other_refs)
    ]
    rounded = sum(parts[1:], parts[0]).astype(jnp.bfloat16)
    for g in range(rounded.shape[0] // PACK):
        out_ref[g * PACK : (g + 1) * PACK] = grouped_product(
            rhs, rounded[g * PACK : (g + 1) * PACK], lambda t: inverse_ref[t], g
        )


def swap(value, panels, apart):
    return lax.ppermute(value, "panel", [(i, i ^ apart) for i in range(panels)])


def mach_swap(value, machs, panels, turn, apart):
    pairs = [
        (mach * panels + i, (mach + turn) % machs * panels + (i ^ apart))
        for mach in range(machs)
        for i in range(panels)
    ]
    return lax.ppermute(value, ("mach", "panel"), pairs)


def cost(flops, size):
    return pl.CostEstimate(flops=flops, bytes_accessed=size, transcendentals=0)


def on_device(
    adjoint, near_blocks, pattern, trim_mask, spline_blocks, spline_owner, spline_local,
    struct_inverse,
):
    _, block_count, rhs, width = adjoint.shape
    entries = pattern.shape[1]
    panels, machs = lax.axis_size("panel"), lax.axis_size("mach")
    struct_count = struct_inverse.shape[0]
    rows, struct_rows = block_count * rhs, struct_count * rhs
    params = pltpu.CompilerParams(vmem_limit_bytes=16 * 1024 * 1024)
    f32, bf16 = jnp.float32, jnp.bfloat16
    own = adjoint.reshape(rows, width)
    beside = {0: 0, panels - 1: panels - 1}
    cross = lax.ppermute(
        own, ("mach", "panel"),
        [
            (
                mach * panels + i,
                (mach ^ (i in beside)) * panels + beside.get(i, i - 1 + 2 * (i % 2)),
            )
            for mach in range(machs)
            for i in range(panels)
        ],
    )
    mirror = swap(own, panels, panels // 2)
    pair = swap(own, panels, 1)
    expand = pl.pallas_call(
        functools.partial(spread_kernel, rhs),
        out_shape=jax.ShapeDtypeStruct((rows, block_count), bf16),
        out_specs=VMEM,
        compiler_params=params,
        cost_estimate=cost(8 * 10**9, 32 * 2**20),
        name="row_order",
    )()
    hot, gate, held, code = pl.pallas_call(
        functools.partial(pick_kernel, panels, rhs, struct_count),
        out_shape=(
            jax.ShapeDtypeStruct(((entries - 2) * rows, 4 * rows), bf16),
            jax.ShapeDtypeStruct((PACK, width), f32),
            jax.ShapeDtypeStruct((rows, width), bf16),
            jax.ShapeDtypeStruct(spline_owner.shape, jnp.int32),
        ),
        in_specs=[VMEM] * 6,
        out_specs=(VMEM,) * 4,
        compiler_params=params,
        cost_estimate=cost(10**6, 2**17),
        name="pick_rows",
    )(expand, pattern, trim_mask, own, spline_owner, spline_local)
    part = pl.pallas_call(
        functools.partial(near_kernel, rhs),
        out_shape=jax.ShapeDtypeStruct((rows, width), f32),
        in_specs=[VMEM] * 5,
        out_specs=VMEM,
        compiler_params=params,
        cost_estimate=cost(10**6, 2**17),
        name="near_field",
    )(hot, held, pair, cross, near_blocks[0])
    half = (panels // 2, struct_rows, width)
    sums, keep, send = pl.pallas_call(
        functools.partial(spline_kernel, rhs),
        out_shape=(
            jax.ShapeDtypeStruct((rows, width), f32),
            jax.ShapeDtypeStruct(half, f32),
            jax.ShapeDtypeStruct(half, bf16),
        ),
        in_specs=[VMEM] * 7,
        out_specs=(VMEM,) * 3,
        scratch_shapes=[
            pltpu.SMEM(spline_owner.shape, jnp.int32),
            pltpu.VMEM((rows, width), f32),
            pltpu.VMEM((panels * struct_rows // TILE, TILE, width), f32),
            pltpu.SemaphoreType.DMA,
        ],
        compiler_params=params,
        cost_estimate=cost(10**6, 2**17),
        name="spline_loads",
    )(pair, mirror, code, part, gate, near_blocks[0], spline_blocks)
    loads = sums.reshape(adjoint.shape) * trim_mask[0].astype(f32)[None, None, :, None]
    got = swap(send, panels, 1)
    steps = panels // 4
    two = (2, struct_rows, width)
    keep, *sends = pl.pallas_call(
        split_kernel,
        out_shape=tuple(
            jax.ShapeDtypeStruct(two, f32 if step == 0 else bf16) for step in range(steps)
        ),
        in_specs=[VMEM, VMEM],
        out_specs=(VMEM,) * steps,
        compiler_params=params,
        cost_estimate=cost(10**6, 2**17),
        name="pair_sum",
    )(keep, got)
    got = [
        swap(sends[step - 1], panels, 4 * step + step % 2) for step in range(steps - 1, 0, -1)
    ]
    one = jax.ShapeDtypeStruct((struct_rows, width), f32)
    columns = pl.pallas_call(
        functools.partial(column_kernel, machs),
        out_shape=(one,) * (2 * machs),
        in_specs=[VMEM] * steps,
        out_specs=(VMEM,) * (2 * machs),
        compiler_params=params,
        cost_estimate=cost(10**6, 2**17),
        name="column_sum",
    )(keep, *got)
    sames = [
        mach_swap(columns[turn], machs, panels, turn, 0) if turn else columns[0]
        for turn in range(machs)
    ]
    others = [mach_swap(columns[machs + turn], machs, panels, turn, 3) for turn in range(machs)]
    struct_adjoint = pl.pallas_call(
        functools.partial(inverse_kernel, rhs, machs),
        out_shape=jax.ShapeDtypeStruct((struct_rows, width), f32),
        in_specs=[VMEM] * (2 * machs + 1),
        out_specs=VMEM,
        compiler_params=params,
        cost_estimate=cost(10**6, 2**17),
        name="struct_solve",
    )(
        *(value for turn in range(machs - 1, -1, -1) for value in (others[turn], sames[turn])),
        struct_inverse,
    )
    return (
        loads,
        struct_adjoint.reshape(struct_count, rhs, width),
    )


def solution(mesh):
    in_specs = (
        P("mach", "panel", None, None),
        P("mach", "panel", None, None, None),
        P("panel", None),
        P("mach", None),
        P("panel", None, None, None),
        P("panel", None),
        P("panel", None),
        P("panel", None, None),
    )
    out_specs = (P("mach", "panel", None, None), P("panel", None, None))
    return jax.shard_map(
        on_device, mesh=mesh, in_specs=in_specs, out_specs=out_specs, check_vma=False
    )
```

```python
import functools

import jax
import jax.numpy as jnp
from jax import lax
from jax.experimental import pallas as pl
from jax.experimental.pallas import tpu as pltpu
from jax.sharding import PartitionSpec as P

SMEM = pl.BlockSpec(memory_space=pltpu.SMEM)
VMEM = pl.BlockSpec(memory_space=pltpu.VMEM)
PACK = 16
TILE = 8


def device_class(index):
    return (index ^ (index >> 1) ^ (index >> 2)) & 1


def spread_kernel(rhs, expand_ref):
    shape = expand_ref.shape
    expand_ref[...] = (
        lax.broadcasted_iota(jnp.int32, shape, 0) // rhs == lax.broadcasted_iota(jnp.int32, shape, 1)
    ).astype(jnp.bfloat16)


def pick_kernel(
    panels, rhs, struct_count, expand_ref, pattern_ref, trim_ref, own_ref, owner_ref, local_ref,
    hot_ref, gate_ref, held_ref, code_ref,
):
    block_count, entries = pattern_ref.shape
    rows = own_ref.shape[0]
    here = lax.axis_index("panel")
    shape = (rows, hot_ref.shape[1])
    offset = lax.broadcasted_iota(jnp.int32, shape, 1) - (
        lax.broadcasted_iota(jnp.int32, shape, 0) % rhs
    )
    block = pattern_ref[...]
    apart = (block // block_count) ^ here
    slot = jnp.where(apart == 0, 0, jnp.where(apart == 1, 1, 2))
    first = (slot * block_count + block % block_count) * rhs
    first = jnp.dot(
        expand_ref[...],
        first.astype(jnp.float32).astype(jnp.bfloat16),
        preferred_element_type=jnp.float32,
    ).astype(jnp.int32)
    for k in range(2, entries):
        hot_ref[(k - 2) * rows : (k - 1) * rows] = (offset == first[:, k : k + 1]).astype(
            jnp.bfloat16
        )
    shape = (gate_ref.shape[0], rhs)
    mine = lax.broadcasted_iota(jnp.int32, shape, 0) % rhs == lax.broadcasted_iota(
        jnp.int32, shape, 1
    )
    gate = jnp.sum(jnp.where(mine, trim_ref[...], 0).astype(jnp.float32), axis=1, keepdims=True)
    gate_ref[...] = jnp.broadcast_to(gate, gate_ref.shape)
    held_ref[...] = own_ref[...]
    owner = owner_ref[...]
    code_ref[...] = (
        (device_class(owner) ^ device_class(here)) * (panels // 2) + (owner >> 1)
    ) * struct_count + local_ref[...]


def grouped_product(rhs, left, blocks_of, group):
    per_group = PACK // rhs
    every = jnp.concatenate([blocks_of(group * per_group + j) for j in range(per_group)], axis=1)
    product = jnp.dot(left, every, preferred_element_type=jnp.float32)
    width = product.shape[1] // per_group
    row = lax.broadcasted_iota(jnp.int32, (PACK, width), 0)
    out = product[:, :width]
    for j in range(1, per_group):
        out = jnp.where(row // rhs == j, product[:, j * width : (j + 1) * width], out)
    return out


def near_kernel(rhs, hot_ref, own_ref, pair_ref, cross_ref, near_ref, part_ref):
    rows, width = own_ref.shape
    others = hot_ref.shape[0] // rows
    own = own_ref[...]
    pool = jnp.concatenate([own, pair_ref[...], cross_ref[...], own], axis=0)
    picked = jnp.dot(hot_ref[...], pool, preferred_element_type=jnp.float32)
    picked = picked.astype(jnp.bfloat16)
    for g in range(rows // PACK):
        left = [own[g * PACK : (g + 1) * PACK]] + [
            picked[k * rows + g * PACK : k * rows + (g + 1) * PACK] for k in range(others)
        ]
        part_ref[g * PACK : (g + 1) * PACK] = grouped_product(
            rhs,
            jnp.concatenate(left, axis=1),
            lambda i: jnp.concatenate(
                [near_ref[i, 0], near_ref[i, 2:].reshape(others * width, width)], axis=0
            ),
            g,
        )


def spline_kernel(
    rhs, _, mirror_ref, code_vmem, part_ref, gate_ref, near_ref, spline_ref,
    sums_ref, keep_ref, send_ref, code_ref, loads_ref, acc, sem,
):
    copy = pltpu.make_async_copy(code_vmem, code_ref, sem)
    copy.start()
    block_count, splines = code_ref.shape
    rows, width = part_ref.shape
    for g in range(rows // PACK):
        group = slice(g * PACK, (g + 1) * PACK)
        far = grouped_product(rhs, mirror_ref[group], lambda i: near_ref[i, 1], g)
        sums_ref[group] = part_ref[group] + far
        loads_ref[group] = gate_ref[...] * sums_ref[group]
    acc[...] = jnp.zeros(acc.shape, jnp.float32)
    upper = lax.broadcasted_iota(jnp.int32, (TILE, width), 0) // rhs
    blank = jnp.zeros((TILE, width), jnp.float32)
    copy.wait()
    for pair in range(0, block_count, 2):
        both = loads_ref[pair * rhs : (pair + 2) * rhs]
        turned = pltpu.roll(both, rhs, 0)
        mine = jnp.concatenate(
            [
                jnp.concatenate([jnp.where(upper == 0, both, turned), blank], axis=1),
                jnp.concatenate([blank, jnp.where(upper == 0, turned, both)], axis=1),
            ],
            axis=0,
        ).astype(jnp.bfloat16)
        blocks = jnp.concatenate(
            [
                jnp.concatenate([spline_ref[i, s] for s in range(splines)], axis=1)
                for i in (pair, pair + 1)
            ],
            axis=0,
        )
        product = jnp.dot(mine, blocks, preferred_element_type=jnp.float32)
        for i in (pair, pair + 1):
            total = product[(i - pair) * TILE : (i - pair + 1) * TILE]
            places, sums = [], []
            for s in range(splines):
                code = code_ref[i, s]
                place = code >> 1
                added = jnp.where(upper == (code & 1), total[:, s * width : (s + 1) * width], 0.0)
                places.append(place)
                sums.append(acc[place] + added)
            for place, value in zip(places, sums):
                acc[place] = value
    tiles = acc.shape[0] // 2
    keep_ref[...] = acc[:tiles].reshape(keep_ref.shape)
    send_ref[...] = acc[tiles:].reshape(send_ref.shape).astype(send_ref.dtype)


def sum_kernel(held_ref, got_ref, out_ref):
    for place in range(held_ref.shape[0]):
        total = held_ref[place] + got_ref[place].astype(jnp.float32)
        for copy in range(out_ref.shape[0]):
            out_ref[copy, place] = total.astype(out_ref.dtype)


def inverse_kernel(rhs, got_ref, inverse_ref, out_ref):
    sources = [got_ref[index].astype(jnp.float32) for index in range(got_ref.shape[0])]
    while len(sources) > 1:
        sources = [a + b for a, b in zip(sources[::2], sources[1::2])] + sources[len(sources) & ~1 :]
    total = sources[0]
    rounded = total.astype(jnp.bfloat16)
    for g in range(total.shape[0] // PACK):
        out_ref[g * PACK : (g + 1) * PACK] = grouped_product(
            rhs, rounded[g * PACK : (g + 1) * PACK], lambda t: inverse_ref[t], g
        )


def swap(value, panels, apart):
    return lax.ppermute(value, "panel", [(i, i ^ apart) for i in range(panels)])


def cost(flops, size):
    return pl.CostEstimate(flops=flops, bytes_accessed=size, transcendentals=0)


def on_device(
    adjoint, near_blocks, pattern, trim_mask, spline_blocks, spline_owner, spline_local,
    struct_inverse,
):
    _, block_count, rhs, width = adjoint.shape
    entries = pattern.shape[1]
    panels, machs = lax.axis_size("panel"), lax.axis_size("mach")
    struct_count = struct_inverse.shape[0]
    rows, struct_rows = block_count * rhs, struct_count * rhs
    params = pltpu.CompilerParams(vmem_limit_bytes=16 * 1024 * 1024)
    f32, bf16 = jnp.float32, jnp.bfloat16
    own = adjoint.reshape(rows, width)
    beside = {0: 0, panels - 1: panels - 1}
    cross = lax.ppermute(
        own, ("mach", "panel"),
        [
            (
                mach * panels + i,
                (mach ^ (i in beside)) * panels + beside.get(i, i - 1 + 2 * (i % 2)),
            )
            for mach in range(machs)
            for i in range(panels)
        ],
    )
    mirror = swap(own, panels, panels // 2)
    pair = swap(own, panels, 1)
    expand = pl.pallas_call(
        functools.partial(spread_kernel, rhs),
        out_shape=jax.ShapeDtypeStruct((rows, block_count), bf16),
        out_specs=VMEM,
        compiler_params=params,
        cost_estimate=cost(8 * 10**9, 32 * 2**20),
        name="row_order",
    )()
    hot, gate, held, code = pl.pallas_call(
        functools.partial(pick_kernel, panels, rhs, struct_count),
        out_shape=(
            jax.ShapeDtypeStruct(((entries - 2) * rows, 4 * rows), bf16),
            jax.ShapeDtypeStruct((PACK, width), f32),
            jax.ShapeDtypeStruct((rows, width), bf16),
            jax.ShapeDtypeStruct(spline_owner.shape, jnp.int32),
        ),
        in_specs=[VMEM] * 6,
        out_specs=(VMEM,) * 4,
        compiler_params=params,
        cost_estimate=cost(10**6, 2**17),
        name="pick_rows",
    )(expand, pattern, trim_mask, own, spline_owner, spline_local)
    part = pl.pallas_call(
        functools.partial(near_kernel, rhs),
        out_shape=jax.ShapeDtypeStruct((rows, width), f32),
        in_specs=[VMEM] * 5,
        out_specs=VMEM,
        compiler_params=params,
        cost_estimate=cost(10**6, 2**17),
        name="near_field",
    )(hot, held, pair, cross, near_blocks[0])
    half = (panels // 2, struct_rows, width)
    sums, keep, send = pl.pallas_call(
        functools.partial(spline_kernel, rhs),
        out_shape=(
            jax.ShapeDtypeStruct((rows, width), f32),
            jax.ShapeDtypeStruct(half, f32),
            jax.ShapeDtypeStruct(half, bf16),
        ),
        in_specs=[VMEM] * 7,
        out_specs=(VMEM,) * 3,
        scratch_shapes=[
            pltpu.SMEM(spline_owner.shape, jnp.int32),
            pltpu.VMEM((rows, width), f32),
            pltpu.VMEM((panels * struct_rows // TILE, TILE, width), f32),
            pltpu.SemaphoreType.DMA,
        ],
        compiler_params=params,
        cost_estimate=cost(10**6, 2**17),
        name="spline_loads",
    )(pair, mirror, code, part, gate, near_blocks[0], spline_blocks)
    loads = sums.reshape(adjoint.shape) * trim_mask[0].astype(f32)[None, None, :, None]
    got = swap(send, panels, 1)
    send = pl.pallas_call(
        sum_kernel,
        out_shape=jax.ShapeDtypeStruct((machs, *half), bf16),
        in_specs=[VMEM, VMEM],
        out_specs=VMEM,
        compiler_params=params,
        cost_estimate=cost(10**6, 2**20),
        name="pair_sum",
    )(keep, got)
    got = lax.all_to_all(
        send.reshape(machs * panels // 2, struct_rows, width), ("mach", "panel"),
        split_axis=0, concat_axis=0, tiled=True,
        axis_index_groups=[
            [
                mach * panels + 2 * chip + (device_class(2 * chip) ^ which)
                for mach in range(machs)
                for chip in range(panels // 2)
            ]
            for which in range(2)
        ],
    )
    struct_adjoint = pl.pallas_call(
        functools.partial(inverse_kernel, rhs),
        out_shape=jax.ShapeDtypeStruct((struct_rows, width), f32),
        in_specs=[VMEM] * 2,
        out_specs=VMEM,
        compiler_params=params,
        cost_estimate=cost(10**9, 2**20),
        name="struct_solve",
    )(got, struct_inverse)
    return (
        loads,
        struct_adjoint.reshape(struct_count, rhs, width),
    )


def solution(mesh):
    in_specs = (
        P("mach", "panel", None, None),
        P("mach", "panel", None, None, None),
        P("panel", None),
        P("mach", None),
        P("panel", None, None, None),
        P("panel", None),
        P("panel", None),
        P("panel", None, None),
    )
    out_specs = (P("mach", "panel", None, None), P("panel", None, None))
    return jax.shard_map(
        on_device, mesh=mesh, in_specs=in_specs, out_specs=out_specs, check_vma=False
    )
```

```python
import functools

import jax
import jax.numpy as jnp
from jax import lax
from jax.experimental import pallas as pl
from jax.experimental.pallas import tpu as pltpu
from jax.sharding import PartitionSpec as P

SMEM = pl.BlockSpec(memory_space=pltpu.SMEM)
VMEM = pl.BlockSpec(memory_space=pltpu.VMEM)
PACK = 16
TILE = 8


def device_class(index):
    return (index ^ (index >> 1) ^ (index >> 2)) & 1


def spread_kernel(rhs, expand_ref):
    shape = expand_ref.shape
    expand_ref[...] = (
        lax.broadcasted_iota(jnp.int32, shape, 0) // rhs == lax.broadcasted_iota(jnp.int32, shape, 1)
    ).astype(jnp.bfloat16)


def pick_kernel(
    panels, rhs, struct_count, expand_ref, pattern_ref, trim_ref, own_ref, owner_ref, local_ref,
    hot_ref, gate_ref, held_ref, code_ref,
):
    block_count, entries = pattern_ref.shape
    rows = own_ref.shape[0]
    here = lax.axis_index("panel")
    shape = (rows, hot_ref.shape[1])
    offset = lax.broadcasted_iota(jnp.int32, shape, 1) - (
        lax.broadcasted_iota(jnp.int32, shape, 0) % rhs
    )
    block = pattern_ref[...]
    apart = (block // block_count) ^ here
    slot = jnp.where(apart == 0, 0, jnp.where(apart == 1, 1, 2))
    first = (slot * block_count + block % block_count) * rhs
    first = jnp.dot(
        expand_ref[...],
        first.astype(jnp.float32).astype(jnp.bfloat16),
        preferred_element_type=jnp.float32,
    ).astype(jnp.int32)
    for k in range(2, entries):
        hot_ref[(k - 2) * rows : (k - 1) * rows] = (offset == first[:, k : k + 1]).astype(
            jnp.bfloat16
        )
    shape = (gate_ref.shape[0], rhs)
    mine = lax.broadcasted_iota(jnp.int32, shape, 0) % rhs == lax.broadcasted_iota(
        jnp.int32, shape, 1
    )
    gate = jnp.sum(jnp.where(mine, trim_ref[...], 0).astype(jnp.float32), axis=1, keepdims=True)
    gate_ref[...] = jnp.broadcast_to(gate, gate_ref.shape)
    held_ref[...] = own_ref[...]
    owner = owner_ref[...]
    code_ref[...] = (
        (device_class(owner) ^ device_class(here)) * (panels // 2)
        + (owner >> 2) * 2
        + (((owner ^ here) >> 1) & 1)
    ) * struct_count + local_ref[...]


def grouped_product(rhs, left, blocks_of, group):
    per_group = PACK // rhs
    every = jnp.concatenate([blocks_of(group * per_group + j) for j in range(per_group)], axis=1)
    product = jnp.dot(left, every, preferred_element_type=jnp.float32)
    width = product.shape[1] // per_group
    row = lax.broadcasted_iota(jnp.int32, (PACK, width), 0)
    out = product[:, :width]
    for j in range(1, per_group):
        out = jnp.where(row // rhs == j, product[:, j * width : (j + 1) * width], out)
    return out


def near_kernel(rhs, hot_ref, own_ref, pair_ref, cross_ref, near_ref, part_ref):
    rows, width = own_ref.shape
    others = hot_ref.shape[0] // rows
    own = own_ref[...]
    pool = jnp.concatenate([own, pair_ref[...], cross_ref[...], own], axis=0)
    picked = jnp.dot(hot_ref[...], pool, preferred_element_type=jnp.float32)
    picked = picked.astype(jnp.bfloat16)
    for g in range(rows // PACK):
        left = [own[g * PACK : (g + 1) * PACK]] + [
            picked[k * rows + g * PACK : k * rows + (g + 1) * PACK] for k in range(others)
        ]
        part_ref[g * PACK : (g + 1) * PACK] = grouped_product(
            rhs,
            jnp.concatenate(left, axis=1),
            lambda i: jnp.concatenate(
                [near_ref[i, 0], near_ref[i, 2:].reshape(others * width, width)], axis=0
            ),
            g,
        )


def spline_kernel(
    rhs, _, mirror_ref, code_vmem, part_ref, gate_ref, near_ref, spline_ref,
    sums_ref, keep_ref, send_ref, code_ref, loads_ref, acc, sem,
):
    copy = pltpu.make_async_copy(code_vmem, code_ref, sem)
    copy.start()
    block_count, splines = code_ref.shape
    rows, width = part_ref.shape
    for g in range(rows // PACK):
        group = slice(g * PACK, (g + 1) * PACK)
        far = grouped_product(rhs, mirror_ref[group], lambda i: near_ref[i, 1], g)
        sums_ref[group] = part_ref[group] + far
        loads_ref[group] = gate_ref[...] * sums_ref[group]
    acc[...] = jnp.zeros(acc.shape, jnp.float32)
    upper = lax.broadcasted_iota(jnp.int32, (TILE, width), 0) // rhs
    blank = jnp.zeros((TILE, width), jnp.float32)
    copy.wait()
    for pair in range(0, block_count, 2):
        both = loads_ref[pair * rhs : (pair + 2) * rhs]
        turned = pltpu.roll(both, rhs, 0)
        mine = jnp.concatenate(
            [
                jnp.concatenate([jnp.where(upper == 0, both, turned), blank], axis=1),
                jnp.concatenate([blank, jnp.where(upper == 0, turned, both)], axis=1),
            ],
            axis=0,
        ).astype(jnp.bfloat16)
        blocks = jnp.concatenate(
            [
                jnp.concatenate([spline_ref[i, s] for s in range(splines)], axis=1)
                for i in (pair, pair + 1)
            ],
            axis=0,
        )
        product = jnp.dot(mine, blocks, preferred_element_type=jnp.float32)
        for i in (pair, pair + 1):
            total = product[(i - pair) * TILE : (i - pair + 1) * TILE]
            places, sums = [], []
            for s in range(splines):
                code = code_ref[i, s]
                place = code >> 1
                added = jnp.where(upper == (code & 1), total[:, s * width : (s + 1) * width], 0.0)
                places.append(place)
                sums.append(acc[place] + added)
            for place, value in zip(places, sums):
                acc[place] = value
    tiles = acc.shape[0] // 2
    keep_ref[...] = acc[:tiles].reshape(keep_ref.shape)
    send_ref[...] = acc[tiles:].reshape(send_ref.shape).astype(send_ref.dtype)


def sum_kernel(held_ref, got_ref, out_ref):
    for place in range(held_ref.shape[0]):
        total = held_ref[place] + got_ref[place].astype(jnp.float32)
        out_ref[place] = total.astype(out_ref.dtype)


def column_kernel(machs, got_ref, *out_refs):
    for place in range(2):
        total = got_ref[place].astype(jnp.float32)
        for source in range(place + 2, got_ref.shape[0], 2):
            total = total + got_ref[source].astype(jnp.float32)
        for out_ref in out_refs[place * machs : (place + 1) * machs]:
            out_ref[...] = total.astype(out_ref.dtype)


def inverse_kernel(rhs, machs, *refs):
    other_refs, same_refs = refs[: 2 * machs : 2], refs[1 : 2 * machs : 2]
    inverse_ref, out_ref = refs[2 * machs :]
    parts = [
        same[...].astype(jnp.float32) + other[...].astype(jnp.float32)
        for same, other in zip(same_refs, other_refs)
    ]
    rounded = sum(parts[1:], parts[0]).astype(jnp.bfloat16)
    for g in range(rounded.shape[0] // PACK):
        out_ref[g * PACK : (g + 1) * PACK] = grouped_product(
            rhs, rounded[g * PACK : (g + 1) * PACK], lambda t: inverse_ref[t], g
        )


def swap(value, panels, apart):
    return lax.ppermute(value, "panel", [(i, i ^ apart) for i in range(panels)])


def mach_swap(value, machs, panels, turn, apart):
    pairs = [
        (mach * panels + i, (mach + turn) % machs * panels + (i ^ apart))
        for mach in range(machs)
        for i in range(panels)
    ]
    return lax.ppermute(value, ("mach", "panel"), pairs)


def cost(flops, size):
    return pl.CostEstimate(flops=flops, bytes_accessed=size, transcendentals=0)


def on_device(
    adjoint, near_blocks, pattern, trim_mask, spline_blocks, spline_owner, spline_local,
    struct_inverse,
):
    _, block_count, rhs, width = adjoint.shape
    entries = pattern.shape[1]
    panels, machs = lax.axis_size("panel"), lax.axis_size("mach")
    struct_count = struct_inverse.shape[0]
    rows, struct_rows = block_count * rhs, struct_count * rhs
    params = pltpu.CompilerParams(vmem_limit_bytes=16 * 1024 * 1024)
    f32, bf16 = jnp.float32, jnp.bfloat16
    own = adjoint.reshape(rows, width)
    beside = {0: 0, panels - 1: panels - 1}
    cross = lax.ppermute(
        own, ("mach", "panel"),
        [
            (
                mach * panels + i,
                (mach ^ (i in beside)) * panels + beside.get(i, i - 1 + 2 * (i % 2)),
            )
            for mach in range(machs)
            for i in range(panels)
        ],
    )
    mirror = swap(own, panels, panels // 2)
    pair = swap(own, panels, 1)
    expand = pl.pallas_call(
        functools.partial(spread_kernel, rhs),
        out_shape=jax.ShapeDtypeStruct((rows, block_count), bf16),
        out_specs=VMEM,
        compiler_params=params,
        cost_estimate=cost(8 * 10**9, 32 * 2**20),
        name="row_order",
    )()
    hot, gate, held, code = pl.pallas_call(
        functools.partial(pick_kernel, panels, rhs, struct_count),
        out_shape=(
            jax.ShapeDtypeStruct(((entries - 2) * rows, 4 * rows), bf16),
            jax.ShapeDtypeStruct((PACK, width), f32),
            jax.ShapeDtypeStruct((rows, width), bf16),
            jax.ShapeDtypeStruct(spline_owner.shape, jnp.int32),
        ),
        in_specs=[VMEM] * 6,
        out_specs=(VMEM,) * 4,
        compiler_params=params,
        cost_estimate=cost(10**6, 2**17),
        name="pick_rows",
    )(expand, pattern, trim_mask, own, spline_owner, spline_local)
    part = pl.pallas_call(
        functools.partial(near_kernel, rhs),
        out_shape=jax.ShapeDtypeStruct((rows, width), f32),
        in_specs=[VMEM] * 5,
        out_specs=VMEM,
        compiler_params=params,
        cost_estimate=cost(10**6, 2**17),
        name="near_field",
    )(hot, held, pair, cross, near_blocks[0])
    half = (panels // 2, struct_rows, width)
    sums, keep, send = pl.pallas_call(
        functools.partial(spline_kernel, rhs),
        out_shape=(
            jax.ShapeDtypeStruct((rows, width), f32),
            jax.ShapeDtypeStruct(half, f32),
            jax.ShapeDtypeStruct(half, bf16),
        ),
        in_specs=[VMEM] * 7,
        out_specs=(VMEM,) * 3,
        scratch_shapes=[
            pltpu.SMEM(spline_owner.shape, jnp.int32),
            pltpu.VMEM((rows, width), f32),
            pltpu.VMEM((panels * struct_rows // TILE, TILE, width), f32),
            pltpu.SemaphoreType.DMA,
        ],
        compiler_params=params,
        cost_estimate=cost(10**6, 2**17),
        name="spline_loads",
    )(pair, mirror, code, part, gate, near_blocks[0], spline_blocks)
    loads = sums.reshape(adjoint.shape) * trim_mask[0].astype(f32)[None, None, :, None]
    got = swap(send, panels, 1)
    send = pl.pallas_call(
        sum_kernel,
        out_shape=jax.ShapeDtypeStruct(half, bf16),
        in_specs=[VMEM, VMEM],
        out_specs=VMEM,
        compiler_params=params,
        cost_estimate=cost(10**6, 2**17),
        name="pair_sum",
    )(keep, got)
    got = lax.all_to_all(
        send, "panel", split_axis=0, concat_axis=0, tiled=True,
        axis_index_groups=[
            [4 * far + (start ^ (far & 1)) for far in range(panels // 4)] for start in range(4)
        ],
    )
    one = jax.ShapeDtypeStruct((struct_rows, width), f32)
    columns = pl.pallas_call(
        functools.partial(column_kernel, machs),
        out_shape=(one,) * (2 * machs),
        in_specs=[VMEM],
        out_specs=(VMEM,) * (2 * machs),
        compiler_params=params,
        cost_estimate=cost(10**6, 2**17),
        name="column_sum",
    )(got)
    sames = [
        mach_swap(columns[turn], machs, panels, turn, 0) if turn else columns[0]
        for turn in range(machs)
    ]
    others = [mach_swap(columns[machs + turn], machs, panels, turn, 3) for turn in range(machs)]
    struct_adjoint = pl.pallas_call(
        functools.partial(inverse_kernel, rhs, machs),
        out_shape=jax.ShapeDtypeStruct((struct_rows, width), f32),
        in_specs=[VMEM] * (2 * machs + 1),
        out_specs=VMEM,
        compiler_params=params,
        cost_estimate=cost(10**6, 2**17),
        name="struct_solve",
    )(
        *(value for turn in range(machs - 1, -1, -1) for value in (others[turn], sames[turn])),
        struct_inverse,
    )
    return (
        loads,
        struct_adjoint.reshape(struct_count, rhs, width),
    )


def solution(mesh):
    in_specs = (
        P("mach", "panel", None, None),
        P("mach", "panel", None, None, None),
        P("panel", None),
        P("mach", None),
        P("panel", None, None, None),
        P("panel", None),
        P("panel", None),
        P("panel", None, None),
    )
    out_specs = (P("mach", "panel", None, None), P("panel", None, None))
    return jax.shard_map(
        on_device, mesh=mesh, in_specs=in_specs, out_specs=out_specs, check_vma=False
    )
```

```python
import functools

import jax
import jax.numpy as jnp
from jax import lax
from jax.experimental import pallas as pl
from jax.experimental.pallas import tpu as pltpu
from jax.sharding import PartitionSpec as P

SMEM = pl.BlockSpec(memory_space=pltpu.SMEM)
VMEM = pl.BlockSpec(memory_space=pltpu.VMEM)
PACK = 16
TILE = 8


def device_class(index):
    return (index ^ (index >> 1) ^ (index >> 2)) & 1


def spread_kernel(rhs, expand_ref):
    shape = expand_ref.shape
    expand_ref[...] = (
        lax.broadcasted_iota(jnp.int32, shape, 0) // rhs == lax.broadcasted_iota(jnp.int32, shape, 1)
    ).astype(jnp.bfloat16)


def pick_kernel(
    panels, rhs, struct_count, expand_ref, pattern_ref, trim_ref, own_ref, owner_ref, local_ref,
    hot_ref, gate_ref, held_ref, code_ref,
):
    block_count, entries = pattern_ref.shape
    rows = own_ref.shape[0]
    here = lax.axis_index("panel")
    shape = (rows, hot_ref.shape[1])
    offset = lax.broadcasted_iota(jnp.int32, shape, 1) - (
        lax.broadcasted_iota(jnp.int32, shape, 0) % rhs
    )
    block = pattern_ref[...]
    apart = (block // block_count) ^ here
    slot = jnp.where(apart == 0, 0, jnp.where(apart == 1, 1, 2))
    first = (slot * block_count + block % block_count) * rhs
    first = jnp.dot(
        expand_ref[...],
        first.astype(jnp.float32).astype(jnp.bfloat16),
        preferred_element_type=jnp.float32,
    ).astype(jnp.int32)
    for k in range(2, entries):
        hot_ref[(k - 2) * rows : (k - 1) * rows] = (offset == first[:, k : k + 1]).astype(
            jnp.bfloat16
        )
    shape = (gate_ref.shape[0], rhs)
    mine = lax.broadcasted_iota(jnp.int32, shape, 0) % rhs == lax.broadcasted_iota(
        jnp.int32, shape, 1
    )
    gate = jnp.sum(jnp.where(mine, trim_ref[...], 0).astype(jnp.float32), axis=1, keepdims=True)
    gate_ref[...] = jnp.broadcast_to(gate, gate_ref.shape)
    held_ref[...] = own_ref[...]
    owner = owner_ref[...]
    code_ref[...] = (
        (device_class(owner) ^ device_class(here)) * (panels // 2) + ((owner ^ here) >> 1)
    ) * struct_count + local_ref[...]


def grouped_product(rhs, left, blocks_of, group):
    per_group = PACK // rhs
    every = jnp.concatenate([blocks_of(group * per_group + j) for j in range(per_group)], axis=1)
    product = jnp.dot(left, every, preferred_element_type=jnp.float32)
    width = product.shape[1] // per_group
    row = lax.broadcasted_iota(jnp.int32, (PACK, width), 0)
    out = product[:, :width]
    for j in range(1, per_group):
        out = jnp.where(row // rhs == j, product[:, j * width : (j + 1) * width], out)
    return out


def near_kernel(rhs, hot_ref, own_ref, pair_ref, cross_ref, near_ref, part_ref):
    rows, width = own_ref.shape
    others = hot_ref.shape[0] // rows
    own = own_ref[...]
    pool = jnp.concatenate([own, pair_ref[...], cross_ref[...], own], axis=0)
    picked = jnp.dot(hot_ref[...], pool, preferred_element_type=jnp.float32)
    picked = picked.astype(jnp.bfloat16)
    for g in range(rows // PACK):
        left = [own[g * PACK : (g + 1) * PACK]] + [
            picked[k * rows + g * PACK : k * rows + (g + 1) * PACK] for k in range(others)
        ]
        part_ref[g * PACK : (g + 1) * PACK] = grouped_product(
            rhs,
            jnp.concatenate(left, axis=1),
            lambda i: jnp.concatenate(
                [near_ref[i, 0], near_ref[i, 2:].reshape(others * width, width)], axis=0
            ),
            g,
        )


def spline_kernel(
    rhs, _, mirror_ref, code_vmem, part_ref, gate_ref, near_ref, spline_ref,
    sums_ref, keep_ref, send_ref, code_ref, loads_ref, acc, sem,
):
    copy = pltpu.make_async_copy(code_vmem, code_ref, sem)
    copy.start()
    block_count, splines = code_ref.shape
    rows, width = part_ref.shape
    for g in range(rows // PACK):
        group = slice(g * PACK, (g + 1) * PACK)
        far = grouped_product(rhs, mirror_ref[group], lambda i: near_ref[i, 1], g)
        sums_ref[group] = part_ref[group] + far
        loads_ref[group] = gate_ref[...] * sums_ref[group]
    acc[...] = jnp.zeros(acc.shape, jnp.float32)
    upper = lax.broadcasted_iota(jnp.int32, (TILE, width), 0) // rhs
    blank = jnp.zeros((TILE, width), jnp.float32)

    def pair_product(pair):
        both = loads_ref[pair * rhs : (pair + 2) * rhs]
        turned = pltpu.roll(both, rhs, 0)
        mine = jnp.concatenate(
            [
                jnp.concatenate([jnp.where(upper == 0, both, turned), blank], axis=1),
                jnp.concatenate([blank, jnp.where(upper == 0, turned, both)], axis=1),
            ],
            axis=0,
        ).astype(jnp.bfloat16)
        blocks = jnp.concatenate(
            [
                jnp.concatenate([spline_ref[i, s] for s in range(splines)], axis=1)
                for i in (pair, pair + 1)
            ],
            axis=0,
        )
        return jnp.dot(mine, blocks, preferred_element_type=jnp.float32)

    pairs = range(0, block_count, 2)
    products = {pair: pair_product(pair) for pair in pairs[:-1]}
    copy.wait()
    products[pairs[-1]] = pair_product(pairs[-1])
    for pair, product in products.items():
        for i in (pair, pair + 1):
            total = product[(i - pair) * TILE : (i - pair + 1) * TILE]
            places, sums = [], []
            for s in range(splines):
                code = code_ref[i, s]
                place = code >> 1
                added = jnp.where(upper == (code & 1), total[:, s * width : (s + 1) * width], 0.0)
                places.append(place)
                sums.append(acc[place] + added)
            for place, value in zip(places, sums):
                acc[place] = value
    tiles = acc.shape[0] // 2
    keep_ref[...] = acc[:tiles].reshape(keep_ref.shape)
    send_ref[...] = acc[tiles:].reshape(send_ref.shape).astype(send_ref.dtype)


def split_kernel(held_ref, got_ref, *out_refs):
    size = out_refs[0].shape[0]
    for step, out_ref in enumerate(out_refs):
        for place in range(size):
            total = held_ref[step * size + place] + got_ref[step * size + place].astype(jnp.float32)
            out_ref[place] = total.astype(out_ref.dtype)


def column_kernel(machs, held_ref, *refs):
    got_refs, out_refs = refs[: -2 * machs], refs[-2 * machs :]
    for place in range(2):
        total = held_ref[place]
        for got_ref in got_refs:
            total = total + got_ref[place].astype(jnp.float32)
        for out_ref in out_refs[place * machs : (place + 1) * machs]:
            out_ref[...] = total.astype(out_ref.dtype)


def inverse_kernel(rhs, machs, *refs):
    other_refs, same_refs = refs[: 2 * machs : 2], refs[1 : 2 * machs : 2]
    inverse_ref, out_ref = refs[2 * machs :]
    parts = [
        same[...].astype(jnp.float32) + other[...].astype(jnp.float32)
        for same, other in zip(same_refs, other_refs)
    ]
    rounded = sum(parts[1:], parts[0]).astype(jnp.bfloat16)
    for g in range(rounded.shape[0] // PACK):
        out_ref[g * PACK : (g + 1) * PACK] = grouped_product(
            rhs, rounded[g * PACK : (g + 1) * PACK], lambda t: inverse_ref[t], g
        )


def swap(value, panels, apart):
    return lax.ppermute(value, "panel", [(i, i ^ apart) for i in range(panels)])


def mach_swap(value, machs, panels, turn, apart):
    pairs = [
        (mach * panels + i, (mach + turn) % machs * panels + (i ^ apart))
        for mach in range(machs)
        for i in range(panels)
    ]
    return lax.ppermute(value, ("mach", "panel"), pairs)


def cost(flops, size):
    return pl.CostEstimate(flops=flops, bytes_accessed=size, transcendentals=0)


def on_device(
    adjoint, near_blocks, pattern, trim_mask, spline_blocks, spline_owner, spline_local,
    struct_inverse,
):
    _, block_count, rhs, width = adjoint.shape
    entries = pattern.shape[1]
    panels, machs = lax.axis_size("panel"), lax.axis_size("mach")
    struct_count = struct_inverse.shape[0]
    rows, struct_rows = block_count * rhs, struct_count * rhs
    params = pltpu.CompilerParams(vmem_limit_bytes=16 * 1024 * 1024)
    f32, bf16 = jnp.float32, jnp.bfloat16
    own = adjoint.reshape(rows, width)
    beside = {0: 0, panels - 1: panels - 1}
    cross = lax.ppermute(
        own, ("mach", "panel"),
        [
            (
                mach * panels + i,
                (mach ^ (i in beside)) * panels + beside.get(i, i - 1 + 2 * (i % 2)),
            )
            for mach in range(machs)
            for i in range(panels)
        ],
    )
    mirror = swap(own, panels, panels // 2)
    pair = swap(own, panels, 1)
    expand = pl.pallas_call(
        functools.partial(spread_kernel, rhs),
        out_shape=jax.ShapeDtypeStruct((rows, block_count), bf16),
        out_specs=VMEM,
        compiler_params=params,
        cost_estimate=cost(8 * 10**9, 32 * 2**20),
        name="row_order",
    )()
    hot, gate, held, code = pl.pallas_call(
        functools.partial(pick_kernel, panels, rhs, struct_count),
        out_shape=(
            jax.ShapeDtypeStruct(((entries - 2) * rows, 4 * rows), bf16),
            jax.ShapeDtypeStruct((PACK, width), f32),
            jax.ShapeDtypeStruct((rows, width), bf16),
            jax.ShapeDtypeStruct(spline_owner.shape, jnp.int32),
        ),
        in_specs=[VMEM] * 6,
        out_specs=(VMEM,) * 4,
        compiler_params=params,
        cost_estimate=cost(10**6, 2**17),
        name="pick_rows",
    )(expand, pattern, trim_mask, own, spline_owner, spline_local)
    part = pl.pallas_call(
        functools.partial(near_kernel, rhs),
        out_shape=jax.ShapeDtypeStruct((rows, width), f32),
        in_specs=[VMEM] * 5,
        out_specs=VMEM,
        compiler_params=params,
        cost_estimate=cost(10**6, 2**17),
        name="near_field",
    )(hot, held, pair, cross, near_blocks[0])
    half = (panels // 2, struct_rows, width)
    sums, keep, send = pl.pallas_call(
        functools.partial(spline_kernel, rhs),
        out_shape=(
            jax.ShapeDtypeStruct((rows, width), f32),
            jax.ShapeDtypeStruct(half, f32),
            jax.ShapeDtypeStruct(half, bf16),
        ),
        in_specs=[VMEM] * 7,
        out_specs=(VMEM,) * 3,
        scratch_shapes=[
            pltpu.SMEM(spline_owner.shape, jnp.int32),
            pltpu.VMEM((rows, width), f32),
            pltpu.VMEM((panels * struct_rows // TILE, TILE, width), f32),
            pltpu.SemaphoreType.DMA,
        ],
        compiler_params=params,
        cost_estimate=cost(10**6, 2**17),
        name="spline_loads",
    )(pair, mirror, code, part, gate, near_blocks[0], spline_blocks)
    loads = sums.reshape(adjoint.shape) * trim_mask[0].astype(f32)[None, None, :, None]
    got = swap(send, panels, 1)
    steps = panels // 4
    two = (2, struct_rows, width)
    keep, *sends = pl.pallas_call(
        split_kernel,
        out_shape=tuple(
            jax.ShapeDtypeStruct(two, f32 if step == 0 else bf16) for step in range(steps)
        ),
        in_specs=[VMEM, VMEM],
        out_specs=(VMEM,) * steps,
        compiler_params=params,
        cost_estimate=cost(10**6, 2**17),
        name="pair_sum",
    )(keep, got)
    got = [
        swap(sends[step - 1], panels, 4 * step + step % 2) for step in range(steps - 1, 0, -1)
    ]
    one = jax.ShapeDtypeStruct((struct_rows, width), f32)
    columns = pl.pallas_call(
        functools.partial(column_kernel, machs),
        out_shape=(one,) * (2 * machs),
        in_specs=[VMEM] * steps,
        out_specs=(VMEM,) * (2 * machs),
        compiler_params=params,
        cost_estimate=cost(10**6, 2**17),
        name="column_sum",
    )(keep, *got)
    sames = [
        mach_swap(columns[turn], machs, panels, turn, 0) if turn else columns[0]
        for turn in range(machs)
    ]
    others = [mach_swap(columns[machs + turn], machs, panels, turn, 3) for turn in range(machs)]
    struct_adjoint = pl.pallas_call(
        functools.partial(inverse_kernel, rhs, machs),
        out_shape=jax.ShapeDtypeStruct((struct_rows, width), f32),
        in_specs=[VMEM] * (2 * machs + 1),
        out_specs=VMEM,
        compiler_params=params,
        cost_estimate=cost(10**6, 2**17),
        name="struct_solve",
    )(
        *(value for turn in range(machs - 1, -1, -1) for value in (others[turn], sames[turn])),
        struct_inverse,
    )
    return (
        loads,
        struct_adjoint.reshape(struct_count, rhs, width),
    )


def solution(mesh):
    in_specs = (
        P("mach", "panel", None, None),
        P("mach", "panel", None, None, None),
        P("panel", None),
        P("mach", None),
        P("panel", None, None, None),
        P("panel", None),
        P("panel", None),
        P("panel", None, None),
    )
    out_specs = (P("mach", "panel", None, None), P("panel", None, None))
    return jax.shard_map(
        on_device, mesh=mesh, in_specs=in_specs, out_specs=out_specs, check_vma=False
    )
```

```python
import functools

import jax
import jax.numpy as jnp
from jax import lax
from jax.experimental import pallas as pl
from jax.experimental.pallas import tpu as pltpu
from jax.sharding import PartitionSpec as P

SMEM = pl.BlockSpec(memory_space=pltpu.SMEM)
VMEM = pl.BlockSpec(memory_space=pltpu.VMEM)
PACK = 16
TILE = 8


def device_class(index):
    return (index ^ (index >> 1) ^ (index >> 2)) & 1


def exchange_of(far, here):
    half = 1 - ((here ^ (here >> 2)) & 1)
    return far ^ (half & ((far >> 1) | (far >> 2) | (far >> 3)) & 1)


def spread_kernel(rhs, expand_ref):
    shape = expand_ref.shape
    expand_ref[...] = (
        lax.broadcasted_iota(jnp.int32, shape, 0) // rhs == lax.broadcasted_iota(jnp.int32, shape, 1)
    ).astype(jnp.bfloat16)


def pick_kernel(
    panels, rhs, struct_count, expand_ref, pattern_ref, trim_ref, own_ref, owner_ref, local_ref,
    hot_ref, gate_ref, held_ref, code_ref,
):
    block_count, entries = pattern_ref.shape
    rows = own_ref.shape[0]
    here = lax.axis_index("panel")
    shape = (rows, hot_ref.shape[1])
    offset = lax.broadcasted_iota(jnp.int32, shape, 1) - (
        lax.broadcasted_iota(jnp.int32, shape, 0) % rhs
    )
    block = pattern_ref[...]
    apart = (block // block_count) ^ here
    slot = jnp.where(apart == 0, 0, jnp.where(apart == 1, 1, 2))
    first = (slot * block_count + block % block_count) * rhs
    first = jnp.dot(
        expand_ref[...],
        first.astype(jnp.float32).astype(jnp.bfloat16),
        preferred_element_type=jnp.float32,
    ).astype(jnp.int32)
    for k in range(2, entries):
        hot_ref[(k - 2) * rows : (k - 1) * rows] = (offset == first[:, k : k + 1]).astype(
            jnp.bfloat16
        )
    shape = (gate_ref.shape[0], rhs)
    mine = lax.broadcasted_iota(jnp.int32, shape, 0) % rhs == lax.broadcasted_iota(
        jnp.int32, shape, 1
    )
    gate = jnp.sum(jnp.where(mine, trim_ref[...], 0).astype(jnp.float32), axis=1, keepdims=True)
    gate_ref[...] = jnp.broadcast_to(gate, gate_ref.shape)
    held_ref[...] = own_ref[...]
    owner = owner_ref[...]
    apart = owner ^ here
    given = device_class(owner) ^ device_class(here)
    code_ref[...] = (
        given * (panels // 2)
        + exchange_of(apart >> 2, here ^ given) * 2
        + ((apart >> 1) & 1)
    ) * struct_count + local_ref[...]


def grouped_product(rhs, left, blocks_of, group):
    per_group = PACK // rhs
    every = jnp.concatenate([blocks_of(group * per_group + j) for j in range(per_group)], axis=1)
    product = jnp.dot(left, every, preferred_element_type=jnp.float32)
    width = product.shape[1] // per_group
    row = lax.broadcasted_iota(jnp.int32, (PACK, width), 0)
    out = product[:, :width]
    for j in range(1, per_group):
        out = jnp.where(row // rhs == j, product[:, j * width : (j + 1) * width], out)
    return out


def near_kernel(rhs, hot_ref, own_ref, pair_ref, cross_ref, near_ref, part_ref):
    rows, width = own_ref.shape
    others = hot_ref.shape[0] // rows
    own = own_ref[...]
    pool = jnp.concatenate([own, pair_ref[...], cross_ref[...], own], axis=0)
    picked = jnp.dot(hot_ref[...], pool, preferred_element_type=jnp.float32)
    picked = picked.astype(jnp.bfloat16)
    for g in range(rows // PACK):
        left = [own[g * PACK : (g + 1) * PACK]] + [
            picked[k * rows + g * PACK : k * rows + (g + 1) * PACK] for k in range(others)
        ]
        part_ref[g * PACK : (g + 1) * PACK] = grouped_product(
            rhs,
            jnp.concatenate(left, axis=1),
            lambda i: jnp.concatenate(
                [near_ref[i, 0], near_ref[i, 2:].reshape(others * width, width)], axis=0
            ),
            g,
        )


def spline_kernel(
    rhs, _, mirror_ref, code_vmem, part_ref, gate_ref, near_ref, spline_ref,
    sums_ref, keep_ref, send_ref, code_ref, loads_ref, acc, sem,
):
    copy = pltpu.make_async_copy(code_vmem, code_ref, sem)
    copy.start()
    block_count, splines = code_ref.shape
    rows, width = part_ref.shape
    for g in range(rows // PACK):
        group = slice(g * PACK, (g + 1) * PACK)
        far = grouped_product(rhs, mirror_ref[group], lambda i: near_ref[i, 1], g)
        sums_ref[group] = part_ref[group] + far
        loads_ref[group] = gate_ref[...] * sums_ref[group]
    acc[...] = jnp.zeros(acc.shape, jnp.float32)
    upper = lax.broadcasted_iota(jnp.int32, (TILE, width), 0) // rhs
    blank = jnp.zeros((TILE, width), jnp.float32)

    def pair_product(pair):
        both = loads_ref[pair * rhs : (pair + 2) * rhs]
        turned = pltpu.roll(both, rhs, 0)
        mine = jnp.concatenate(
            [
                jnp.concatenate([jnp.where(upper == 0, both, turned), blank], axis=1),
                jnp.concatenate([blank, jnp.where(upper == 0, turned, both)], axis=1),
            ],
            axis=0,
        ).astype(jnp.bfloat16)
        blocks = jnp.concatenate(
            [
                jnp.concatenate([spline_ref[i, s] for s in range(splines)], axis=1)
                for i in (pair, pair + 1)
            ],
            axis=0,
        )
        return jnp.dot(mine, blocks, preferred_element_type=jnp.float32)

    pairs = range(0, block_count, 2)
    products = {pair: pair_product(pair) for pair in pairs[:-1]}
    copy.wait()
    products[pairs[-1]] = pair_product(pairs[-1])
    for pair, product in products.items():
        for i in (pair, pair + 1):
            total = product[(i - pair) * TILE : (i - pair + 1) * TILE]
            places, sums = [], []
            for s in range(splines):
                code = code_ref[i, s]
                place = code >> 1
                added = jnp.where(upper == (code & 1), total[:, s * width : (s + 1) * width], 0.0)
                places.append(place)
                sums.append(acc[place] + added)
            for place, value in zip(places, sums):
                acc[place] = value
    tiles = acc.shape[0] // 2
    keep_ref[...] = acc[:tiles].reshape(keep_ref.shape)
    send_ref[...] = acc[tiles:].reshape(send_ref.shape).astype(send_ref.dtype)


def split_kernel(held_ref, got_ref, *out_refs):
    size = out_refs[0].shape[0]
    for step, out_ref in enumerate(out_refs):
        for place in range(size):
            total = held_ref[step * size + place] + got_ref[step * size + place].astype(jnp.float32)
            out_ref[place] = total.astype(out_ref.dtype)


def column_kernel(machs, held_ref, *refs):
    got_refs, out_refs = refs[: -2 * machs], refs[-2 * machs :]
    for place in range(2):
        total = held_ref[place]
        for got_ref in got_refs:
            total = total + got_ref[place].astype(jnp.float32)
        for out_ref in out_refs[place * machs : (place + 1) * machs]:
            out_ref[...] = total.astype(out_ref.dtype)


def inverse_kernel(rhs, machs, *refs):
    other_refs, same_refs = refs[: 2 * machs : 2], refs[1 : 2 * machs : 2]
    inverse_ref, out_ref = refs[2 * machs :]
    parts = [
        same[...].astype(jnp.float32) + other[...].astype(jnp.float32)
        for same, other in zip(same_refs, other_refs)
    ]
    rounded = sum(parts[1:], parts[0]).astype(jnp.bfloat16)
    for g in range(rounded.shape[0] // PACK):
        out_ref[g * PACK : (g + 1) * PACK] = grouped_product(
            rhs, rounded[g * PACK : (g + 1) * PACK], lambda t: inverse_ref[t], g
        )


def swap(value, panels, apart):
    return lax.ppermute(value, "panel", [(i, i ^ apart) for i in range(panels)])


def mach_swap(value, machs, panels, turn, apart):
    pairs = [
        (mach * panels + i, (mach + turn) % machs * panels + (i ^ apart))
        for mach in range(machs)
        for i in range(panels)
    ]
    return lax.ppermute(value, ("mach", "panel"), pairs)


def cost(flops, size):
    return pl.CostEstimate(flops=flops, bytes_accessed=size, transcendentals=0)


def on_device(
    adjoint, near_blocks, pattern, trim_mask, spline_blocks, spline_owner, spline_local,
    struct_inverse,
):
    _, block_count, rhs, width = adjoint.shape
    entries = pattern.shape[1]
    panels, machs = lax.axis_size("panel"), lax.axis_size("mach")
    struct_count = struct_inverse.shape[0]
    rows, struct_rows = block_count * rhs, struct_count * rhs
    params = pltpu.CompilerParams(vmem_limit_bytes=16 * 1024 * 1024)
    f32, bf16 = jnp.float32, jnp.bfloat16
    own = adjoint.reshape(rows, width)
    beside = {0: 0, panels - 1: panels - 1}
    cross = lax.ppermute(
        own, ("mach", "panel"),
        [
            (
                mach * panels + i,
                (mach ^ (i in beside)) * panels + beside.get(i, i - 1 + 2 * (i % 2)),
            )
            for mach in range(machs)
            for i in range(panels)
        ],
    )
    mirror = swap(own, panels, panels // 2)
    pair = swap(own, panels, 1)
    expand = pl.pallas_call(
        functools.partial(spread_kernel, rhs),
        out_shape=jax.ShapeDtypeStruct((rows, block_count), bf16),
        out_specs=VMEM,
        compiler_params=params,
        cost_estimate=cost(8 * 10**9, 32 * 2**20),
        name="row_order",
    )()
    hot, gate, held, code = pl.pallas_call(
        functools.partial(pick_kernel, panels, rhs, struct_count),
        out_shape=(
            jax.ShapeDtypeStruct(((entries - 2) * rows, 4 * rows), bf16),
            jax.ShapeDtypeStruct((PACK, width), f32),
            jax.ShapeDtypeStruct((rows, width), bf16),
            jax.ShapeDtypeStruct(spline_owner.shape, jnp.int32),
        ),
        in_specs=[VMEM] * 6,
        out_specs=(VMEM,) * 4,
        compiler_params=params,
        cost_estimate=cost(10**6, 2**17),
        name="pick_rows",
    )(expand, pattern, trim_mask, own, spline_owner, spline_local)
    part = pl.pallas_call(
        functools.partial(near_kernel, rhs),
        out_shape=jax.ShapeDtypeStruct((rows, width), f32),
        in_specs=[VMEM] * 5,
        out_specs=VMEM,
        compiler_params=params,
        cost_estimate=cost(10**6, 2**17),
        name="near_field",
    )(hot, held, pair, cross, near_blocks[0])
    half = (panels // 2, struct_rows, width)
    sums, keep, send = pl.pallas_call(
        functools.partial(spline_kernel, rhs),
        out_shape=(
            jax.ShapeDtypeStruct((rows, width), f32),
            jax.ShapeDtypeStruct(half, f32),
            jax.ShapeDtypeStruct(half, bf16),
        ),
        in_specs=[VMEM] * 7,
        out_specs=(VMEM,) * 3,
        scratch_shapes=[
            pltpu.SMEM(spline_owner.shape, jnp.int32),
            pltpu.VMEM((rows, width), f32),
            pltpu.VMEM((panels * struct_rows // TILE, TILE, width), f32),
            pltpu.SemaphoreType.DMA,
        ],
        compiler_params=params,
        cost_estimate=cost(10**6, 2**17),
        name="spline_loads",
    )(pair, mirror, code, part, gate, near_blocks[0], spline_blocks)
    loads = sums.reshape(adjoint.shape) * trim_mask[0].astype(f32)[None, None, :, None]
    got = swap(send, panels, 1)
    steps = panels // 4
    two = (2, struct_rows, width)
    keep, *sends = pl.pallas_call(
        split_kernel,
        out_shape=tuple(
            jax.ShapeDtypeStruct(two, f32 if step == 0 else bf16) for step in range(steps)
        ),
        in_specs=[VMEM, VMEM],
        out_specs=(VMEM,) * steps,
        compiler_params=params,
        cost_estimate=cost(10**6, 2**17),
        name="pair_sum",
    )(keep, got)
    got = []
    for step in range(steps - 1, 0, -1):
        pairs = []
        for i in range(panels):
            far = exchange_of(step, i)
            pairs.append((i, i ^ (4 * far + far % 2)))
        got.append(lax.ppermute(sends[step - 1], "panel", pairs))
    one = jax.ShapeDtypeStruct((struct_rows, width), f32)
    columns = pl.pallas_call(
        functools.partial(column_kernel, machs),
        out_shape=(one,) * (2 * machs),
        in_specs=[VMEM] * steps,
        out_specs=(VMEM,) * (2 * machs),
        compiler_params=params,
        cost_estimate=cost(10**6, 2**17),
        name="column_sum",
    )(keep, *got)
    sames = [
        mach_swap(columns[turn], machs, panels, turn, 0) if turn else columns[0]
        for turn in range(machs)
    ]
    others = [mach_swap(columns[machs + turn], machs, panels, turn, 3) for turn in range(machs)]
    struct_adjoint = pl.pallas_call(
        functools.partial(inverse_kernel, rhs, machs),
        out_shape=jax.ShapeDtypeStruct((struct_rows, width), f32),
        in_specs=[VMEM] * (2 * machs + 1),
        out_specs=VMEM,
        compiler_params=params,
        cost_estimate=cost(10**6, 2**17),
        name="struct_solve",
    )(
        *(value for turn in range(machs - 1, -1, -1) for value in (others[turn], sames[turn])),
        struct_inverse,
    )
    return (
        loads,
        struct_adjoint.reshape(struct_count, rhs, width),
    )


def solution(mesh):
    in_specs = (
        P("mach", "panel", None, None),
        P("mach", "panel", None, None, None),
        P("panel", None),
        P("mach", None),
        P("panel", None, None, None),
        P("panel", None),
        P("panel", None),
        P("panel", None, None),
    )
    out_specs = (P("mach", "panel", None, None), P("panel", None, None))
    return jax.shard_map(
        on_device, mesh=mesh, in_specs=in_specs, out_specs=out_specs, check_vma=False
    )
```

```python
import functools

import jax
import jax.numpy as jnp
from jax import lax
from jax.experimental import pallas as pl
from jax.experimental.pallas import tpu as pltpu
from jax.sharding import PartitionSpec as P

SMEM = pl.BlockSpec(memory_space=pltpu.SMEM)
VMEM = pl.BlockSpec(memory_space=pltpu.VMEM)
PACK = 16
TILE = 8


def device_class(index):
    return (index ^ (index >> 1) ^ (index >> 2)) & 1


def exchange_of(far, here):
    half = 1 - ((here ^ (here >> 2)) & 1)
    return far ^ (half & ((far >> 1) | (far >> 2) | (far >> 3)) & 1)


def spread_kernel(rhs, expand_ref):
    shape = expand_ref.shape
    expand_ref[...] = (
        lax.broadcasted_iota(jnp.int32, shape, 0) // rhs == lax.broadcasted_iota(jnp.int32, shape, 1)
    ).astype(jnp.bfloat16)


def pick_kernel(
    panels, rhs, struct_count, expand_ref, pattern_ref, trim_ref, own_ref, owner_ref, local_ref,
    hot_ref, gate_ref, held_ref, code_ref,
):
    block_count, entries = pattern_ref.shape
    rows = own_ref.shape[0]
    here = lax.axis_index("panel")
    shape = (rows, hot_ref.shape[1])
    offset = lax.broadcasted_iota(jnp.int32, shape, 1) - (
        lax.broadcasted_iota(jnp.int32, shape, 0) % rhs
    )
    block = pattern_ref[...]
    apart = (block // block_count) ^ here
    slot = jnp.where(apart == 0, 0, jnp.where(apart == 1, 1, 2))
    first = (slot * block_count + block % block_count) * rhs
    first = jnp.dot(
        expand_ref[...],
        first.astype(jnp.float32).astype(jnp.bfloat16),
        preferred_element_type=jnp.float32,
    ).astype(jnp.int32)
    for k in range(2, entries):
        hot_ref[(k - 2) * rows : (k - 1) * rows] = (offset == first[:, k : k + 1]).astype(
            jnp.bfloat16
        )
    shape = (gate_ref.shape[0], rhs)
    mine = lax.broadcasted_iota(jnp.int32, shape, 0) % rhs == lax.broadcasted_iota(
        jnp.int32, shape, 1
    )
    gate = jnp.sum(jnp.where(mine, trim_ref[...], 0).astype(jnp.float32), axis=1, keepdims=True)
    gate_ref[...] = jnp.broadcast_to(gate, gate_ref.shape)
    held_ref[...] = own_ref[...]
    owner = owner_ref[...]
    apart = owner ^ here
    given = device_class(owner) ^ device_class(here)
    code_ref[...] = (
        given * (panels // 2)
        + exchange_of(apart >> 2, here ^ given) * 2
        + ((apart >> 1) & 1)
    ) * struct_count + local_ref[...]


def grouped_product(rhs, left, blocks_of, group):
    per_group = PACK // rhs
    every = jnp.concatenate([blocks_of(group * per_group + j) for j in range(per_group)], axis=1)
    product = jnp.dot(left, every, preferred_element_type=jnp.float32)
    width = product.shape[1] // per_group
    row = lax.broadcasted_iota(jnp.int32, (PACK, width), 0)
    out = product[:, :width]
    for j in range(1, per_group):
        out = jnp.where(row // rhs == j, product[:, j * width : (j + 1) * width], out)
    return out


def near_kernel(rhs, hot_ref, own_ref, pair_ref, cross_ref, near_ref, part_ref):
    rows, width = own_ref.shape
    others = hot_ref.shape[0] // rows
    own = own_ref[...]
    pool = jnp.concatenate([own, pair_ref[...], cross_ref[...], own], axis=0)
    picked = jnp.dot(hot_ref[...], pool, preferred_element_type=jnp.float32)
    picked = picked.astype(jnp.bfloat16)
    for g in range(rows // PACK):
        left = [own[g * PACK : (g + 1) * PACK]] + [
            picked[k * rows + g * PACK : k * rows + (g + 1) * PACK] for k in range(others)
        ]
        part_ref[g * PACK : (g + 1) * PACK] = grouped_product(
            rhs,
            jnp.concatenate(left, axis=1),
            lambda i: jnp.concatenate(
                [near_ref[i, 0], near_ref[i, 2:].reshape(others * width, width)], axis=0
            ),
            g,
        )


def spline_kernel(
    rhs, _, mirror_ref, code_vmem, part_ref, gate_ref, near_ref, spline_ref,
    sums_ref, acc, send_ref, code_ref, sem,
):
    copy = pltpu.make_async_copy(code_vmem, code_ref, sem)
    copy.start()
    block_count, splines = code_ref.shape
    rows, width = part_ref.shape
    tiles = acc.shape[0] // 2
    loads = []
    for g in range(rows // PACK):
        group = slice(g * PACK, (g + 1) * PACK)
        sums = part_ref[group] + grouped_product(
            rhs, mirror_ref[group], lambda i: near_ref[i, 1], g
        )
        sums_ref[group] = sums
        gated = gate_ref[...] * sums
        loads += [gated[row : row + TILE] for row in range(0, PACK, TILE)]
    acc[...] = jnp.zeros(acc.shape, jnp.float32)
    upper = lax.broadcasted_iota(jnp.int32, (TILE, width), 0) // rhs
    blank = jnp.zeros((TILE, width), jnp.float32)

    def pair_product(pair):
        both = loads[pair // 2]
        turned = pltpu.roll(both, rhs, 0)
        mine = jnp.concatenate(
            [
                jnp.concatenate([jnp.where(upper == 0, both, turned), blank], axis=1),
                jnp.concatenate([blank, jnp.where(upper == 0, turned, both)], axis=1),
            ],
            axis=0,
        ).astype(jnp.bfloat16)
        blocks = jnp.concatenate(
            [
                jnp.concatenate([spline_ref[i, s] for s in range(splines)], axis=1)
                for i in (pair, pair + 1)
            ],
            axis=0,
        )
        return jnp.dot(mine, blocks, preferred_element_type=jnp.float32)

    pairs = range(0, block_count, 2)
    products = {pair: pair_product(pair) for pair in pairs[:-1]}
    copy.wait()
    products[pairs[-1]] = pair_product(pairs[-1])
    for pair, product in products.items():
        for i in (pair, pair + 1):
            total = product[(i - pair) * TILE : (i - pair + 1) * TILE]
            places, sums = [], []
            for s in range(splines):
                code = code_ref[i, s]
                place = code >> 1
                added = jnp.where(upper == (code & 1), total[:, s * width : (s + 1) * width], 0.0)
                places.append(place)
                sums.append(acc[place] + added)
            for place, value in zip(places, sums):
                acc[place] = value
    send_ref[...] = acc[tiles:].reshape(send_ref.shape).astype(send_ref.dtype)


def split_kernel(acc, got_ref, *out_refs):
    size, struct_rows, _ = out_refs[0].shape
    height = struct_rows // TILE
    for step, out_ref in enumerate(out_refs):
        for place in range(size):
            index = step * size + place
            held = acc[index * height : (index + 1) * height].reshape(out_ref.shape[1:])
            out_ref[place] = (held + got_ref[index].astype(jnp.float32)).astype(out_ref.dtype)


def column_kernel(machs, held_ref, *refs):
    got_refs, out_refs = refs[: -2 * machs], refs[-2 * machs :]
    for place in range(2):
        total = held_ref[place]
        for got_ref in got_refs:
            total = total + got_ref[place].astype(jnp.float32)
        for out_ref in out_refs[place * machs : (place + 1) * machs]:
            out_ref[...] = total.astype(out_ref.dtype)


def inverse_kernel(rhs, machs, *refs):
    other_refs, same_refs = refs[: 2 * machs : 2], refs[1 : 2 * machs : 2]
    inverse_ref, out_ref = refs[2 * machs :]
    parts = [
        same[...].astype(jnp.float32) + other[...].astype(jnp.float32)
        for same, other in zip(same_refs, other_refs)
    ]
    rounded = sum(parts[1:], parts[0]).astype(jnp.bfloat16)
    for g in range(rounded.shape[0] // PACK):
        out_ref[g * PACK : (g + 1) * PACK] = grouped_product(
            rhs, rounded[g * PACK : (g + 1) * PACK], lambda t: inverse_ref[t], g
        )


def swap(value, panels, apart):
    return lax.ppermute(value, "panel", [(i, i ^ apart) for i in range(panels)])


def mach_swap(value, machs, panels, turn, apart):
    pairs = [
        (mach * panels + i, (mach + turn) % machs * panels + (i ^ apart))
        for mach in range(machs)
        for i in range(panels)
    ]
    return lax.ppermute(value, ("mach", "panel"), pairs)


def cost(flops, size):
    return pl.CostEstimate(flops=flops, bytes_accessed=size, transcendentals=0)


def on_device(
    adjoint, near_blocks, pattern, trim_mask, spline_blocks, spline_owner, spline_local,
    struct_inverse,
):
    _, block_count, rhs, width = adjoint.shape
    entries = pattern.shape[1]
    panels, machs = lax.axis_size("panel"), lax.axis_size("mach")
    struct_count = struct_inverse.shape[0]
    rows, struct_rows = block_count * rhs, struct_count * rhs
    params = pltpu.CompilerParams(vmem_limit_bytes=16 * 1024 * 1024)
    f32, bf16 = jnp.float32, jnp.bfloat16
    own = adjoint.reshape(rows, width)
    beside = {0: 0, panels - 1: panels - 1}
    cross = lax.ppermute(
        own, ("mach", "panel"),
        [
            (
                mach * panels + i,
                (mach ^ (i in beside)) * panels + beside.get(i, i - 1 + 2 * (i % 2)),
            )
            for mach in range(machs)
            for i in range(panels)
        ],
    )
    mirror = swap(own, panels, panels // 2)
    pair = swap(own, panels, 1)
    expand = pl.pallas_call(
        functools.partial(spread_kernel, rhs),
        out_shape=jax.ShapeDtypeStruct((rows, block_count), bf16),
        out_specs=VMEM,
        compiler_params=params,
        cost_estimate=cost(8 * 10**9, 32 * 2**20),
        name="row_order",
    )()
    hot, gate, held, code = pl.pallas_call(
        functools.partial(pick_kernel, panels, rhs, struct_count),
        out_shape=(
            jax.ShapeDtypeStruct(((entries - 2) * rows, 4 * rows), bf16),
            jax.ShapeDtypeStruct((PACK, width), f32),
            jax.ShapeDtypeStruct((rows, width), bf16),
            jax.ShapeDtypeStruct(spline_owner.shape, jnp.int32),
        ),
        in_specs=[VMEM] * 6,
        out_specs=(VMEM,) * 4,
        compiler_params=params,
        cost_estimate=cost(10**6, 2**17),
        name="pick_rows",
    )(expand, pattern, trim_mask, own, spline_owner, spline_local)
    part = pl.pallas_call(
        functools.partial(near_kernel, rhs),
        out_shape=jax.ShapeDtypeStruct((rows, width), f32),
        in_specs=[VMEM] * 5,
        out_specs=VMEM,
        compiler_params=params,
        cost_estimate=cost(10**6, 2**17),
        name="near_field",
    )(hot, held, pair, cross, near_blocks[0])
    sums, acc, send = pl.pallas_call(
        functools.partial(spline_kernel, rhs),
        out_shape=(
            jax.ShapeDtypeStruct((rows, width), f32),
            jax.ShapeDtypeStruct((panels * struct_rows // TILE, TILE, width), f32),
            jax.ShapeDtypeStruct((panels // 2, struct_rows, width), bf16),
        ),
        in_specs=[VMEM] * 7,
        out_specs=(VMEM,) * 3,
        scratch_shapes=[
            pltpu.SMEM(spline_owner.shape, jnp.int32),
            pltpu.SemaphoreType.DMA,
        ],
        compiler_params=params,
        cost_estimate=cost(10**6, 2**17),
        name="spline_loads",
    )(pair, mirror, code, part, gate, near_blocks[0], spline_blocks)
    loads = sums.reshape(adjoint.shape) * trim_mask[0].astype(f32)[None, None, :, None]
    got = swap(send, panels, 1)
    steps = panels // 4
    two = (2, struct_rows, width)
    keep, *sends = pl.pallas_call(
        split_kernel,
        out_shape=tuple(
            jax.ShapeDtypeStruct(two, f32 if step == 0 else bf16) for step in range(steps)
        ),
        in_specs=[VMEM, VMEM],
        out_specs=(VMEM,) * steps,
        compiler_params=params,
        cost_estimate=cost(10**6, 2**17),
        name="pair_sum",
    )(acc, got)
    got = []
    for step in range(steps - 1, 0, -1):
        pairs = []
        for i in range(panels):
            far = exchange_of(step, i)
            pairs.append((i, i ^ (4 * far + far % 2)))
        got.append(lax.ppermute(sends[step - 1], "panel", pairs))
    one = jax.ShapeDtypeStruct((struct_rows, width), f32)
    columns = pl.pallas_call(
        functools.partial(column_kernel, machs),
        out_shape=(one,) * (2 * machs),
        in_specs=[VMEM] * steps,
        out_specs=(VMEM,) * (2 * machs),
        compiler_params=params,
        cost_estimate=cost(10**6, 2**17),
        name="column_sum",
    )(keep, *got)
    sames = [
        mach_swap(columns[turn], machs, panels, turn, 0) if turn else columns[0]
        for turn in range(machs)
    ]
    others = [mach_swap(columns[machs + turn], machs, panels, turn, 3) for turn in range(machs)]
    struct_adjoint = pl.pallas_call(
        functools.partial(inverse_kernel, rhs, machs),
        out_shape=jax.ShapeDtypeStruct((struct_rows, width), f32),
        in_specs=[VMEM] * (2 * machs + 1),
        out_specs=VMEM,
        compiler_params=params,
        cost_estimate=cost(10**6, 2**17),
        name="struct_solve",
    )(
        *(value for turn in range(machs - 1, -1, -1) for value in (others[turn], sames[turn])),
        struct_inverse,
    )
    return (
        loads,
        struct_adjoint.reshape(struct_count, rhs, width),
    )


def solution(mesh):
    in_specs = (
        P("mach", "panel", None, None),
        P("mach", "panel", None, None, None),
        P("panel", None),
        P("mach", None),
        P("panel", None, None, None),
        P("panel", None),
        P("panel", None),
        P("panel", None, None),
    )
    out_specs = (P("mach", "panel", None, None), P("panel", None, None))
    return jax.shard_map(
        on_device, mesh=mesh, in_specs=in_specs, out_specs=out_specs, check_vma=False
    )
```

```python
import functools

import jax
import jax.numpy as jnp
from jax import lax
from jax.experimental import pallas as pl
from jax.experimental.pallas import tpu as pltpu
from jax.sharding import PartitionSpec as P

SMEM = pl.BlockSpec(memory_space=pltpu.SMEM)
VMEM = pl.BlockSpec(memory_space=pltpu.VMEM)
PACK = 16
TILE = 8


def device_class(index):
    return (index ^ (index >> 1) ^ (index >> 3)) & 1


def spread_kernel(rhs, expand_ref):
    shape = expand_ref.shape
    expand_ref[...] = (
        lax.broadcasted_iota(jnp.int32, shape, 0) // rhs == lax.broadcasted_iota(jnp.int32, shape, 1)
    ).astype(jnp.bfloat16)


def pick_kernel(
    panels, rhs, struct_count, expand_ref, pattern_ref, trim_ref, own_ref, owner_ref, local_ref,
    hot_ref, gate_ref, held_ref, code_ref,
):
    block_count, entries = pattern_ref.shape
    rows = own_ref.shape[0]
    here = lax.axis_index("panel")
    shape = (rows, hot_ref.shape[1])
    offset = lax.broadcasted_iota(jnp.int32, shape, 1) - (
        lax.broadcasted_iota(jnp.int32, shape, 0) % rhs
    )
    block = pattern_ref[...]
    apart = (block // block_count) ^ here
    slot = jnp.where(apart == 0, 0, jnp.where(apart == 1, 1, 2))
    first = (slot * block_count + block % block_count) * rhs
    first = jnp.dot(
        expand_ref[...],
        first.astype(jnp.float32).astype(jnp.bfloat16),
        preferred_element_type=jnp.float32,
    ).astype(jnp.int32)
    for k in range(2, entries):
        hot_ref[(k - 2) * rows : (k - 1) * rows] = (offset == first[:, k : k + 1]).astype(
            jnp.bfloat16
        )
    shape = (gate_ref.shape[0], rhs)
    mine = lax.broadcasted_iota(jnp.int32, shape, 0) % rhs == lax.broadcasted_iota(
        jnp.int32, shape, 1
    )
    gate = jnp.sum(jnp.where(mine, trim_ref[...], 0).astype(jnp.float32), axis=1, keepdims=True)
    gate_ref[...] = jnp.broadcast_to(gate, gate_ref.shape)
    held_ref[...] = own_ref[...]
    owner = owner_ref[...]
    code_ref[...] = (
        (device_class(owner) ^ device_class(here)) * (panels // 2) + ((owner ^ here) >> 1)
    ) * struct_count + local_ref[...]


def grouped_product(rhs, left, blocks_of, group):
    per_group = PACK // rhs
    every = jnp.concatenate([blocks_of(group * per_group + j) for j in range(per_group)], axis=1)
    product = jnp.dot(left, every, preferred_element_type=jnp.float32)
    width = product.shape[1] // per_group
    row = lax.broadcasted_iota(jnp.int32, (PACK, width), 0)
    out = product[:, :width]
    for j in range(1, per_group):
        out = jnp.where(row // rhs == j, product[:, j * width : (j + 1) * width], out)
    return out


def near_kernel(rhs, hot_ref, own_ref, pair_ref, cross_ref, near_ref, part_ref):
    rows, width = own_ref.shape
    others = hot_ref.shape[0] // rows
    own = own_ref[...]
    pool = jnp.concatenate([own, pair_ref[...], cross_ref[...], own], axis=0)
    picked = jnp.dot(hot_ref[...], pool, preferred_element_type=jnp.float32)
    picked = picked.astype(jnp.bfloat16)
    for g in range(rows // PACK):
        left = [own[g * PACK : (g + 1) * PACK]] + [
            picked[k * rows + g * PACK : k * rows + (g + 1) * PACK] for k in range(others)
        ]
        part_ref[g * PACK : (g + 1) * PACK] = grouped_product(
            rhs,
            jnp.concatenate(left, axis=1),
            lambda i: jnp.concatenate(
                [near_ref[i, 0], near_ref[i, 2:].reshape(others * width, width)], axis=0
            ),
            g,
        )


def spline_kernel(
    rhs, _, mirror_ref, code_vmem, part_ref, gate_ref, near_ref, spline_ref,
    sums_ref, acc, pair_ref, far_ref, code_ref, sem,
):
    copy = pltpu.make_async_copy(code_vmem, code_ref, sem)
    copy.start()
    block_count, splines = code_ref.shape
    rows, width = part_ref.shape
    loads = []
    for g in range(rows // PACK):
        group = slice(g * PACK, (g + 1) * PACK)
        sums = part_ref[group] + grouped_product(
            rhs, mirror_ref[group], lambda i: near_ref[i, 1], g
        )
        sums_ref[group] = sums
        gated = gate_ref[...] * sums
        loads += [gated[row : row + TILE] for row in range(0, PACK, TILE)]
    acc[...] = jnp.zeros(acc.shape, jnp.float32)
    upper = lax.broadcasted_iota(jnp.int32, (TILE, width), 0) // rhs
    blank = jnp.zeros((TILE, width), jnp.float32)

    def pair_product(pair):
        both = loads[pair // 2]
        turned = pltpu.roll(both, rhs, 0)
        mine = jnp.concatenate(
            [
                jnp.concatenate([jnp.where(upper == 0, both, turned), blank], axis=1),
                jnp.concatenate([blank, jnp.where(upper == 0, turned, both)], axis=1),
            ],
            axis=0,
        ).astype(jnp.bfloat16)
        blocks = jnp.concatenate(
            [
                jnp.concatenate([spline_ref[i, s] for s in range(splines)], axis=1)
                for i in (pair, pair + 1)
            ],
            axis=0,
        )
        return jnp.dot(mine, blocks, preferred_element_type=jnp.float32)

    pairs = range(0, block_count, 2)
    products = {pair: pair_product(pair) for pair in pairs[:-1]}
    copy.wait()
    products[pairs[-1]] = pair_product(pairs[-1])
    for pair, product in products.items():
        for i in (pair, pair + 1):
            total = product[(i - pair) * TILE : (i - pair + 1) * TILE]
            places, sums = [], []
            for s in range(splines):
                code = code_ref[i, s]
                place = code >> 1
                added = jnp.where(upper == (code & 1), total[:, s * width : (s + 1) * width], 0.0)
                places.append(place)
                sums.append(acc[place] + added)
            for place, value in zip(places, sums):
                acc[place] = value
    tiles, far_tiles = acc.shape[0] // 2, far_ref.shape[1] * far_ref.shape[2] // TILE
    kept = slice(tiles, 2 * tiles - far_tiles)
    pair_ref[...] = acc[kept].reshape(pair_ref.shape).astype(pair_ref.dtype)
    for which in range(2):
        group = slice((which + 1) * tiles - far_tiles, (which + 1) * tiles)
        far_ref[which] = acc[group].reshape(far_ref.shape[1:]).astype(far_ref.dtype)


def split_kernel(acc, got_ref, *out_refs):
    size, struct_rows, _ = out_refs[0].shape
    height = struct_rows // TILE
    for step, out_ref in enumerate(out_refs):
        for place in range(size):
            index = step * size + place
            held = acc[index * height : (index + 1) * height].reshape(out_ref.shape[1:])
            out_ref[place] = (held + got_ref[index].astype(jnp.float32)).astype(out_ref.dtype)


def hand_kernel(held_ref, far_ref, keep_ref, given_ref):
    keep_ref[...] = held_ref[...] + far_ref[0].astype(jnp.float32)
    given_ref[...] = far_ref[1]


def gather_kernel(held_ref, *refs):
    got_refs, out_ref = refs[:-1], refs[-1]
    total = held_ref[...]
    for got_ref in got_refs:
        total = total + got_ref[...].astype(jnp.float32)
    out_ref[...] = total


def column_kernel(machs, held_ref, got_ref, *out_refs):
    for place in range(2):
        total = held_ref[place] + got_ref[place].astype(jnp.float32)
        for out_ref in out_refs[place * machs : (place + 1) * machs]:
            out_ref[...] = total.astype(out_ref.dtype)


def inverse_kernel(rhs, machs, *refs):
    other_refs, same_refs = refs[: 2 * machs : 2], refs[1 : 2 * machs : 2]
    inverse_ref, out_ref = refs[2 * machs :]
    parts = [
        same[...].astype(jnp.float32) + other[...].astype(jnp.float32)
        for same, other in zip(same_refs, other_refs)
    ]
    rounded = sum(parts[1:], parts[0]).astype(jnp.bfloat16)
    for g in range(rounded.shape[0] // PACK):
        out_ref[g * PACK : (g + 1) * PACK] = grouped_product(
            rhs, rounded[g * PACK : (g + 1) * PACK], lambda t: inverse_ref[t], g
        )


def mask_of(step):
    return 4 * step + (step >> 1) % 2


def swap(value, panels, apart):
    return lax.ppermute(value, "panel", [(i, i ^ apart) for i in range(panels)])


def mach_swap(value, machs, panels, turn, apart):
    pairs = [
        (mach * panels + i, (mach + turn) % machs * panels + (i ^ apart))
        for mach in range(machs)
        for i in range(panels)
    ]
    return lax.ppermute(value, ("mach", "panel"), pairs)


def cost(flops, size):
    return pl.CostEstimate(flops=flops, bytes_accessed=size, transcendentals=0)


def on_device(
    adjoint, near_blocks, pattern, trim_mask, spline_blocks, spline_owner, spline_local,
    struct_inverse,
):
    _, block_count, rhs, width = adjoint.shape
    entries = pattern.shape[1]
    panels, machs = lax.axis_size("panel"), lax.axis_size("mach")
    struct_count = struct_inverse.shape[0]
    rows, struct_rows = block_count * rhs, struct_count * rhs
    params = pltpu.CompilerParams(vmem_limit_bytes=16 * 1024 * 1024)
    f32, bf16 = jnp.float32, jnp.bfloat16
    own = adjoint.reshape(rows, width)
    beside = {0: 0, panels - 1: panels - 1}
    cross = lax.ppermute(
        own, ("mach", "panel"),
        [
            (
                mach * panels + i,
                (mach ^ (i in beside)) * panels + beside.get(i, i - 1 + 2 * (i % 2)),
            )
            for mach in range(machs)
            for i in range(panels)
        ],
    )
    mirror = swap(own, panels, panels // 2)
    pair = swap(own, panels, 1)
    expand = pl.pallas_call(
        functools.partial(spread_kernel, rhs),
        out_shape=jax.ShapeDtypeStruct((rows, block_count), bf16),
        out_specs=VMEM,
        compiler_params=params,
        cost_estimate=cost(8 * 10**9, 32 * 2**20),
        name="row_order",
    )()
    hot, gate, held, code = pl.pallas_call(
        functools.partial(pick_kernel, panels, rhs, struct_count),
        out_shape=(
            jax.ShapeDtypeStruct(((entries - 2) * rows, 4 * rows), bf16),
            jax.ShapeDtypeStruct((PACK, width), f32),
            jax.ShapeDtypeStruct((rows, width), bf16),
            jax.ShapeDtypeStruct(spline_owner.shape, jnp.int32),
        ),
        in_specs=[VMEM] * 6,
        out_specs=(VMEM,) * 4,
        compiler_params=params,
        cost_estimate=cost(10**6, 2**17),
        name="pick_rows",
    )(expand, pattern, trim_mask, own, spline_owner, spline_local)
    part = pl.pallas_call(
        functools.partial(near_kernel, rhs),
        out_shape=jax.ShapeDtypeStruct((rows, width), f32),
        in_specs=[VMEM] * 5,
        out_specs=VMEM,
        compiler_params=params,
        cost_estimate=cost(10**6, 2**17),
        name="near_field",
    )(hot, held, pair, cross, near_blocks[0])
    steps = panels // 4
    two = (2, struct_rows, width)
    sums, acc, send, far = pl.pallas_call(
        functools.partial(spline_kernel, rhs),
        out_shape=(
            jax.ShapeDtypeStruct((rows, width), f32),
            jax.ShapeDtypeStruct((panels * struct_rows // TILE, TILE, width), f32),
            jax.ShapeDtypeStruct((2 * (steps - 1), struct_rows, width), bf16),
            jax.ShapeDtypeStruct((2, *two), bf16),
        ),
        in_specs=[VMEM] * 7,
        out_specs=(VMEM,) * 4,
        scratch_shapes=[
            pltpu.SMEM(spline_owner.shape, jnp.int32),
            pltpu.SemaphoreType.DMA,
        ],
        compiler_params=params,
        cost_estimate=cost(10**6, 2**17),
        name="spline_loads",
    )(pair, mirror, code, part, gate, near_blocks[0], spline_blocks)
    loads = sums.reshape(adjoint.shape) * trim_mask[0].astype(f32)[None, None, :, None]
    got = swap(send, panels, 1)
    far = swap(far, panels, mask_of(steps - 1))
    keep, *sends = pl.pallas_call(
        split_kernel,
        out_shape=tuple(
            jax.ShapeDtypeStruct(two, f32 if step == 0 else bf16) for step in range(steps - 1)
        ),
        in_specs=[VMEM, VMEM],
        out_specs=(VMEM,) * (steps - 1),
        compiler_params=params,
        cost_estimate=cost(10**6, 2**17),
        name="pair_sum",
    )(acc, got)
    got = [swap(sends[step - 1], panels, mask_of(step)) for step in range(steps - 2, 0, -1)]
    keep, given = pl.pallas_call(
        hand_kernel,
        out_shape=(jax.ShapeDtypeStruct(two, f32), jax.ShapeDtypeStruct(two, bf16)),
        in_specs=[VMEM, VMEM],
        out_specs=(VMEM, VMEM),
        compiler_params=params,
        cost_estimate=cost(10**6, 2**17),
        name="hand_over",
    )(keep, far)
    given = swap(given, panels, 1)
    keep = pl.pallas_call(
        gather_kernel,
        out_shape=jax.ShapeDtypeStruct(two, f32),
        in_specs=[VMEM] * (steps - 1),
        out_specs=VMEM,
        compiler_params=params,
        cost_estimate=cost(4 * 10**9, 16 * 2**20),
        name="far_sum",
    )(keep, *got)
    one = jax.ShapeDtypeStruct((struct_rows, width), f32)
    columns = pl.pallas_call(
        functools.partial(column_kernel, machs),
        out_shape=(one,) * (2 * machs),
        in_specs=[VMEM] * 2,
        out_specs=(VMEM,) * (2 * machs),
        compiler_params=params,
        cost_estimate=cost(10**6, 2**17),
        name="column_sum",
    )(keep, given)
    sames = [
        mach_swap(columns[turn], machs, panels, turn, 0) if turn else columns[0]
        for turn in range(machs)
    ]
    others = [mach_swap(columns[machs + turn], machs, panels, turn, 3) for turn in range(machs)]
    struct_adjoint = pl.pallas_call(
        functools.partial(inverse_kernel, rhs, machs),
        out_shape=jax.ShapeDtypeStruct((struct_rows, width), f32),
        in_specs=[VMEM] * (2 * machs + 1),
        out_specs=VMEM,
        compiler_params=params,
        cost_estimate=cost(10**6, 2**17),
        name="struct_solve",
    )(
        *(value for turn in range(machs - 1, -1, -1) for value in (others[turn], sames[turn])),
        struct_inverse,
    )
    return (
        loads,
        struct_adjoint.reshape(struct_count, rhs, width),
    )


def solution(mesh):
    in_specs = (
        P("mach", "panel", None, None),
        P("mach", "panel", None, None, None),
        P("panel", None),
        P("mach", None),
        P("panel", None, None, None),
        P("panel", None),
        P("panel", None),
        P("panel", None, None),
    )
    out_specs = (P("mach", "panel", None, None), P("panel", None, None))
    return jax.shard_map(
        on_device, mesh=mesh, in_specs=in_specs, out_specs=out_specs, check_vma=False
    )
```

```python
import functools

import jax
import jax.numpy as jnp
from jax import lax
from jax.experimental import pallas as pl
from jax.experimental.pallas import tpu as pltpu
from jax.sharding import PartitionSpec as P

SMEM = pl.BlockSpec(memory_space=pltpu.SMEM)
VMEM = pl.BlockSpec(memory_space=pltpu.VMEM)
PACK = 16
TILE = 8


def device_class(index):
    return (index ^ (index >> 1) ^ (index >> 3)) & 1


def spread_kernel(rhs, expand_ref):
    shape = expand_ref.shape
    expand_ref[...] = (
        lax.broadcasted_iota(jnp.int32, shape, 0) // rhs == lax.broadcasted_iota(jnp.int32, shape, 1)
    ).astype(jnp.bfloat16)


def pick_kernel(
    panels, rhs, struct_count, expand_ref, pattern_ref, trim_ref, own_ref, owner_ref, local_ref,
    hot_ref, gate_ref, held_ref, code_ref,
):
    block_count, entries = pattern_ref.shape
    rows = own_ref.shape[0]
    here = lax.axis_index("panel")
    shape = (rows, hot_ref.shape[1])
    offset = lax.broadcasted_iota(jnp.int32, shape, 1) - (
        lax.broadcasted_iota(jnp.int32, shape, 0) % rhs
    )
    block = pattern_ref[...]
    apart = (block // block_count) ^ here
    slot = jnp.where(apart == 0, 0, jnp.where(apart == 1, 1, 2))
    first = (slot * block_count + block % block_count) * rhs
    first = jnp.dot(
        expand_ref[...],
        first.astype(jnp.float32).astype(jnp.bfloat16),
        preferred_element_type=jnp.float32,
    ).astype(jnp.int32)
    for k in range(2, entries):
        hot_ref[(k - 2) * rows : (k - 1) * rows] = (offset == first[:, k : k + 1]).astype(
            jnp.bfloat16
        )
    shape = (gate_ref.shape[0], rhs)
    mine = lax.broadcasted_iota(jnp.int32, shape, 0) % rhs == lax.broadcasted_iota(
        jnp.int32, shape, 1
    )
    gate = jnp.sum(jnp.where(mine, trim_ref[...], 0).astype(jnp.float32), axis=1, keepdims=True)
    gate_ref[...] = jnp.broadcast_to(gate, gate_ref.shape)
    held_ref[...] = own_ref[...]
    owner = owner_ref[...]
    code_ref[...] = (
        (device_class(owner) ^ device_class(here)) * (panels // 2) + ((owner ^ here) >> 1)
    ) * struct_count + local_ref[...]


def grouped_product(rhs, left, blocks_of, group):
    per_group = PACK // rhs
    every = jnp.concatenate([blocks_of(group * per_group + j) for j in range(per_group)], axis=1)
    product = jnp.dot(left, every, preferred_element_type=jnp.float32)
    width = product.shape[1] // per_group
    row = lax.broadcasted_iota(jnp.int32, (PACK, width), 0)
    out = product[:, :width]
    for j in range(1, per_group):
        out = jnp.where(row // rhs == j, product[:, j * width : (j + 1) * width], out)
    return out


def near_kernel(rhs, hot_ref, own_ref, pair_ref, cross_ref, near_ref, part_ref):
    rows, width = own_ref.shape
    others = hot_ref.shape[0] // rows
    own = own_ref[...]
    pool = jnp.concatenate([own, pair_ref[...], cross_ref[...], own], axis=0)
    picked = jnp.dot(hot_ref[...], pool, preferred_element_type=jnp.float32)
    picked = picked.astype(jnp.bfloat16)
    for g in range(rows // PACK):
        left = [own[g * PACK : (g + 1) * PACK]] + [
            picked[k * rows + g * PACK : k * rows + (g + 1) * PACK] for k in range(others)
        ]
        part_ref[g * PACK : (g + 1) * PACK] = grouped_product(
            rhs,
            jnp.concatenate(left, axis=1),
            lambda i: jnp.concatenate(
                [near_ref[i, 0], near_ref[i, 2:].reshape(others * width, width)], axis=0
            ),
            g,
        )


def spline_kernel(
    rhs, _, mirror_ref, code_vmem, part_ref, gate_ref, near_ref, spline_ref,
    sums_ref, acc, pair_ref, code_ref, sem,
):
    copy = pltpu.make_async_copy(code_vmem, code_ref, sem)
    copy.start()
    block_count, splines = code_ref.shape
    rows, width = part_ref.shape
    loads = []
    for g in range(rows // PACK):
        group = slice(g * PACK, (g + 1) * PACK)
        sums = part_ref[group] + grouped_product(
            rhs, mirror_ref[group], lambda i: near_ref[i, 1], g
        )
        sums_ref[group] = sums
        gated = gate_ref[...] * sums
        loads += [gated[row : row + TILE] for row in range(0, PACK, TILE)]
    acc[...] = jnp.zeros(acc.shape, jnp.float32)
    upper = lax.broadcasted_iota(jnp.int32, (TILE, width), 0) // rhs
    blank = jnp.zeros((TILE, width), jnp.float32)

    def pair_product(pair):
        both = loads[pair // 2]
        turned = pltpu.roll(both, rhs, 0)
        mine = jnp.concatenate(
            [
                jnp.concatenate([jnp.where(upper == 0, both, turned), blank], axis=1),
                jnp.concatenate([blank, jnp.where(upper == 0, turned, both)], axis=1),
            ],
            axis=0,
        ).astype(jnp.bfloat16)
        blocks = jnp.concatenate(
            [
                jnp.concatenate([spline_ref[i, s] for s in range(splines)], axis=1)
                for i in (pair, pair + 1)
            ],
            axis=0,
        )
        return jnp.dot(mine, blocks, preferred_element_type=jnp.float32)

    pairs = range(0, block_count, 2)
    products = {pair: pair_product(pair) for pair in pairs[:-1]}
    copy.wait()
    products[pairs[-1]] = pair_product(pairs[-1])
    for pair, product in products.items():
        for i in (pair, pair + 1):
            total = product[(i - pair) * TILE : (i - pair + 1) * TILE]
            places, sums = [], []
            for s in range(splines):
                code = code_ref[i, s]
                place = code >> 1
                added = jnp.where(upper == (code & 1), total[:, s * width : (s + 1) * width], 0.0)
                places.append(place)
                sums.append(acc[place] + added)
            for place, value in zip(places, sums):
                acc[place] = value
    tiles = acc.shape[0] // 2
    size = pair_ref.shape[0] * pair_ref.shape[1] // TILE
    pair_ref[...] = acc[tiles : tiles + size].reshape(pair_ref.shape).astype(pair_ref.dtype)


def far_kernel(acc, far_ref):
    tiles, size = acc.shape[0] // 2, far_ref.shape[1] * far_ref.shape[2] // TILE
    for which in range(2):
        group = slice((which + 1) * tiles - size, (which + 1) * tiles)
        far_ref[which] = acc[group].reshape(far_ref.shape[1:]).astype(far_ref.dtype)


def split_kernel(acc, got_ref, *out_refs):
    size, struct_rows, _ = out_refs[0].shape
    height = struct_rows // TILE
    for step, out_ref in enumerate(out_refs):
        for place in range(size):
            index = step * size + place
            held = acc[index * height : (index + 1) * height].reshape(out_ref.shape[1:])
            out_ref[place] = (held + got_ref[index].astype(jnp.float32)).astype(out_ref.dtype)


def hand_kernel(held_ref, far_ref, keep_ref, given_ref):
    keep_ref[...] = held_ref[...] + far_ref[0].astype(jnp.float32)
    given_ref[...] = far_ref[1]


def gather_kernel(held_ref, *refs):
    got_refs, out_ref = refs[:-1], refs[-1]
    total = held_ref[...]
    for got_ref in got_refs:
        total = total + got_ref[...].astype(jnp.float32)
    out_ref[...] = total


def column_kernel(machs, held_ref, got_ref, *out_refs):
    for place in range(2):
        total = held_ref[place] + got_ref[place].astype(jnp.float32)
        for out_ref in out_refs[place * machs : (place + 1) * machs]:
            out_ref[...] = total.astype(out_ref.dtype)


def inverse_kernel(rhs, machs, *refs):
    other_refs, same_refs = refs[: 2 * machs : 2], refs[1 : 2 * machs : 2]
    inverse_ref, out_ref = refs[2 * machs :]
    parts = [
        same[...].astype(jnp.float32) + other[...].astype(jnp.float32)
        for same, other in zip(same_refs, other_refs)
    ]
    rounded = sum(parts[1:], parts[0]).astype(jnp.bfloat16)
    for g in range(rounded.shape[0] // PACK):
        out_ref[g * PACK : (g + 1) * PACK] = grouped_product(
            rhs, rounded[g * PACK : (g + 1) * PACK], lambda t: inverse_ref[t], g
        )


def mask_of(step):
    return 4 * step + (step >> 1) % 2


def swap(value, panels, apart):
    return lax.ppermute(value, "panel", [(i, i ^ apart) for i in range(panels)])


def mach_swap(value, machs, panels, turn, apart):
    pairs = [
        (mach * panels + i, (mach + turn) % machs * panels + (i ^ apart))
        for mach in range(machs)
        for i in range(panels)
    ]
    return lax.ppermute(value, ("mach", "panel"), pairs)


def cost(flops, size):
    return pl.CostEstimate(flops=flops, bytes_accessed=size, transcendentals=0)


def on_device(
    adjoint, near_blocks, pattern, trim_mask, spline_blocks, spline_owner, spline_local,
    struct_inverse,
):
    _, block_count, rhs, width = adjoint.shape
    entries = pattern.shape[1]
    panels, machs = lax.axis_size("panel"), lax.axis_size("mach")
    struct_count = struct_inverse.shape[0]
    rows, struct_rows = block_count * rhs, struct_count * rhs
    params = pltpu.CompilerParams(vmem_limit_bytes=16 * 1024 * 1024)
    f32, bf16 = jnp.float32, jnp.bfloat16
    own = adjoint.reshape(rows, width)
    beside = {0: 0, panels - 1: panels - 1}
    cross = lax.ppermute(
        own, ("mach", "panel"),
        [
            (
                mach * panels + i,
                (mach ^ (i in beside)) * panels + beside.get(i, i - 1 + 2 * (i % 2)),
            )
            for mach in range(machs)
            for i in range(panels)
        ],
    )
    mirror = swap(own, panels, panels // 2)
    pair = swap(own, panels, 1)
    expand = pl.pallas_call(
        functools.partial(spread_kernel, rhs),
        out_shape=jax.ShapeDtypeStruct((rows, block_count), bf16),
        out_specs=VMEM,
        compiler_params=params,
        cost_estimate=cost(8 * 10**9, 32 * 2**20),
        name="row_order",
    )()
    hot, gate, held, code = pl.pallas_call(
        functools.partial(pick_kernel, panels, rhs, struct_count),
        out_shape=(
            jax.ShapeDtypeStruct(((entries - 2) * rows, 4 * rows), bf16),
            jax.ShapeDtypeStruct((PACK, width), f32),
            jax.ShapeDtypeStruct((rows, width), bf16),
            jax.ShapeDtypeStruct(spline_owner.shape, jnp.int32),
        ),
        in_specs=[VMEM] * 6,
        out_specs=(VMEM,) * 4,
        compiler_params=params,
        cost_estimate=cost(10**6, 2**17),
        name="pick_rows",
    )(expand, pattern, trim_mask, own, spline_owner, spline_local)
    part = pl.pallas_call(
        functools.partial(near_kernel, rhs),
        out_shape=jax.ShapeDtypeStruct((rows, width), f32),
        in_specs=[VMEM] * 5,
        out_specs=VMEM,
        compiler_params=params,
        cost_estimate=cost(10**6, 2**17),
        name="near_field",
    )(hot, held, pair, cross, near_blocks[0])
    steps = panels // 4
    two = (2, struct_rows, width)
    sums, acc, send = pl.pallas_call(
        functools.partial(spline_kernel, rhs),
        out_shape=(
            jax.ShapeDtypeStruct((rows, width), f32),
            jax.ShapeDtypeStruct((panels * struct_rows // TILE, TILE, width), f32),
            jax.ShapeDtypeStruct((2 * (steps - 1), struct_rows, width), bf16),
        ),
        in_specs=[VMEM] * 7,
        out_specs=(VMEM,) * 3,
        scratch_shapes=[
            pltpu.SMEM(spline_owner.shape, jnp.int32),
            pltpu.SemaphoreType.DMA,
        ],
        compiler_params=params,
        cost_estimate=cost(10**6, 2**17),
        name="spline_loads",
    )(pair, mirror, code, part, gate, near_blocks[0], spline_blocks)
    far = pl.pallas_call(
        far_kernel,
        out_shape=jax.ShapeDtypeStruct((2, *two), bf16),
        in_specs=[VMEM],
        out_specs=VMEM,
        compiler_params=params,
        cost_estimate=cost(10**6, 2**17),
        name="far_loads",
    )(acc)
    loads = sums.reshape(adjoint.shape) * trim_mask[0].astype(f32)[None, None, :, None]
    got = swap(send, panels, 1)
    far = swap(far, panels, mask_of(steps - 1))
    keep, *sends = pl.pallas_call(
        split_kernel,
        out_shape=tuple(
            jax.ShapeDtypeStruct(two, f32 if step == 0 else bf16) for step in range(steps - 1)
        ),
        in_specs=[VMEM, VMEM],
        out_specs=(VMEM,) * (steps - 1),
        compiler_params=params,
        cost_estimate=cost(10**6, 2**17),
        name="pair_sum",
    )(acc, got)
    got = [swap(sends[step - 1], panels, mask_of(step)) for step in range(steps - 2, 0, -1)]
    keep, given = pl.pallas_call(
        hand_kernel,
        out_shape=(jax.ShapeDtypeStruct(two, f32), jax.ShapeDtypeStruct(two, bf16)),
        in_specs=[VMEM, VMEM],
        out_specs=(VMEM, VMEM),
        compiler_params=params,
        cost_estimate=cost(10**6, 2**17),
        name="hand_over",
    )(keep, far)
    given = swap(given, panels, 1)
    keep = pl.pallas_call(
        gather_kernel,
        out_shape=jax.ShapeDtypeStruct(two, f32),
        in_specs=[VMEM] * (steps - 1),
        out_specs=VMEM,
        compiler_params=params,
        cost_estimate=cost(4 * 10**9, 16 * 2**20),
        name="far_sum",
    )(keep, *got)
    one = jax.ShapeDtypeStruct((struct_rows, width), f32)
    columns = pl.pallas_call(
        functools.partial(column_kernel, machs),
        out_shape=(one,) * (2 * machs),
        in_specs=[VMEM] * 2,
        out_specs=(VMEM,) * (2 * machs),
        compiler_params=params,
        cost_estimate=cost(10**6, 2**17),
        name="column_sum",
    )(keep, given)
    sames = [
        mach_swap(columns[turn], machs, panels, turn, 0) if turn else columns[0]
        for turn in range(machs)
    ]
    others = [mach_swap(columns[machs + turn], machs, panels, turn, 3) for turn in range(machs)]
    struct_adjoint = pl.pallas_call(
        functools.partial(inverse_kernel, rhs, machs),
        out_shape=jax.ShapeDtypeStruct((struct_rows, width), f32),
        in_specs=[VMEM] * (2 * machs + 1),
        out_specs=VMEM,
        compiler_params=params,
        cost_estimate=cost(10**6, 2**17),
        name="struct_solve",
    )(
        *(value for turn in range(machs - 1, -1, -1) for value in (others[turn], sames[turn])),
        struct_inverse,
    )
    return (
        loads,
        struct_adjoint.reshape(struct_count, rhs, width),
    )


def solution(mesh):
    in_specs = (
        P("mach", "panel", None, None),
        P("mach", "panel", None, None, None),
        P("panel", None),
        P("mach", None),
        P("panel", None, None, None),
        P("panel", None),
        P("panel", None),
        P("panel", None, None),
    )
    out_specs = (P("mach", "panel", None, None), P("panel", None, None))
    return jax.shard_map(
        on_device, mesh=mesh, in_specs=in_specs, out_specs=out_specs, check_vma=False
    )
```

```python
import functools

import jax
import jax.numpy as jnp
from jax import lax
from jax.experimental import pallas as pl
from jax.experimental.pallas import tpu as pltpu
from jax.sharding import PartitionSpec as P

SMEM = pl.BlockSpec(memory_space=pltpu.SMEM)
VMEM = pl.BlockSpec(memory_space=pltpu.VMEM)
PACK = 16
TILE = 8


def device_class(index):
    return (index ^ (index >> 1) ^ (index >> 3)) & 1


def spread_kernel(rhs, expand_ref):
    shape = expand_ref.shape
    expand_ref[...] = (
        lax.broadcasted_iota(jnp.int32, shape, 0) // rhs == lax.broadcasted_iota(jnp.int32, shape, 1)
    ).astype(jnp.bfloat16)


def pick_kernel(
    panels, rhs, struct_count, expand_ref, pattern_ref, trim_ref, own_ref, owner_ref, local_ref,
    hot_ref, gate_ref, held_ref, code_ref,
):
    block_count, entries = pattern_ref.shape
    rows = own_ref.shape[0]
    here = lax.axis_index("panel")
    shape = (rows, hot_ref.shape[1])
    offset = lax.broadcasted_iota(jnp.int32, shape, 1) - (
        lax.broadcasted_iota(jnp.int32, shape, 0) % rhs
    )
    block = pattern_ref[...]
    apart = (block // block_count) ^ here
    slot = jnp.where(apart == 0, 0, jnp.where(apart == 1, 1, 2))
    first = (slot * block_count + block % block_count) * rhs
    first = jnp.dot(
        expand_ref[...],
        first.astype(jnp.float32).astype(jnp.bfloat16),
        preferred_element_type=jnp.float32,
    ).astype(jnp.int32)
    for k in range(2, entries):
        hot_ref[(k - 2) * rows : (k - 1) * rows] = (offset == first[:, k : k + 1]).astype(
            jnp.bfloat16
        )
    shape = (gate_ref.shape[0], rhs)
    mine = lax.broadcasted_iota(jnp.int32, shape, 0) % rhs == lax.broadcasted_iota(
        jnp.int32, shape, 1
    )
    gate = jnp.sum(jnp.where(mine, trim_ref[...], 0).astype(jnp.float32), axis=1, keepdims=True)
    gate_ref[...] = jnp.broadcast_to(gate, gate_ref.shape)
    held_ref[...] = own_ref[...]
    owner = owner_ref[...]
    code_ref[...] = (
        (device_class(owner) ^ device_class(here)) * (panels // 2) + ((owner ^ here) >> 1)
    ) * struct_count + local_ref[...]


def grouped_product(rhs, left, blocks_of, group):
    per_group = PACK // rhs
    every = jnp.concatenate([blocks_of(group * per_group + j) for j in range(per_group)], axis=1)
    product = jnp.dot(left, every, preferred_element_type=jnp.float32)
    width = product.shape[1] // per_group
    row = lax.broadcasted_iota(jnp.int32, (PACK, width), 0)
    out = product[:, :width]
    for j in range(1, per_group):
        out = jnp.where(row // rhs == j, product[:, j * width : (j + 1) * width], out)
    return out


def near_kernel(rhs, hot_ref, own_ref, pair_ref, cross_ref, near_ref, part_ref):
    rows, width = own_ref.shape
    others = hot_ref.shape[0] // rows
    own = own_ref[...]
    pool = jnp.concatenate([own, pair_ref[...], cross_ref[...], own], axis=0)
    picked = jnp.dot(hot_ref[...], pool, preferred_element_type=jnp.float32)
    picked = picked.astype(jnp.bfloat16)
    for g in range(rows // PACK):
        left = [own[g * PACK : (g + 1) * PACK]] + [
            picked[k * rows + g * PACK : k * rows + (g + 1) * PACK] for k in range(others)
        ]
        part_ref[g * PACK : (g + 1) * PACK] = grouped_product(
            rhs,
            jnp.concatenate(left, axis=1),
            lambda i: jnp.concatenate(
                [near_ref[i, 0], near_ref[i, 2:].reshape(others * width, width)], axis=0
            ),
            g,
        )


def spline_kernel(
    rhs, _, mirror_ref, code_vmem, part_ref, gate_ref, near_ref, spline_ref,
    sums_ref, acc, pair_ref, code_ref, sem,
):
    copy = pltpu.make_async_copy(code_vmem, code_ref, sem)
    copy.start()
    block_count, splines = code_ref.shape
    rows, width = part_ref.shape
    loads = []
    for g in range(rows // PACK):
        group = slice(g * PACK, (g + 1) * PACK)
        sums = part_ref[group] + grouped_product(
            rhs, mirror_ref[group], lambda i: near_ref[i, 1], g
        )
        sums_ref[group] = sums
        gated = gate_ref[...] * sums
        loads += [gated[row : row + TILE] for row in range(0, PACK, TILE)]
    acc[...] = jnp.zeros(acc.shape, jnp.float32)
    upper = lax.broadcasted_iota(jnp.int32, (TILE, width), 0) // rhs
    blank = jnp.zeros((TILE, width), jnp.float32)

    def pair_product(pair):
        both = loads[pair // 2]
        turned = pltpu.roll(both, rhs, 0)
        mine = jnp.concatenate(
            [
                jnp.concatenate([jnp.where(upper == 0, both, turned), blank], axis=1),
                jnp.concatenate([blank, jnp.where(upper == 0, turned, both)], axis=1),
            ],
            axis=0,
        ).astype(jnp.bfloat16)
        blocks = jnp.concatenate(
            [
                jnp.concatenate([spline_ref[i, s] for s in range(splines)], axis=1)
                for i in (pair, pair + 1)
            ],
            axis=0,
        )
        return jnp.dot(mine, blocks, preferred_element_type=jnp.float32)

    pairs = range(0, block_count, 2)
    products = {pair: pair_product(pair) for pair in pairs[:-1]}
    copy.wait()
    products[pairs[-1]] = pair_product(pairs[-1])
    for pair, product in products.items():
        for i in (pair, pair + 1):
            total = product[(i - pair) * TILE : (i - pair + 1) * TILE]
            places, sums = [], []
            for s in range(splines):
                code = code_ref[i, s]
                place = code >> 1
                added = jnp.where(upper == (code & 1), total[:, s * width : (s + 1) * width], 0.0)
                places.append(place)
                sums.append(acc[place] + added)
            for place, value in zip(places, sums):
                acc[place] = value
    tiles = acc.shape[0] // 2
    size = pair_ref.shape[0] * pair_ref.shape[1] // TILE
    pair_ref[...] = acc[tiles : tiles + size].reshape(pair_ref.shape).astype(pair_ref.dtype)


def far_kernel(acc, far_ref):
    tiles, size = acc.shape[0] // 2, far_ref.shape[1] * far_ref.shape[2] // TILE
    for which in range(2):
        group = slice((which + 1) * tiles - size, (which + 1) * tiles)
        far_ref[which] = acc[group].reshape(far_ref.shape[1:]).astype(far_ref.dtype)


def split_kernel(acc, got_ref, *out_refs):
    size, struct_rows, _ = out_refs[0].shape
    height = struct_rows // TILE
    for step, out_ref in enumerate(out_refs):
        for place in range(size):
            index = step * size + place
            held = acc[index * height : (index + 1) * height].reshape(out_ref.shape[1:])
            out_ref[place] = (held + got_ref[index].astype(jnp.float32)).astype(out_ref.dtype)


def hand_kernel(held_ref, far_ref, keep_ref, given_ref):
    keep_ref[...] = held_ref[...] + far_ref[0].astype(jnp.float32)
    given_ref[...] = far_ref[1]


def gather_kernel(held_ref, *refs):
    got_refs, out_ref = refs[:-1], refs[-1]
    total = held_ref[...]
    for got_ref in got_refs:
        total = total + got_ref[...].astype(jnp.float32)
    out_ref[...] = total


def column_kernel(machs, held_ref, got_ref, *out_refs):
    for place in range(2):
        total = held_ref[place] + got_ref[place].astype(jnp.float32)
        for out_ref in out_refs[place * machs : (place + 1) * machs]:
            out_ref[...] = total.astype(out_ref.dtype)


def inverse_kernel(rhs, machs, *refs):
    other_refs, same_refs = refs[: 2 * machs : 2], refs[1 : 2 * machs : 2]
    inverse_ref, out_ref = refs[2 * machs :]
    parts = [
        same[...].astype(jnp.float32) + other[...].astype(jnp.float32)
        for same, other in zip(same_refs, other_refs)
    ]
    rounded = sum(parts[1:], parts[0]).astype(jnp.bfloat16)
    for g in range(rounded.shape[0] // PACK):
        out_ref[g * PACK : (g + 1) * PACK] = grouped_product(
            rhs, rounded[g * PACK : (g + 1) * PACK], lambda t: inverse_ref[t], g
        )


def mask_of(step):
    return 4 * step + (step >> 1) % 2


def swap(value, panels, apart):
    return lax.ppermute(value, "panel", [(i, i ^ apart) for i in range(panels)])


def mach_swap(value, machs, panels, turn, apart):
    pairs = [
        (mach * panels + i, (mach + turn) % machs * panels + (i ^ apart))
        for mach in range(machs)
        for i in range(panels)
    ]
    return lax.ppermute(value, ("mach", "panel"), pairs)


def cost(flops, size):
    return pl.CostEstimate(flops=flops, bytes_accessed=size, transcendentals=0)


def on_device(
    adjoint, near_blocks, pattern, trim_mask, spline_blocks, spline_owner, spline_local,
    struct_inverse,
):
    _, block_count, rhs, width = adjoint.shape
    entries = pattern.shape[1]
    panels, machs = lax.axis_size("panel"), lax.axis_size("mach")
    struct_count = struct_inverse.shape[0]
    rows, struct_rows = block_count * rhs, struct_count * rhs
    params = pltpu.CompilerParams(vmem_limit_bytes=16 * 1024 * 1024)
    f32, bf16 = jnp.float32, jnp.bfloat16
    own = adjoint.reshape(rows, width)
    beside = {0: 0, panels - 1: panels - 1}
    cross = lax.ppermute(
        own, ("mach", "panel"),
        [
            (
                mach * panels + i,
                (mach ^ (i in beside)) * panels + beside.get(i, i - 1 + 2 * (i % 2)),
            )
            for mach in range(machs)
            for i in range(panels)
        ],
    )
    mirror = swap(own, panels, panels // 2)
    pair = swap(own, panels, 1)
    expand = pl.pallas_call(
        functools.partial(spread_kernel, rhs),
        out_shape=jax.ShapeDtypeStruct((rows, block_count), bf16),
        out_specs=VMEM,
        compiler_params=params,
        cost_estimate=cost(8 * 10**9, 32 * 2**20),
        name="row_order",
    )()
    hot, gate, held, code = pl.pallas_call(
        functools.partial(pick_kernel, panels, rhs, struct_count),
        out_shape=(
            jax.ShapeDtypeStruct(((entries - 2) * rows, 4 * rows), bf16),
            jax.ShapeDtypeStruct((PACK, width), f32),
            jax.ShapeDtypeStruct((rows, width), bf16),
            jax.ShapeDtypeStruct(spline_owner.shape, jnp.int32),
        ),
        in_specs=[VMEM] * 6,
        out_specs=(VMEM,) * 4,
        compiler_params=params,
        cost_estimate=cost(10**6, 2**17),
        name="pick_rows",
    )(expand, pattern, trim_mask, own, spline_owner, spline_local)
    part = pl.pallas_call(
        functools.partial(near_kernel, rhs),
        out_shape=jax.ShapeDtypeStruct((rows, width), f32),
        in_specs=[VMEM] * 5,
        out_specs=VMEM,
        compiler_params=params,
        cost_estimate=cost(10**6, 2**17),
        name="near_field",
    )(hot, held, pair, cross, near_blocks[0])
    steps = panels // 4
    two = (2, struct_rows, width)
    sums, acc, send = pl.pallas_call(
        functools.partial(spline_kernel, rhs),
        out_shape=(
            jax.ShapeDtypeStruct((rows, width), f32),
            jax.ShapeDtypeStruct((panels * struct_rows // TILE, TILE, width), f32),
            jax.ShapeDtypeStruct((2 * (steps - 1), struct_rows, width), bf16),
        ),
        in_specs=[VMEM] * 7,
        out_specs=(VMEM,) * 3,
        scratch_shapes=[
            pltpu.SMEM(spline_owner.shape, jnp.int32),
            pltpu.SemaphoreType.DMA,
        ],
        compiler_params=params,
        cost_estimate=cost(10**6, 2**17),
        name="spline_loads",
    )(cross, mirror, code, part, gate, near_blocks[0], spline_blocks)
    far = pl.pallas_call(
        far_kernel,
        out_shape=jax.ShapeDtypeStruct((2, *two), bf16),
        in_specs=[VMEM],
        out_specs=VMEM,
        compiler_params=params,
        cost_estimate=cost(10**6, 2**17),
        name="far_loads",
    )(acc)
    loads = sums.reshape(adjoint.shape) * trim_mask[0].astype(f32)[None, None, :, None]
    got = swap(send, panels, 1)
    far = swap(far, panels, mask_of(steps - 1))
    keep, *sends = pl.pallas_call(
        split_kernel,
        out_shape=tuple(
            jax.ShapeDtypeStruct(two, f32 if step == 0 else bf16) for step in range(steps - 1)
        ),
        in_specs=[VMEM, VMEM],
        out_specs=(VMEM,) * (steps - 1),
        compiler_params=params,
        cost_estimate=cost(10**6, 2**17),
        name="pair_sum",
    )(acc, got)
    got = [swap(sends[step - 1], panels, mask_of(step)) for step in range(steps - 2, 0, -1)]
    keep, given = pl.pallas_call(
        hand_kernel,
        out_shape=(jax.ShapeDtypeStruct(two, f32), jax.ShapeDtypeStruct(two, bf16)),
        in_specs=[VMEM, VMEM],
        out_specs=(VMEM, VMEM),
        compiler_params=params,
        cost_estimate=cost(10**6, 2**17),
        name="hand_over",
    )(keep, far)
    given = swap(given, panels, 1)
    keep = pl.pallas_call(
        gather_kernel,
        out_shape=jax.ShapeDtypeStruct(two, f32),
        in_specs=[VMEM] * (steps - 1),
        out_specs=VMEM,
        compiler_params=params,
        cost_estimate=cost(4 * 10**9, 16 * 2**20),
        name="far_sum",
    )(keep, *got)
    one = jax.ShapeDtypeStruct((struct_rows, width), f32)
    columns = pl.pallas_call(
        functools.partial(column_kernel, machs),
        out_shape=(one,) * (2 * machs),
        in_specs=[VMEM] * 2,
        out_specs=(VMEM,) * (2 * machs),
        compiler_params=params,
        cost_estimate=cost(10**6, 2**17),
        name="column_sum",
    )(keep, given)
    sames = [
        mach_swap(columns[turn], machs, panels, turn, 0) if turn else columns[0]
        for turn in range(machs)
    ]
    others = [mach_swap(columns[machs + turn], machs, panels, turn, 3) for turn in range(machs)]
    struct_adjoint = pl.pallas_call(
        functools.partial(inverse_kernel, rhs, machs),
        out_shape=jax.ShapeDtypeStruct((struct_rows, width), f32),
        in_specs=[VMEM] * (2 * machs + 1),
        out_specs=VMEM,
        compiler_params=params,
        cost_estimate=cost(10**6, 2**17),
        name="struct_solve",
    )(
        *(value for turn in range(machs - 1, -1, -1) for value in (others[turn], sames[turn])),
        struct_inverse,
    )
    return (
        loads,
        struct_adjoint.reshape(struct_count, rhs, width),
    )


def solution(mesh):
    in_specs = (
        P("mach", "panel", None, None),
        P("mach", "panel", None, None, None),
        P("panel", None),
        P("mach", None),
        P("panel", None, None, None),
        P("panel", None),
        P("panel", None),
        P("panel", None, None),
    )
    out_specs = (P("mach", "panel", None, None), P("panel", None, None))
    return jax.shard_map(
        on_device, mesh=mesh, in_specs=in_specs, out_specs=out_specs, check_vma=False
    )
```

```python
import functools

import jax
import jax.numpy as jnp
from jax import lax
from jax.experimental import pallas as pl
from jax.experimental.pallas import tpu as pltpu
from jax.sharding import PartitionSpec as P

SMEM = pl.BlockSpec(memory_space=pltpu.SMEM)
VMEM = pl.BlockSpec(memory_space=pltpu.VMEM)
PACK = 16
TILE = 8


def device_class(index):
    return (index ^ (index >> 1) ^ (index >> 3)) & 1


def spread_kernel(rhs, expand_ref):
    shape = expand_ref.shape
    expand_ref[...] = (
        lax.broadcasted_iota(jnp.int32, shape, 0) // rhs == lax.broadcasted_iota(jnp.int32, shape, 1)
    ).astype(jnp.bfloat16)


def pick_kernel(
    panels, rhs, struct_count, expand_ref, pattern_ref, trim_ref, own_ref, owner_ref, local_ref,
    hot_ref, gate_ref, held_ref, code_ref,
):
    block_count, entries = pattern_ref.shape
    rows = own_ref.shape[0]
    here = lax.axis_index("panel")
    shape = (rows, hot_ref.shape[1])
    offset = lax.broadcasted_iota(jnp.int32, shape, 1) - (
        lax.broadcasted_iota(jnp.int32, shape, 0) % rhs
    )
    block = pattern_ref[...]
    apart = (block // block_count) ^ here
    slot = jnp.where(apart == 0, 0, jnp.where(apart == 1, 1, 2))
    first = (slot * block_count + block % block_count) * rhs
    first = jnp.dot(
        expand_ref[...],
        first.astype(jnp.float32).astype(jnp.bfloat16),
        preferred_element_type=jnp.float32,
    ).astype(jnp.int32)
    for k in range(2, entries):
        hot_ref[(k - 2) * rows : (k - 1) * rows] = (offset == first[:, k : k + 1]).astype(
            jnp.bfloat16
        )
    shape = (gate_ref.shape[0], rhs)
    mine = lax.broadcasted_iota(jnp.int32, shape, 0) % rhs == lax.broadcasted_iota(
        jnp.int32, shape, 1
    )
    gate = jnp.sum(jnp.where(mine, trim_ref[...], 0).astype(jnp.float32), axis=1, keepdims=True)
    gate_ref[...] = jnp.broadcast_to(gate, gate_ref.shape)
    held_ref[...] = own_ref[...]
    owner = owner_ref[...]
    code_ref[...] = (
        (device_class(owner) ^ device_class(here)) * (panels // 2) + ((owner ^ here) >> 1)
    ) * struct_count + local_ref[...]


def grouped_product(rhs, left, blocks_of, group):
    per_group = PACK // rhs
    every = jnp.concatenate([blocks_of(group * per_group + j) for j in range(per_group)], axis=1)
    product = jnp.dot(left, every, preferred_element_type=jnp.float32)
    width = product.shape[1] // per_group
    row = lax.broadcasted_iota(jnp.int32, (PACK, width), 0)
    out = product[:, :width]
    for j in range(1, per_group):
        out = jnp.where(row // rhs == j, product[:, j * width : (j + 1) * width], out)
    return out


def near_kernel(rhs, hot_ref, own_ref, pair_ref, cross_ref, near_ref, part_ref):
    rows, width = own_ref.shape
    others = hot_ref.shape[0] // rows
    own = own_ref[...]
    pool = jnp.concatenate([own, pair_ref[...], cross_ref[...], own], axis=0)
    picked = jnp.dot(hot_ref[...], pool, preferred_element_type=jnp.float32)
    picked = picked.astype(jnp.bfloat16)
    for g in range(rows // PACK):
        left = [own[g * PACK : (g + 1) * PACK]] + [
            picked[k * rows + g * PACK : k * rows + (g + 1) * PACK] for k in range(others)
        ]
        part_ref[g * PACK : (g + 1) * PACK] = grouped_product(
            rhs,
            jnp.concatenate(left, axis=1),
            lambda i: jnp.concatenate(
                [near_ref[i, 0], near_ref[i, 2:].reshape(others * width, width)], axis=0
            ),
            g,
        )


def spline_kernel(
    rhs, _, mirror_ref, code_vmem, part_ref, gate_ref, near_ref, spline_ref,
    sums_ref, acc, pair_ref, code_ref, sem,
):
    copy = pltpu.make_async_copy(code_vmem, code_ref, sem)
    copy.start()
    block_count, splines = code_ref.shape
    rows, width = part_ref.shape
    loads = []
    for g in range(rows // PACK):
        group = slice(g * PACK, (g + 1) * PACK)
        sums = part_ref[group] + grouped_product(
            rhs, mirror_ref[group], lambda i: near_ref[i, 1], g
        )
        sums_ref[group] = sums
        gated = gate_ref[...] * sums
        loads += [gated[row : row + TILE] for row in range(0, PACK, TILE)]
    acc[...] = jnp.zeros(acc.shape, jnp.float32)
    upper = lax.broadcasted_iota(jnp.int32, (TILE, width), 0) // rhs
    blank = jnp.zeros((TILE, width), jnp.float32)

    def pair_product(pair):
        both = loads[pair // 2]
        turned = pltpu.roll(both, rhs, 0)
        mine = jnp.concatenate(
            [
                jnp.concatenate([jnp.where(upper == 0, both, turned), blank], axis=1),
                jnp.concatenate([blank, jnp.where(upper == 0, turned, both)], axis=1),
            ],
            axis=0,
        ).astype(jnp.bfloat16)
        blocks = jnp.concatenate(
            [
                jnp.concatenate([spline_ref[i, s] for s in range(splines)], axis=1)
                for i in (pair, pair + 1)
            ],
            axis=0,
        )
        return jnp.dot(mine, blocks, preferred_element_type=jnp.float32)

    pairs = range(0, block_count, 2)
    ready = len(pairs) // 2
    products = {pair: pair_product(pair) for pair in pairs[:ready]}
    copy.wait()
    for pair in pairs:
        product = products[pair] if pair in products else pair_product(pair)
        for i in (pair, pair + 1):
            total = product[(i - pair) * TILE : (i - pair + 1) * TILE]
            places, sums = [], []
            for s in range(splines):
                code = code_ref[i, s]
                place = code >> 1
                added = jnp.where(upper == (code & 1), total[:, s * width : (s + 1) * width], 0.0)
                places.append(place)
                sums.append(acc[place] + added)
            for place, value in zip(places, sums):
                acc[place] = value
    tiles = acc.shape[0] // 2
    size = pair_ref.shape[0] * pair_ref.shape[1] // TILE
    pair_ref[...] = acc[tiles : tiles + size].reshape(pair_ref.shape).astype(pair_ref.dtype)


def far_kernel(acc, far_ref):
    tiles, size = acc.shape[0] // 2, far_ref.shape[1] * far_ref.shape[2] // TILE
    for which in range(2):
        group = slice((which + 1) * tiles - size, (which + 1) * tiles)
        far_ref[which] = acc[group].reshape(far_ref.shape[1:]).astype(far_ref.dtype)


def split_kernel(acc, got_ref, *out_refs):
    size, struct_rows, _ = out_refs[0].shape
    height = struct_rows // TILE
    for step, out_ref in enumerate(out_refs):
        for place in range(size):
            index = step * size + place
            held = acc[index * height : (index + 1) * height].reshape(out_ref.shape[1:])
            out_ref[place] = (held + got_ref[index].astype(jnp.float32)).astype(out_ref.dtype)


def hand_kernel(held_ref, far_ref, keep_ref, given_ref):
    keep_ref[...] = held_ref[...] + far_ref[0].astype(jnp.float32)
    given_ref[...] = far_ref[1]


def gather_kernel(held_ref, *refs):
    got_refs, out_ref = refs[:-1], refs[-1]
    total = held_ref[...]
    for got_ref in got_refs:
        total = total + got_ref[...].astype(jnp.float32)
    out_ref[...] = total


def column_kernel(machs, held_ref, got_ref, *out_refs):
    for place in range(2):
        total = held_ref[place] + got_ref[place].astype(jnp.float32)
        for out_ref in out_refs[place * machs : (place + 1) * machs]:
            out_ref[...] = total.astype(out_ref.dtype)


def inverse_kernel(rhs, machs, *refs):
    other_refs, same_refs = refs[: 2 * machs : 2], refs[1 : 2 * machs : 2]
    inverse_ref, out_ref = refs[2 * machs :]
    parts = [
        same[...].astype(jnp.float32) + other[...].astype(jnp.float32)
        for same, other in zip(same_refs, other_refs)
    ]
    rounded = sum(parts[1:], parts[0]).astype(jnp.bfloat16)
    for g in range(rounded.shape[0] // PACK):
        out_ref[g * PACK : (g + 1) * PACK] = grouped_product(
            rhs, rounded[g * PACK : (g + 1) * PACK], lambda t: inverse_ref[t], g
        )


def mask_of(step):
    return 4 * step + (step >> 1) % 2


def swap(value, panels, apart):
    return lax.ppermute(value, "panel", [(i, i ^ apart) for i in range(panels)])


def mach_swap(value, machs, panels, turn, apart):
    pairs = [
        (mach * panels + i, (mach + turn) % machs * panels + (i ^ apart))
        for mach in range(machs)
        for i in range(panels)
    ]
    return lax.ppermute(value, ("mach", "panel"), pairs)


def cost(flops, size):
    return pl.CostEstimate(flops=flops, bytes_accessed=size, transcendentals=0)


def on_device(
    adjoint, near_blocks, pattern, trim_mask, spline_blocks, spline_owner, spline_local,
    struct_inverse,
):
    _, block_count, rhs, width = adjoint.shape
    entries = pattern.shape[1]
    panels, machs = lax.axis_size("panel"), lax.axis_size("mach")
    struct_count = struct_inverse.shape[0]
    rows, struct_rows = block_count * rhs, struct_count * rhs
    params = pltpu.CompilerParams(vmem_limit_bytes=16 * 1024 * 1024)
    f32, bf16 = jnp.float32, jnp.bfloat16
    own = adjoint.reshape(rows, width)
    beside = {0: 0, panels - 1: panels - 1}
    cross = lax.ppermute(
        own, ("mach", "panel"),
        [
            (
                mach * panels + i,
                (mach ^ (i in beside)) * panels + beside.get(i, i - 1 + 2 * (i % 2)),
            )
            for mach in range(machs)
            for i in range(panels)
        ],
    )
    mirror = swap(own, panels, panels // 2)
    pair = swap(own, panels, 1)
    expand = pl.pallas_call(
        functools.partial(spread_kernel, rhs),
        out_shape=jax.ShapeDtypeStruct((rows, block_count), bf16),
        out_specs=VMEM,
        compiler_params=params,
        cost_estimate=cost(8 * 10**9, 32 * 2**20),
        name="row_order",
    )()
    hot, gate, held, code = pl.pallas_call(
        functools.partial(pick_kernel, panels, rhs, struct_count),
        out_shape=(
            jax.ShapeDtypeStruct(((entries - 2) * rows, 4 * rows), bf16),
            jax.ShapeDtypeStruct((PACK, width), f32),
            jax.ShapeDtypeStruct((rows, width), bf16),
            jax.ShapeDtypeStruct(spline_owner.shape, jnp.int32),
        ),
        in_specs=[VMEM] * 6,
        out_specs=(VMEM,) * 4,
        compiler_params=params,
        cost_estimate=cost(10**6, 2**17),
        name="pick_rows",
    )(expand, pattern, trim_mask, own, spline_owner, spline_local)
    part = pl.pallas_call(
        functools.partial(near_kernel, rhs),
        out_shape=jax.ShapeDtypeStruct((rows, width), f32),
        in_specs=[VMEM] * 5,
        out_specs=VMEM,
        compiler_params=params,
        cost_estimate=cost(10**6, 2**17),
        name="near_field",
    )(hot, held, pair, cross, near_blocks[0])
    steps = panels // 4
    two = (2, struct_rows, width)
    sums, acc, send = pl.pallas_call(
        functools.partial(spline_kernel, rhs),
        out_shape=(
            jax.ShapeDtypeStruct((rows, width), f32),
            jax.ShapeDtypeStruct((panels * struct_rows // TILE, TILE, width), f32),
            jax.ShapeDtypeStruct((2 * (steps - 1), struct_rows, width), bf16),
        ),
        in_specs=[VMEM] * 7,
        out_specs=(VMEM,) * 3,
        scratch_shapes=[
            pltpu.SMEM(spline_owner.shape, jnp.int32),
            pltpu.SemaphoreType.DMA,
        ],
        compiler_params=params,
        cost_estimate=cost(10**6, 2**17),
        name="spline_loads",
    )(cross, mirror, code, part, gate, near_blocks[0], spline_blocks)
    far = pl.pallas_call(
        far_kernel,
        out_shape=jax.ShapeDtypeStruct((2, *two), bf16),
        in_specs=[VMEM],
        out_specs=VMEM,
        compiler_params=params,
        cost_estimate=cost(10**6, 2**17),
        name="far_loads",
    )(acc)
    loads = sums.reshape(adjoint.shape) * trim_mask[0].astype(f32)[None, None, :, None]
    got = swap(send, panels, 1)
    far = swap(far, panels, mask_of(steps - 1))
    keep, *sends = pl.pallas_call(
        split_kernel,
        out_shape=tuple(
            jax.ShapeDtypeStruct(two, f32 if step == 0 else bf16) for step in range(steps - 1)
        ),
        in_specs=[VMEM, VMEM],
        out_specs=(VMEM,) * (steps - 1),
        compiler_params=params,
        cost_estimate=cost(10**6, 2**17),
        name="pair_sum",
    )(acc, got)
    got = [swap(sends[step - 1], panels, mask_of(step)) for step in range(steps - 2, 0, -1)]
    keep, given = pl.pallas_call(
        hand_kernel,
        out_shape=(jax.ShapeDtypeStruct(two, f32), jax.ShapeDtypeStruct(two, bf16)),
        in_specs=[VMEM, VMEM],
        out_specs=(VMEM, VMEM),
        compiler_params=params,
        cost_estimate=cost(10**6, 2**17),
        name="hand_over",
    )(keep, far)
    given = swap(given, panels, 1)
    keep = pl.pallas_call(
        gather_kernel,
        out_shape=jax.ShapeDtypeStruct(two, f32),
        in_specs=[VMEM] * (steps - 1),
        out_specs=VMEM,
        compiler_params=params,
        cost_estimate=cost(4 * 10**9, 16 * 2**20),
        name="far_sum",
    )(keep, *got)
    one = jax.ShapeDtypeStruct((struct_rows, width), f32)
    columns = pl.pallas_call(
        functools.partial(column_kernel, machs),
        out_shape=(one,) * (2 * machs),
        in_specs=[VMEM] * 2,
        out_specs=(VMEM,) * (2 * machs),
        compiler_params=params,
        cost_estimate=cost(10**6, 2**17),
        name="column_sum",
    )(keep, given)
    sames = [
        mach_swap(columns[turn], machs, panels, turn, 0) if turn else columns[0]
        for turn in range(machs)
    ]
    others = [mach_swap(columns[machs + turn], machs, panels, turn, 3) for turn in range(machs)]
    struct_adjoint = pl.pallas_call(
        functools.partial(inverse_kernel, rhs, machs),
        out_shape=jax.ShapeDtypeStruct((struct_rows, width), f32),
        in_specs=[VMEM] * (2 * machs + 1),
        out_specs=VMEM,
        compiler_params=params,
        cost_estimate=cost(10**6, 2**17),
        name="struct_solve",
    )(
        *(value for turn in range(machs - 1, -1, -1) for value in (others[turn], sames[turn])),
        struct_inverse,
    )
    return (
        loads,
        struct_adjoint.reshape(struct_count, rhs, width),
    )


def solution(mesh):
    in_specs = (
        P("mach", "panel", None, None),
        P("mach", "panel", None, None, None),
        P("panel", None),
        P("mach", None),
        P("panel", None, None, None),
        P("panel", None),
        P("panel", None),
        P("panel", None, None),
    )
    out_specs = (P("mach", "panel", None, None), P("panel", None, None))
    return jax.shard_map(
        on_device, mesh=mesh, in_specs=in_specs, out_specs=out_specs, check_vma=False
    )
```

```python
import functools

import jax
import jax.numpy as jnp
from jax import lax
from jax.experimental import pallas as pl
from jax.experimental.pallas import tpu as pltpu
from jax.sharding import PartitionSpec as P

SMEM = pl.BlockSpec(memory_space=pltpu.SMEM)
VMEM = pl.BlockSpec(memory_space=pltpu.VMEM)
PACK = 16
TILE = 8


def device_class(index):
    return (index ^ (index >> 1) ^ (index >> 3)) & 1


def spread_kernel(rhs, expand_ref):
    shape = expand_ref.shape
    expand_ref[...] = (
        lax.broadcasted_iota(jnp.int32, shape, 0) // rhs == lax.broadcasted_iota(jnp.int32, shape, 1)
    ).astype(jnp.bfloat16)


def pick_kernel(
    panels, rhs, struct_count, expand_ref, pattern_ref, trim_ref, own_ref, owner_ref, local_ref,
    hot_ref, gate_ref, held_ref, code_ref,
):
    block_count, entries = pattern_ref.shape
    rows = own_ref.shape[0]
    here = lax.axis_index("panel")
    shape = (rows, hot_ref.shape[1])
    offset = lax.broadcasted_iota(jnp.int32, shape, 1) - (
        lax.broadcasted_iota(jnp.int32, shape, 0) % rhs
    )
    block = pattern_ref[...]
    apart = (block // block_count) ^ here
    slot = jnp.where(apart == 0, 0, jnp.where(apart == 1, 1, 2))
    first = (slot * block_count + block % block_count) * rhs
    first = jnp.dot(
        expand_ref[...],
        first.astype(jnp.float32).astype(jnp.bfloat16),
        preferred_element_type=jnp.float32,
    ).astype(jnp.int32)
    for k in range(2, entries):
        hot_ref[(k - 2) * rows : (k - 1) * rows] = (offset == first[:, k : k + 1]).astype(
            jnp.bfloat16
        )
    shape = (gate_ref.shape[0], rhs)
    mine = lax.broadcasted_iota(jnp.int32, shape, 0) % rhs == lax.broadcasted_iota(
        jnp.int32, shape, 1
    )
    gate = jnp.sum(jnp.where(mine, trim_ref[...], 0).astype(jnp.float32), axis=1, keepdims=True)
    gate_ref[...] = jnp.broadcast_to(gate, gate_ref.shape)
    held_ref[...] = own_ref[...]
    owner = owner_ref[...]
    code_ref[...] = (
        (device_class(owner) ^ device_class(here)) * (panels // 2) + ((owner ^ here) >> 1)
    ) * struct_count + local_ref[...]


def grouped_product(rhs, left, blocks_of, group):
    per_group = PACK // rhs
    every = jnp.concatenate([blocks_of(group * per_group + j) for j in range(per_group)], axis=1)
    product = jnp.dot(left, every, preferred_element_type=jnp.float32)
    width = product.shape[1] // per_group
    row = lax.broadcasted_iota(jnp.int32, (PACK, width), 0)
    out = product[:, :width]
    for j in range(1, per_group):
        out = jnp.where(row // rhs == j, product[:, j * width : (j + 1) * width], out)
    return out


def near_kernel(rhs, hot_ref, own_ref, pair_ref, cross_ref, near_ref, part_ref):
    rows, width = own_ref.shape
    others = hot_ref.shape[0] // rows
    own = own_ref[...]
    pool = jnp.concatenate([own, pair_ref[...], cross_ref[...], own], axis=0)
    picked = jnp.dot(hot_ref[...], pool, preferred_element_type=jnp.float32)
    picked = picked.astype(jnp.bfloat16)
    for g in range(rows // PACK):
        left = [own[g * PACK : (g + 1) * PACK]] + [
            picked[k * rows + g * PACK : k * rows + (g + 1) * PACK] for k in range(others)
        ]
        part_ref[g * PACK : (g + 1) * PACK] = grouped_product(
            rhs,
            jnp.concatenate(left, axis=1),
            lambda i: jnp.concatenate(
                [near_ref[i, 0], near_ref[i, 2:].reshape(others * width, width)], axis=0
            ),
            g,
        )


def spline_kernel(
    rhs, _, mirror_ref, code_vmem, part_ref, gate_ref, near_ref, spline_ref,
    sums_ref, acc, pair_ref, code_ref, sem,
):
    copy = pltpu.make_async_copy(code_vmem, code_ref, sem)
    copy.start()
    block_count, splines = code_ref.shape
    rows, width = part_ref.shape
    loads = []
    for g in range(rows // PACK):
        group = slice(g * PACK, (g + 1) * PACK)
        sums = part_ref[group] + grouped_product(
            rhs, mirror_ref[group], lambda i: near_ref[i, 1], g
        )
        sums_ref[group] = sums
        gated = gate_ref[...] * sums
        loads += [gated[row : row + TILE] for row in range(0, PACK, TILE)]
    acc[...] = jnp.zeros(acc.shape, jnp.float32)
    upper = lax.broadcasted_iota(jnp.int32, (TILE, width), 0) // rhs
    blank = jnp.zeros((TILE, width), jnp.float32)

    def pair_product(pair):
        both = loads[pair // 2]
        turned = pltpu.roll(both, rhs, 0)
        mine = jnp.concatenate(
            [
                jnp.concatenate([jnp.where(upper == 0, both, turned), blank], axis=1),
                jnp.concatenate([blank, jnp.where(upper == 0, turned, both)], axis=1),
            ],
            axis=0,
        ).astype(jnp.bfloat16)
        blocks = jnp.concatenate(
            [
                jnp.concatenate([spline_ref[i, s] for s in range(splines)], axis=1)
                for i in (pair, pair + 1)
            ],
            axis=0,
        )
        return jnp.dot(mine, blocks, preferred_element_type=jnp.float32)

    pairs = range(0, block_count, 2)
    products = {pair: pair_product(pair) for pair in pairs}
    copy.wait()
    for pair, product in products.items():
        for i in (pair, pair + 1):
            total = product[(i - pair) * TILE : (i - pair + 1) * TILE]
            places, sums = [], []
            for s in range(splines):
                code = code_ref[i, s]
                place = code >> 1
                added = jnp.where(upper == (code & 1), total[:, s * width : (s + 1) * width], 0.0)
                places.append(place)
                sums.append(acc[place] + added)
            for place, value in zip(places, sums):
                acc[place] = value
    tiles = acc.shape[0] // 2
    size = pair_ref.shape[0] * pair_ref.shape[1] // TILE
    pair_ref[...] = acc[tiles : tiles + size].reshape(pair_ref.shape).astype(pair_ref.dtype)


def far_kernel(acc, far_ref):
    tiles, size = acc.shape[0] // 2, far_ref.shape[1] * far_ref.shape[2] // TILE
    for which in range(2):
        group = slice((which + 1) * tiles - size, (which + 1) * tiles)
        far_ref[which] = acc[group].reshape(far_ref.shape[1:]).astype(far_ref.dtype)


def split_kernel(acc, got_ref, *out_refs):
    size, struct_rows, _ = out_refs[0].shape
    height = struct_rows // TILE
    for step, out_ref in enumerate(out_refs):
        for place in range(size):
            index = step * size + place
            held = acc[index * height : (index + 1) * height].reshape(out_ref.shape[1:])
            out_ref[place] = (held + got_ref[index].astype(jnp.float32)).astype(out_ref.dtype)


def hand_kernel(held_ref, far_ref, keep_ref, given_ref):
    keep_ref[...] = held_ref[...] + far_ref[0].astype(jnp.float32)
    given_ref[...] = far_ref[1]


def gather_kernel(held_ref, *refs):
    got_refs, out_ref = refs[:-1], refs[-1]
    total = held_ref[...]
    for got_ref in got_refs:
        total = total + got_ref[...].astype(jnp.float32)
    out_ref[...] = total


def column_kernel(machs, held_ref, got_ref, *out_refs):
    for place in range(2):
        total = held_ref[place] + got_ref[place].astype(jnp.float32)
        for out_ref in out_refs[place * machs : (place + 1) * machs]:
            out_ref[...] = total.astype(out_ref.dtype)


def inverse_kernel(rhs, machs, *refs):
    other_refs, same_refs = refs[: 2 * machs : 2], refs[1 : 2 * machs : 2]
    inverse_ref, out_ref = refs[2 * machs :]
    parts = [
        same[...].astype(jnp.float32) + other[...].astype(jnp.float32)
        for same, other in zip(same_refs, other_refs)
    ]
    rounded = sum(parts[1:], parts[0]).astype(jnp.bfloat16)
    for g in range(rounded.shape[0] // PACK):
        out_ref[g * PACK : (g + 1) * PACK] = grouped_product(
            rhs, rounded[g * PACK : (g + 1) * PACK], lambda t: inverse_ref[t], g
        )


def mask_of(step):
    return 4 * step + (step >> 1) % 2


def swap(value, panels, apart):
    return lax.ppermute(value, "panel", [(i, i ^ apart) for i in range(panels)])


def mach_swap(value, machs, panels, turn, apart):
    pairs = [
        (mach * panels + i, (mach + turn) % machs * panels + (i ^ apart))
        for mach in range(machs)
        for i in range(panels)
    ]
    return lax.ppermute(value, ("mach", "panel"), pairs)


def cost(flops, size):
    return pl.CostEstimate(flops=flops, bytes_accessed=size, transcendentals=0)


def on_device(
    adjoint, near_blocks, pattern, trim_mask, spline_blocks, spline_owner, spline_local,
    struct_inverse,
):
    _, block_count, rhs, width = adjoint.shape
    entries = pattern.shape[1]
    panels, machs = lax.axis_size("panel"), lax.axis_size("mach")
    struct_count = struct_inverse.shape[0]
    rows, struct_rows = block_count * rhs, struct_count * rhs
    params = pltpu.CompilerParams(vmem_limit_bytes=16 * 1024 * 1024)
    f32, bf16 = jnp.float32, jnp.bfloat16
    own = adjoint.reshape(rows, width)
    beside = {0: 0, panels - 1: panels - 1}
    cross = lax.ppermute(
        own, ("mach", "panel"),
        [
            (
                mach * panels + i,
                (mach ^ (i in beside)) * panels + beside.get(i, i - 1 + 2 * (i % 2)),
            )
            for mach in range(machs)
            for i in range(panels)
        ],
    )
    mirror = swap(own, panels, panels // 2)
    pair = swap(own, panels, 1)
    expand = pl.pallas_call(
        functools.partial(spread_kernel, rhs),
        out_shape=jax.ShapeDtypeStruct((rows, block_count), bf16),
        out_specs=VMEM,
        compiler_params=params,
        cost_estimate=cost(8 * 10**9, 32 * 2**20),
        name="row_order",
    )()
    hot, gate, held, code = pl.pallas_call(
        functools.partial(pick_kernel, panels, rhs, struct_count),
        out_shape=(
            jax.ShapeDtypeStruct(((entries - 2) * rows, 4 * rows), bf16),
            jax.ShapeDtypeStruct((PACK, width), f32),
            jax.ShapeDtypeStruct((rows, width), bf16),
            jax.ShapeDtypeStruct(spline_owner.shape, jnp.int32),
        ),
        in_specs=[VMEM] * 6,
        out_specs=(VMEM,) * 4,
        compiler_params=params,
        cost_estimate=cost(10**6, 2**17),
        name="pick_rows",
    )(expand, pattern, trim_mask, own, spline_owner, spline_local)
    part = pl.pallas_call(
        functools.partial(near_kernel, rhs),
        out_shape=jax.ShapeDtypeStruct((rows, width), f32),
        in_specs=[VMEM] * 5,
        out_specs=VMEM,
        compiler_params=params,
        cost_estimate=cost(10**6, 2**17),
        name="near_field",
    )(hot, held, pair, cross, near_blocks[0])
    steps = panels // 4
    two = (2, struct_rows, width)
    sums, acc, send = pl.pallas_call(
        functools.partial(spline_kernel, rhs),
        out_shape=(
            jax.ShapeDtypeStruct((rows, width), f32),
            jax.ShapeDtypeStruct((panels * struct_rows // TILE, TILE, width), f32),
            jax.ShapeDtypeStruct((2 * (steps - 1), struct_rows, width), bf16),
        ),
        in_specs=[VMEM] * 7,
        out_specs=(VMEM,) * 3,
        scratch_shapes=[
            pltpu.SMEM(spline_owner.shape, jnp.int32),
            pltpu.SemaphoreType.DMA,
        ],
        compiler_params=params,
        cost_estimate=cost(10**6, 2**17),
        name="spline_loads",
    )(cross, mirror, code, part, gate, near_blocks[0], spline_blocks)
    far = pl.pallas_call(
        far_kernel,
        out_shape=jax.ShapeDtypeStruct((2, *two), bf16),
        in_specs=[VMEM],
        out_specs=VMEM,
        compiler_params=params,
        cost_estimate=cost(10**6, 2**17),
        name="far_loads",
    )(acc)
    loads = sums.reshape(adjoint.shape) * trim_mask[0].astype(f32)[None, None, :, None]
    got = swap(send, panels, 1)
    far = swap(far, panels, mask_of(steps - 1))
    keep, *sends = pl.pallas_call(
        split_kernel,
        out_shape=tuple(
            jax.ShapeDtypeStruct(two, f32 if step == 0 else bf16) for step in range(steps - 1)
        ),
        in_specs=[VMEM, VMEM],
        out_specs=(VMEM,) * (steps - 1),
        compiler_params=params,
        cost_estimate=cost(10**6, 2**17),
        name="pair_sum",
    )(acc, got)
    got = [swap(sends[step - 1], panels, mask_of(step)) for step in range(steps - 2, 0, -1)]
    keep, given = pl.pallas_call(
        hand_kernel,
        out_shape=(jax.ShapeDtypeStruct(two, f32), jax.ShapeDtypeStruct(two, bf16)),
        in_specs=[VMEM, VMEM],
        out_specs=(VMEM, VMEM),
        compiler_params=params,
        cost_estimate=cost(10**6, 2**17),
        name="hand_over",
    )(keep, far)
    given = swap(given, panels, 1)
    keep = pl.pallas_call(
        gather_kernel,
        out_shape=jax.ShapeDtypeStruct(two, f32),
        in_specs=[VMEM] * (steps - 1),
        out_specs=VMEM,
        compiler_params=params,
        cost_estimate=cost(4 * 10**9, 16 * 2**20),
        name="far_sum",
    )(keep, *got)
    one = jax.ShapeDtypeStruct((struct_rows, width), f32)
    columns = pl.pallas_call(
        functools.partial(column_kernel, machs),
        out_shape=(one,) * (2 * machs),
        in_specs=[VMEM] * 2,
        out_specs=(VMEM,) * (2 * machs),
        compiler_params=params,
        cost_estimate=cost(10**6, 2**17),
        name="column_sum",
    )(keep, given)
    sames = [
        mach_swap(columns[turn], machs, panels, turn, 0) if turn else columns[0]
        for turn in range(machs)
    ]
    others = [mach_swap(columns[machs + turn], machs, panels, turn, 3) for turn in range(machs)]
    struct_adjoint = pl.pallas_call(
        functools.partial(inverse_kernel, rhs, machs),
        out_shape=jax.ShapeDtypeStruct((struct_rows, width), f32),
        in_specs=[VMEM] * (2 * machs + 1),
        out_specs=VMEM,
        compiler_params=params,
        cost_estimate=cost(10**6, 2**17),
        name="struct_solve",
    )(
        *(value for turn in range(machs - 1, -1, -1) for value in (others[turn], sames[turn])),
        struct_inverse,
    )
    return (
        loads,
        struct_adjoint.reshape(struct_count, rhs, width),
    )


def solution(mesh):
    in_specs = (
        P("mach", "panel", None, None),
        P("mach", "panel", None, None, None),
        P("panel", None),
        P("mach", None),
        P("panel", None, None, None),
        P("panel", None),
        P("panel", None),
        P("panel", None, None),
    )
    out_specs = (P("mach", "panel", None, None), P("panel", None, None))
    return jax.shard_map(
        on_device, mesh=mesh, in_specs=in_specs, out_specs=out_specs, check_vma=False
    )
```

```python
import functools

import jax
import jax.numpy as jnp
from jax import lax
from jax.experimental import pallas as pl
from jax.experimental.pallas import tpu as pltpu
from jax.sharding import PartitionSpec as P

SMEM = pl.BlockSpec(memory_space=pltpu.SMEM)
VMEM = pl.BlockSpec(memory_space=pltpu.VMEM)
PACK = 16
TILE = 8


def device_class(index):
    return (index ^ (index >> 1) ^ (index >> 3)) & 1


def spread_kernel(rhs, expand_ref):
    shape = expand_ref.shape
    expand_ref[...] = (
        lax.broadcasted_iota(jnp.int32, shape, 0) // rhs == lax.broadcasted_iota(jnp.int32, shape, 1)
    ).astype(jnp.bfloat16)


def pick_kernel(
    panels, rhs, struct_count, expand_ref, pattern_ref, trim_ref, own_ref, owner_ref, local_ref,
    hot_ref, gate_ref, held_ref, code_ref,
):
    block_count, entries = pattern_ref.shape
    rows = own_ref.shape[0]
    here = lax.axis_index("panel")
    shape = (rows, hot_ref.shape[1])
    offset = lax.broadcasted_iota(jnp.int32, shape, 1) - (
        lax.broadcasted_iota(jnp.int32, shape, 0) % rhs
    )
    block = pattern_ref[...]
    apart = (block // block_count) ^ here
    slot = jnp.where(apart == 0, 0, jnp.where(apart == 1, 1, 2))
    first = (slot * block_count + block % block_count) * rhs
    first = jnp.dot(
        expand_ref[...],
        first.astype(jnp.float32).astype(jnp.bfloat16),
        preferred_element_type=jnp.float32,
    ).astype(jnp.int32)
    for k in range(2, entries):
        hot_ref[(k - 2) * rows : (k - 1) * rows] = (offset == first[:, k : k + 1]).astype(
            jnp.bfloat16
        )
    shape = (gate_ref.shape[0], rhs)
    mine = lax.broadcasted_iota(jnp.int32, shape, 0) % rhs == lax.broadcasted_iota(
        jnp.int32, shape, 1
    )
    gate = jnp.sum(jnp.where(mine, trim_ref[...], 0).astype(jnp.float32), axis=1, keepdims=True)
    gate_ref[...] = jnp.broadcast_to(gate, gate_ref.shape)
    held_ref[...] = own_ref[...]
    owner = owner_ref[...]
    code_ref[...] = (
        (device_class(owner) ^ device_class(here)) * (panels // 2) + ((owner ^ here) >> 1)
    ) * struct_count + local_ref[...]


def grouped_product(rhs, left, blocks_of, group):
    per_group = PACK // rhs
    every = jnp.concatenate([blocks_of(group * per_group + j) for j in range(per_group)], axis=1)
    product = jnp.dot(left, every, preferred_element_type=jnp.float32)
    width = product.shape[1] // per_group
    row = lax.broadcasted_iota(jnp.int32, (PACK, width), 0)
    out = product[:, :width]
    for j in range(1, per_group):
        out = jnp.where(row // rhs == j, product[:, j * width : (j + 1) * width], out)
    return out


def near_kernel(rhs, hot_ref, own_ref, pair_ref, cross_ref, near_ref, part_ref):
    rows, width = own_ref.shape
    others = hot_ref.shape[0] // rows
    own = own_ref[...]
    pool = jnp.concatenate([own, pair_ref[...], cross_ref[...], own], axis=0)
    picked = jnp.dot(hot_ref[...], pool, preferred_element_type=jnp.float32)
    picked = picked.astype(jnp.bfloat16)
    for g in range(rows // PACK):
        left = [own[g * PACK : (g + 1) * PACK]] + [
            picked[k * rows + g * PACK : k * rows + (g + 1) * PACK] for k in range(others)
        ]
        part_ref[g * PACK : (g + 1) * PACK] = grouped_product(
            rhs,
            jnp.concatenate(left, axis=1),
            lambda i: jnp.concatenate(
                [near_ref[i, 0], near_ref[i, 2:].reshape(others * width, width)], axis=0
            ),
            g,
        )


def spline_kernel(
    rhs, _, mirror_ref, code_vmem, part_ref, gate_ref, near_ref, spline_ref,
    sums_ref, acc, pair_ref, code_ref, sem,
):
    copy = pltpu.make_async_copy(code_vmem, code_ref, sem)
    copy.start()
    block_count, splines = code_ref.shape
    rows, width = part_ref.shape
    loads = []
    for g in range(rows // PACK):
        group = slice(g * PACK, (g + 1) * PACK)
        sums = part_ref[group] + grouped_product(
            rhs, mirror_ref[group], lambda i: near_ref[i, 1], g
        )
        sums_ref[group] = sums
        gated = gate_ref[...] * sums
        loads += [gated[row : row + TILE] for row in range(0, PACK, TILE)]
    acc[...] = jnp.zeros(acc.shape, jnp.float32)
    upper = lax.broadcasted_iota(jnp.int32, (TILE, width), 0) // rhs
    blank = jnp.zeros((TILE, width), jnp.float32)

    def pair_product(pair):
        both = loads[pair // 2]
        turned = pltpu.roll(both, rhs, 0)
        mine = jnp.concatenate(
            [
                jnp.concatenate([jnp.where(upper == 0, both, turned), blank], axis=1),
                jnp.concatenate([blank, jnp.where(upper == 0, turned, both)], axis=1),
            ],
            axis=0,
        ).astype(jnp.bfloat16)
        blocks = jnp.concatenate(
            [
                jnp.concatenate([spline_ref[i, s] for s in range(splines)], axis=1)
                for i in (pair, pair + 1)
            ],
            axis=0,
        )
        return jnp.dot(mine, blocks, preferred_element_type=jnp.float32)

    pairs = range(0, block_count, 2)
    products = {pair: pair_product(pair) for pair in pairs}
    copy.wait()
    for pair, product in products.items():
        places, sums = [], []
        for which in range(2):
            total = product[which * TILE : (which + 1) * TILE]
            for s in range(splines):
                code = code_ref[pair + which, s]
                place = (which, code >> 1)
                added = jnp.where(upper == (code & 1), total[:, s * width : (s + 1) * width], 0.0)
                places.append(place)
                sums.append(acc[place] + added)
        for place, value in zip(places, sums):
            acc[place] = value
    tiles = acc.shape[1] // 2
    size = pair_ref.shape[0] * pair_ref.shape[1] // TILE
    kept = acc[0, tiles : tiles + size] + acc[1, tiles : tiles + size]
    pair_ref[...] = kept.reshape(pair_ref.shape).astype(pair_ref.dtype)


def far_kernel(acc, far_ref):
    tiles, size = acc.shape[1] // 2, far_ref.shape[1] * far_ref.shape[2] // TILE
    for which in range(2):
        group = slice((which + 1) * tiles - size, (which + 1) * tiles)
        far_ref[which] = (acc[0, group] + acc[1, group]).reshape(far_ref.shape[1:]).astype(far_ref.dtype)


def split_kernel(acc, got_ref, *out_refs):
    size, struct_rows, _ = out_refs[0].shape
    height = struct_rows // TILE
    for step, out_ref in enumerate(out_refs):
        for place in range(size):
            index = step * size + place
            rows = slice(index * height, (index + 1) * height)
            held = (acc[0, rows] + acc[1, rows]).reshape(out_ref.shape[1:])
            out_ref[place] = (held + got_ref[index].astype(jnp.float32)).astype(out_ref.dtype)


def hand_kernel(held_ref, far_ref, keep_ref, given_ref):
    keep_ref[...] = held_ref[...] + far_ref[0].astype(jnp.float32)
    given_ref[...] = far_ref[1]


def gather_kernel(held_ref, *refs):
    got_refs, out_ref = refs[:-1], refs[-1]
    total = held_ref[...]
    for got_ref in got_refs:
        total = total + got_ref[...].astype(jnp.float32)
    out_ref[...] = total


def column_kernel(machs, held_ref, got_ref, *out_refs):
    for place in range(2):
        total = held_ref[place] + got_ref[place].astype(jnp.float32)
        for out_ref in out_refs[place * machs : (place + 1) * machs]:
            out_ref[...] = total.astype(out_ref.dtype)


def inverse_kernel(rhs, machs, *refs):
    other_refs, same_refs = refs[: 2 * machs : 2], refs[1 : 2 * machs : 2]
    inverse_ref, out_ref = refs[2 * machs :]
    parts = [
        same[...].astype(jnp.float32) + other[...].astype(jnp.float32)
        for same, other in zip(same_refs, other_refs)
    ]
    rounded = sum(parts[1:], parts[0]).astype(jnp.bfloat16)
    for g in range(rounded.shape[0] // PACK):
        out_ref[g * PACK : (g + 1) * PACK] = grouped_product(
            rhs, rounded[g * PACK : (g + 1) * PACK], lambda t: inverse_ref[t], g
        )


def mask_of(step):
    return 4 * step + (step >> 1) % 2


def swap(value, panels, apart):
    return lax.ppermute(value, "panel", [(i, i ^ apart) for i in range(panels)])


def mach_swap(value, machs, panels, turn, apart):
    pairs = [
        (mach * panels + i, (mach + turn) % machs * panels + (i ^ apart))
        for mach in range(machs)
        for i in range(panels)
    ]
    return lax.ppermute(value, ("mach", "panel"), pairs)


def cost(flops, size):
    return pl.CostEstimate(flops=flops, bytes_accessed=size, transcendentals=0)


def on_device(
    adjoint, near_blocks, pattern, trim_mask, spline_blocks, spline_owner, spline_local,
    struct_inverse,
):
    _, block_count, rhs, width = adjoint.shape
    entries = pattern.shape[1]
    panels, machs = lax.axis_size("panel"), lax.axis_size("mach")
    struct_count = struct_inverse.shape[0]
    rows, struct_rows = block_count * rhs, struct_count * rhs
    params = pltpu.CompilerParams(vmem_limit_bytes=16 * 1024 * 1024)
    f32, bf16 = jnp.float32, jnp.bfloat16
    own = adjoint.reshape(rows, width)
    beside = {0: 0, panels - 1: panels - 1}
    cross = lax.ppermute(
        own, ("mach", "panel"),
        [
            (
                mach * panels + i,
                (mach ^ (i in beside)) * panels + beside.get(i, i - 1 + 2 * (i % 2)),
            )
            for mach in range(machs)
            for i in range(panels)
        ],
    )
    mirror = swap(own, panels, panels // 2)
    pair = swap(own, panels, 1)
    expand = pl.pallas_call(
        functools.partial(spread_kernel, rhs),
        out_shape=jax.ShapeDtypeStruct((rows, block_count), bf16),
        out_specs=VMEM,
        compiler_params=params,
        cost_estimate=cost(8 * 10**9, 32 * 2**20),
        name="row_order",
    )()
    hot, gate, held, code = pl.pallas_call(
        functools.partial(pick_kernel, panels, rhs, struct_count),
        out_shape=(
            jax.ShapeDtypeStruct(((entries - 2) * rows, 4 * rows), bf16),
            jax.ShapeDtypeStruct((PACK, width), f32),
            jax.ShapeDtypeStruct((rows, width), bf16),
            jax.ShapeDtypeStruct(spline_owner.shape, jnp.int32),
        ),
        in_specs=[VMEM] * 6,
        out_specs=(VMEM,) * 4,
        compiler_params=params,
        cost_estimate=cost(10**6, 2**17),
        name="pick_rows",
    )(expand, pattern, trim_mask, own, spline_owner, spline_local)
    part = pl.pallas_call(
        functools.partial(near_kernel, rhs),
        out_shape=jax.ShapeDtypeStruct((rows, width), f32),
        in_specs=[VMEM] * 5,
        out_specs=VMEM,
        compiler_params=params,
        cost_estimate=cost(10**6, 2**17),
        name="near_field",
    )(hot, held, pair, cross, near_blocks[0])
    steps = panels // 4
    two = (2, struct_rows, width)
    sums, acc, send = pl.pallas_call(
        functools.partial(spline_kernel, rhs),
        out_shape=(
            jax.ShapeDtypeStruct((rows, width), f32),
            jax.ShapeDtypeStruct((2, panels * struct_rows // TILE, TILE, width), f32),
            jax.ShapeDtypeStruct((2 * (steps - 1), struct_rows, width), bf16),
        ),
        in_specs=[VMEM] * 7,
        out_specs=(VMEM,) * 3,
        scratch_shapes=[
            pltpu.SMEM(spline_owner.shape, jnp.int32),
            pltpu.SemaphoreType.DMA,
        ],
        compiler_params=params,
        cost_estimate=cost(10**6, 2**17),
        name="spline_loads",
    )(cross, mirror, code, part, gate, near_blocks[0], spline_blocks)
    far = pl.pallas_call(
        far_kernel,
        out_shape=jax.ShapeDtypeStruct((2, *two), bf16),
        in_specs=[VMEM],
        out_specs=VMEM,
        compiler_params=params,
        cost_estimate=cost(10**6, 2**17),
        name="far_loads",
    )(acc)
    loads = sums.reshape(adjoint.shape) * trim_mask[0].astype(f32)[None, None, :, None]
    got = swap(send, panels, 1)
    far = swap(far, panels, mask_of(steps - 1))
    keep, *sends = pl.pallas_call(
        split_kernel,
        out_shape=tuple(
            jax.ShapeDtypeStruct(two, f32 if step == 0 else bf16) for step in range(steps - 1)
        ),
        in_specs=[VMEM, VMEM],
        out_specs=(VMEM,) * (steps - 1),
        compiler_params=params,
        cost_estimate=cost(10**6, 2**17),
        name="pair_sum",
    )(acc, got)
    got = [swap(sends[step - 1], panels, mask_of(step)) for step in range(steps - 2, 0, -1)]
    keep, given = pl.pallas_call(
        hand_kernel,
        out_shape=(jax.ShapeDtypeStruct(two, f32), jax.ShapeDtypeStruct(two, bf16)),
        in_specs=[VMEM, VMEM],
        out_specs=(VMEM, VMEM),
        compiler_params=params,
        cost_estimate=cost(10**6, 2**17),
        name="hand_over",
    )(keep, far)
    given = swap(given, panels, 1)
    keep = pl.pallas_call(
        gather_kernel,
        out_shape=jax.ShapeDtypeStruct(two, f32),
        in_specs=[VMEM] * (steps - 1),
        out_specs=VMEM,
        compiler_params=params,
        cost_estimate=cost(4 * 10**9, 16 * 2**20),
        name="far_sum",
    )(keep, *got)
    one = jax.ShapeDtypeStruct((struct_rows, width), f32)
    columns = pl.pallas_call(
        functools.partial(column_kernel, machs),
        out_shape=(one,) * (2 * machs),
        in_specs=[VMEM] * 2,
        out_specs=(VMEM,) * (2 * machs),
        compiler_params=params,
        cost_estimate=cost(10**6, 2**17),
        name="column_sum",
    )(keep, given)
    sames = [
        mach_swap(columns[turn], machs, panels, turn, 0) if turn else columns[0]
        for turn in range(machs)
    ]
    others = [mach_swap(columns[machs + turn], machs, panels, turn, 3) for turn in range(machs)]
    struct_adjoint = pl.pallas_call(
        functools.partial(inverse_kernel, rhs, machs),
        out_shape=jax.ShapeDtypeStruct((struct_rows, width), f32),
        in_specs=[VMEM] * (2 * machs + 1),
        out_specs=VMEM,
        compiler_params=params,
        cost_estimate=cost(10**6, 2**17),
        name="struct_solve",
    )(
        *(value for turn in range(machs - 1, -1, -1) for value in (others[turn], sames[turn])),
        struct_inverse,
    )
    return (
        loads,
        struct_adjoint.reshape(struct_count, rhs, width),
    )


def solution(mesh):
    in_specs = (
        P("mach", "panel", None, None),
        P("mach", "panel", None, None, None),
        P("panel", None),
        P("mach", None),
        P("panel", None, None, None),
        P("panel", None),
        P("panel", None),
        P("panel", None, None),
    )
    out_specs = (P("mach", "panel", None, None), P("panel", None, None))
    return jax.shard_map(
        on_device, mesh=mesh, in_specs=in_specs, out_specs=out_specs, check_vma=False
    )
```
